32 devices in a mesh: fsdp: 4 (over x, core), pair: 8 (over z, y).
Axes of the slice: x: 2, y: 2, z: 4, core: 2. Of those that a mesh axis runs over, the one named last changes fastest.
Arguments:
- tokens: bfloat16 [16384, 8192], P('pair', 'fsdp'), may hold values from -6 to 6
- cotangent: bfloat16 [16384, 1024], P('pair', 'fsdp'), may hold values from -6 to 6
- value_weight: bfloat16 [8192, 1024], P('fsdp'), may hold values from -0.0625 to 0.0625
- adapter_down: bfloat16 [48, 8192, 128], P(None, 'fsdp'), may hold values from -0.0625 to 0.0625
- adapter_up: bfloat16 [48, 128, 1024], P(None, None, 'fsdp'), may hold values from -0.5 to 0.5
- pair_ids: int32 [32], P('pair'), may hold values from 0 to 47
- ranks: int32 [48], replicated, may hold values from 16 to 128, as said below
Outputs:
- input_grad: bfloat16 [16384, 8192], P('pair', 'fsdp')
- down_grad: bfloat16 [48, 8192, 128], P('pair', 'fsdp')
- up_grad: bfloat16 [48, 128, 1024], P('pair', None, 'fsdp')
The draws below stay inside these ranges and needn't reach their ends.
Inputs may be any that keep to these rules, and one draw needn't show every extreme that they name: `ranks`: each rank is 128, 64, 32 or 16; both ends occur in every draw.
All inputs are finite; a program needn't handle non-finite values.
Results may differ from the reference program's by a relative error of at most 0.022.
Values may be sent and summed in bfloat16 or wider, within the bound.
No kernel may reach another device: no remote copies, remote signals or barrier semaphores. Data moves between devices by JAX's collectives and lax.ppermute only.
A program may use at most 192 MiB of HBM per device.

```python
import math
import jax
import jax.numpy as jnp
import numpy as np
from jax import lax

D = 8192
NPAIR = 48
RMAX = 128
BLOCK = 512
TOKB = 2048
KV = 1024
TOKENS = 16384
NBLOCKS = 32
N_PAIR = 8


def draw_ranks(key, part):
    first, second = jax.random.split(key)
    level = jax.random.randint(first, (NPAIR,), 0, 4)
    values = RMAX // jnp.power(2, level).astype(jnp.int32)
    places = jax.random.permutation(second, NPAIR)
    values = values.at[places[0]].set(RMAX)
    values = values.at[places[1]].set(RMAX // 8)
    return values.astype(jnp.int32)


def with_ends(array, rng, low, high):
    longest = array.shape.index(max(array.shape))
    spots = []
    for shift in (0, 1):
        where = [jax.random.randint(jax.random.fold_in(rng, axis), (), 0, length) for axis, length in enumerate(array.shape)]
        where[longest] = (where[longest] + shift) % array.shape[longest]
        spots.append(tuple(where))
    return array.at[spots[0]].set(low).at[spots[1]].set(high)


def level_of(stream_key, shape, cuts, least, largest):
    level, own = 1.0, jax.random.fold_in(stream_key, 6)
    for dim, shards_of in cuts:
        draws = jnp.exp(jax.random.uniform(jax.random.fold_in(own, dim), (shards_of,), jnp.float32, least / len(cuts), largest / len(cuts)))
        level = level * jnp.repeat(draws, shape[dim] // shards_of).reshape([-1 if axis == dim else 1 for axis in range(len(shape))])
    return level


def cumulative_ranks(count, skew):
    weights = [(1 << 20) // math.isqrt(rank ** skew) + 1 for rank in range(1, count + 1)]
    scale = 1 + sum(weights) // (1 << 30)
    return np.cumsum(np.array([max(1, weight // scale) for weight in weights]))


def ranked(key, dims, count, lean):
    table = cumulative_ranks(count, lean)
    lot = jax.random.randint(jax.random.fold_in(key, 1), dims, 0, int(table[count - 1]))
    rank = jnp.searchsorted(jnp.asarray(table, jnp.int32), lot, side="right")
    return jax.random.permutation(jax.random.fold_in(key, 2), count)[rank].astype(jnp.int32)


def centred(own_key, dims, scale, most, shards=(), kind=jnp.bfloat16):
    result = scale * jax.random.normal(own_key, dims, jnp.float32)
    if shards:
        result = result * level_of(own_key, dims, shards, -0.22, 0.18)
    return jnp.clip(result, -most, most).astype(kind)


def setup_inputs(seed: int = 0) -> dict:
    splits = jax.random.split(jax.random.key(seed), 8)
    tokens = centred(splits[0], (TOKENS, D), 1.0, 6.0, ((0, 8), (1, 4)))
    cotangent = centred(splits[1], (TOKENS, KV), 1.0, 6.0, ((0, 8), (1, 4)))
    value_weight = centred(splits[2], (D, KV), D ** -0.5, 0.0625, ((0, 4),))
    adapter_down = centred(splits[3], (NPAIR, D, RMAX), D ** -0.5, 0.0625, ((1, 4),))
    adapter_up = centred(splits[4], (NPAIR, RMAX, KV), RMAX ** -0.5, 0.5, ((2, 4),))
    pair_ids = with_ends(ranked(splits[5], (NBLOCKS,), NPAIR, 2), jax.random.fold_in(splits[5], 3), 0, NPAIR - 1).astype(jnp.int32)
    ranks = draw_ranks(jax.random.fold_in(splits[7], 71), 0)
    return {"tokens": tokens, "cotangent": cotangent, "value_weight": value_weight, "adapter_down": adapter_down, "adapter_up": adapter_up, "pair_ids": pair_ids, "ranks": ranks}


def reference(tokens, cotangent, value_weight, adapter_down, adapter_up, pair_ids, ranks):
    block_count = TOKB // BLOCK
    columns = jnp.arange(RMAX, dtype=jnp.int32)
    mask = (columns[None, :] < ranks[:, None]).astype(jnp.float32)
    scale = 32.0 / ranks.astype(jnp.float32)
    norm = 1.0 / math.sqrt(TOKENS)
    weight_f = value_weight.astype(jnp.float32)
    group_x = tokens.reshape(N_PAIR, block_count, BLOCK, D)
    group_c = cotangent.reshape(N_PAIR, block_count, BLOCK, KV)
    group_ids = pair_ids.reshape(N_PAIR, block_count)
    pair_range = jnp.arange(NPAIR, dtype=jnp.int32)

    def step(carry, inputs):
        total_a, total_b = carry
        xs, cs, ids = inputs
        x_f = xs.astype(jnp.float32)
        c_f = cs.astype(jnp.float32)
        selected_down_adapter = adapter_down[ids].astype(jnp.float32)
        b_sel = adapter_up[ids].astype(jnp.float32)
        rows_mask = mask[ids][:, None, :]
        block_offset = scale[ids]
        low = jnp.einsum('btd,bdr->btr', x_f, selected_down_adapter)
        back = jnp.einsum('btk,brk->btr', c_f, b_sel)
        low_b = (low * rows_mask).astype(jnp.bfloat16)
        backward_up_part = (back * rows_mask).astype(jnp.bfloat16)
        frozen_output = jnp.einsum('btk,dk->btd', c_f, weight_f).astype(jnp.bfloat16)
        adapter_output = jnp.einsum('eiz,efz->eif', backward_up_part.astype(jnp.float32), selected_down_adapter)
        input_gradient_total = (frozen_output.astype(jnp.float32) + block_offset[:, None, None] * adapter_output).astype(jnp.bfloat16)
        coef = block_offset * norm
        term_a = jnp.einsum('btd,btr->bdr', x_f, backward_up_part.astype(jnp.float32)) * coef[:, None, None]
        term_b = jnp.einsum('btr,btk->brk', low_b.astype(jnp.float32), c_f) * coef[:, None, None]
        onehot = (ids[:, None] == pair_range[None, :]).astype(jnp.float32)
        part_a = jnp.einsum('bp,bdr->pdr', onehot, term_a).astype(jnp.bfloat16)
        part_b = jnp.einsum('bp,brk->prk', onehot, term_b).astype(jnp.bfloat16)
        return ((total_a + part_a.astype(jnp.float32), total_b + part_b.astype(jnp.float32)), input_gradient_total)
    init = (jnp.zeros((NPAIR, D, RMAX), jnp.float32), jnp.zeros((NPAIR, RMAX, KV), jnp.float32))
    (total_a, total_b), grads = lax.scan(step, init, (group_x, group_c, group_ids))
    input_grad = grads.reshape(TOKENS, D)
    return (input_grad, total_a.astype(jnp.bfloat16), total_b.astype(jnp.bfloat16))
```

```python
import functools
import math

import jax
import jax.numpy as jnp
from jax import lax
from jax.experimental import pallas as pl
from jax.experimental.pallas import tpu as pltpu
from jax.sharding import PartitionSpec as P

BUCKETS = ((384, 256), (384, 384), (512, 384), (512, 768))
ALIGN = 16
HEAD = 8
NT = (((1,), (1,)), ((), ()))
VMEM = 56 * 1024 * 1024


def call(kernel, out_shape, grid, in_specs, out_specs, scratch=(), flops=0, moved=0, prefetch=1):
    return pl.pallas_call(
        kernel,
        out_shape=out_shape,
        grid_spec=pltpu.PrefetchScalarGridSpec(
            num_scalar_prefetch=prefetch,
            grid=grid,
            in_specs=in_specs,
            out_specs=out_specs,
            scratch_shapes=list(scratch),
        ),
        compiler_params=pltpu.CompilerParams(vmem_limit_bytes=VMEM),
        cost_estimate=pl.CostEstimate(flops=flops, bytes_accessed=moved, transcendentals=0),
    )


def whole(shape):
    return pl.BlockSpec(shape, lambda i, *s: (0,) * len(shape))


def swap(x, axis, bit):
    size = lax.axis_size(axis)
    return lax.ppermute(x, axis, [(i, i ^ bit) for i in range(size)])


def gather_ids(ids, axis):
    me = lax.axis_index(axis)
    bit = 1
    while bit < lax.axis_size(axis):
        other = swap(ids, axis, bit)
        low = (me & bit) == 0
        ids = jnp.where(low, jnp.concatenate([ids, other]), jnp.concatenate([other, ids]))
        bit *= 2
    return ids


def sum_over(x, axis):
    half = x.shape[0] // 2
    wide = lambda v: v.astype(jnp.float32)
    total = (wide(x[:half]) + wide(swap(x[half:], axis, 1))).astype(x.dtype)
    bit = 2
    while bit < lax.axis_size(axis):
        total = (wide(total) + wide(swap(total, axis, bit))).astype(x.dtype)
        bit *= 2
    return jnp.concatenate([total, swap(total, axis, 1)], axis=0)


class Layout:
    def __init__(self, groups, blocks, npair):
        self.groups, self.blocks, self.npair = groups, blocks, npair
        count = groups * blocks
        self.off = HEAD
        self.first = self.off + count
        self.owner = self.first + count
        self.into = self.owner + count
        self.pair_into = self.into + count
        self.pair_rank = self.pair_into + npair
        self.size = self.pair_rank + npair


def plan_kernel(lay, ids, ranks, where_ref, plan):
    groups, blocks, npair = lay.groups, lay.blocks, lay.npair
    per = npair // groups
    plan[0] = where_ref[0]
    plan[1] = where_ref[1]

    def clear(p, carry):
        plan[lay.pair_rank + p] = 0
        return carry

    lax.fori_loop(0, npair, clear, 0)

    def group(g, widest):
        total = jnp.int32(0)
        for b in range(blocks):
            i = g * blocks + b
            pair = ids[i]
            rank = ranks[pair]
            plan[lay.pair_rank + pair] = rank
            place, new = total, rank
            for a in range(b):
                same = ids[g * blocks + a] == pair
                place = jnp.where(same, plan[lay.off + g * blocks + a], place)
                new = jnp.where(same, 0, new)
            plan[lay.off + i] = place
            plan[lay.first + i] = new
            total = total + new
        return jnp.maximum(widest, total)

    widest = lax.fori_loop(0, groups, group, jnp.int32(0))

    def owner(o, fullest):
        total = jnp.int32(0)
        for k in range(per):
            p = o * per + k
            plan[lay.pair_into + p] = total
            total = total + plan[lay.pair_rank + p]
        return jnp.maximum(fullest, total)

    fullest = lax.fori_loop(0, groups, owner, jnp.int32(0))

    def block(i, carry):
        pair = ids[i]
        plan[lay.owner + i] = lax.div(pair, jnp.int32(per))
        plan[lay.into + i] = plan[lay.pair_into + pair]
        return carry

    lax.fori_loop(0, groups * blocks, block, 0)
    choice = jnp.int32(len(BUCKETS) - 1)
    for k in reversed(range(len(BUCKETS) - 1)):
        fits = jnp.logical_and(widest <= BUCKETS[k][0], fullest <= BUCKETS[k][1])
        choice = jnp.where(fits, k, choice)
    plan[2] = choice


def make_plan(lay, ids, ranks, where):
    smem = pl.BlockSpec(memory_space=pltpu.SMEM)
    return pl.pallas_call(
        functools.partial(plan_kernel, lay),
        out_shape=jax.ShapeDtypeStruct((lay.size,), jnp.int32),
        in_specs=[smem] * 3,
        out_specs=smem,
    )(ids, ranks, where)


def back_kernel(ids, cot, up, out):
    out[...] = lax.dot_general(cot[...], up[0], NT, preferred_element_type=jnp.float32).astype(out.dtype)


def back_terms(local, cotangent, adapter_up, blocks):
    rows, width = cotangent.shape
    length = rows // blocks
    rmax = adapter_up.shape[1]
    return call(
        back_kernel,
        jax.ShapeDtypeStruct((rows, rmax), jnp.bfloat16),
        (blocks,),
        [
            pl.BlockSpec((length, width), lambda i, s: (i ^ s[blocks], 0)),
            pl.BlockSpec((1, rmax, width), lambda i, s: (s[i ^ s[blocks]], 0, 0)),
        ],
        pl.BlockSpec((length, rmax), lambda i, s: (i, 0)),
        flops=2 * rows * width * rmax,
        moved=2 * rows * (width + rmax),
    )(local, cotangent, adapter_up)


def low_kernel(ids, x, down, out):
    out[...] = jnp.dot(x[...], down[0], preferred_element_type=jnp.float32).astype(out.dtype)


def low_terms(local, tokens, adapter_down, blocks):
    rows, width = tokens.shape
    length = rows // blocks
    rmax = adapter_down.shape[2]
    return call(
        low_kernel,
        jax.ShapeDtypeStruct((rows, rmax), jnp.bfloat16),
        (blocks,),
        [
            pl.BlockSpec((length, width), lambda i, s: (i ^ s[blocks], 0)),
            pl.BlockSpec((1, width, rmax), lambda i, s: (s[i ^ s[blocks]], 0, 0)),
        ],
        pl.BlockSpec((length, rmax), lambda i, s: (i, 0)),
        flops=2 * rows * width * rmax,
        moved=2 * rows * (width + rmax),
    )(local, tokens, adapter_down)


def iota(shape, axis):
    return lax.broadcasted_iota(jnp.int32, shape, axis)


def row_coefs(lay, plan, scales, norm, place, unit):
    me = plan[0]
    out = jnp.zeros(place.shape, jnp.float32)
    for b in range(lay.blocks):
        i = me * lay.blocks + b
        start = lax.div(plan[lay.off + i], jnp.int32(unit))
        stop = lax.div(plan[lay.off + i] + plan[lay.first + i], jnp.int32(unit))
        inside = jnp.logical_and(place >= start, place < stop)
        out = jnp.where(inside, scales[b] * norm, out)
    return out


def block_rank(local_ranks, b):
    return local_ranks[b]


def down_kernel(lay, norm, half, plan, local, scales, x, back, *rest):
    outs, packed = rest[:-1], rest[-1]
    width = packed.shape[0]
    step = pl.program_id(0)
    length = back.shape[0] // lay.blocks
    rmax = back.shape[1]
    me = plan[0]

    @pl.when(step == 0)
    def _():
        own = local[2 * lay.blocks]
        for b in range(lay.blocks):
            rank = local[lay.blocks + b]
            start = plan[lay.off + me * lay.blocks + b]
            r = iota((width, rmax), 1)
            pick = jnp.logical_and(iota((width, rmax), 0) == r + start, r < rank).astype(jnp.bfloat16)
            rows = back[pl.ds(pl.multiple_of((b ^ own) * length, length), length), :]
            packed[:, b * length : (b + 1) * length] = lax.dot_general(
                pick, rows, NT, preferred_element_type=jnp.float32
            ).astype(jnp.bfloat16)

    coefs = row_coefs(lay, plan, scales, norm, iota((width, 1), 0), 1)
    term = (jnp.dot(packed[...], x[...], preferred_element_type=jnp.float32) * coefs).astype(jnp.bfloat16)
    for s, out in enumerate(outs):

        @pl.when(step == s)
        def _(out=out):
            out[...] = term


def down_terms(lay, norm, width, plan, local, scales, tokens, back):
    rows, features = tokens.shape
    part = features // lay.groups
    return call(
        functools.partial(down_kernel, lay, norm, 0),
        [jax.ShapeDtypeStruct((width, part), jnp.bfloat16)] * lay.groups,
        (lay.groups,),
        [pl.BlockSpec((rows, part), lambda i, plan, *s: (0, i ^ plan[0])), whole(back.shape)],
        [whole((width, part))] * lay.groups,
        [pltpu.VMEM((width, rows), jnp.bfloat16)],
        flops=2 * rows * features * width,
        moved=2 * features * (rows + width),
        prefetch=3,
    )(plan, local, scales, tokens, back)


def up_kernel(lay, norm, plan, local, scales, low, cot, *outs):
    groups = lay.groups
    slot = outs[0].shape[0]
    width = slot * groups
    length = low.shape[0] // lay.blocks
    rmax = low.shape[1]
    me = plan[0]
    own = local[2 * lay.blocks]
    total = jnp.zeros((width, cot.shape[1]), jnp.float32)
    for b in range(lay.blocks):
        rank = local[lay.blocks + b]
        start = lax.div(plan[lay.off + me * lay.blocks + b], jnp.int32(groups))
        r = iota((width, rmax), 1)
        place = ((r % groups) ^ me) * slot + start + r // groups
        pick = jnp.logical_and(iota((width, rmax), 0) == place, r < rank).astype(jnp.bfloat16)
        rows = low[pl.ds(pl.multiple_of((b ^ own) * length, length), length), :]
        packed = lax.dot_general(pick, rows, NT, preferred_element_type=jnp.float32).astype(jnp.bfloat16)
        total += jnp.dot(packed, cot[b * length : (b + 1) * length, :], preferred_element_type=jnp.float32)
    coefs = row_coefs(lay, plan, scales, norm, iota((width, 1), 0) % slot, groups)
    total = (total * coefs).astype(jnp.bfloat16)
    for s, out in enumerate(outs):
        out[...] = total[s * slot : (s + 1) * slot, :]


def up_terms(lay, norm, width, plan, local, scales, low, cotangent):
    rows, features = cotangent.shape
    slot = width // lay.groups
    return call(
        functools.partial(up_kernel, lay, norm),
        [jax.ShapeDtypeStruct((slot, features), jnp.bfloat16)] * lay.groups,
        (1,),
        [whole(low.shape), whole(cotangent.shape)],
        [whole((slot, features))] * lay.groups,
        flops=2 * rows * features * width,
        moved=2 * features * (rows + width),
        prefetch=3,
    )(plan, local, scales, low, cotangent)


def grad_kernel(blocks, tiles, parts, plan, local, scales, *refs):
    cots, (weight, down, back, out, cat) = refs[:parts], refs[parts:]
    step = pl.program_id(0)
    block = lax.div(step, jnp.int32(tiles))
    mine = plan[1]
    width = cots[0].shape[1]
    for s, cot in enumerate(cots):
        cat[:, pl.ds(pl.multiple_of((mine ^ s) * width, width), width)] = cot[...]
    rank = local[blocks + block]
    rows = jnp.where(iota(back.shape, 1) < rank, back[...], jnp.zeros_like(back))
    scale = scales[block]
    chunk = 512
    for c in range(0, out.shape[1], chunk):
        base = lax.dot_general(cat[...], weight[c : c + chunk, :], NT, preferred_element_type=jnp.float32)
        extra = lax.dot_general(rows, down[0, c : c + chunk, :], NT, preferred_element_type=jnp.float32)
        out[:, c : c + chunk] = (base + scale * extra).astype(out.dtype)


def input_gradient(lay, plan, local, scales, cots, weight, adapter_down, back):
    rows, width = cots[0].shape
    features, values = weight.shape
    blocks = lay.blocks
    tile = min(256, rows // blocks)
    tiles = rows // blocks // tile
    rmax = back.shape[1]
    here = lambda i, plan, local, scales: (i, 0)
    kept = lambda i, plan, local, scales: (i ^ (local[2 * blocks] * tiles), 0)
    return call(
        functools.partial(grad_kernel, blocks, tiles, len(cots)),
        jax.ShapeDtypeStruct((rows, features), jnp.bfloat16),
        (rows // tile,),
        [pl.BlockSpec((tile, width), here)] * len(cots)
        + [
            whole(weight.shape),
            pl.BlockSpec((1, features, rmax), lambda i, plan, local, scales: (local[lax.div(i, tiles)], 0, 0)),
            pl.BlockSpec((tile, rmax), kept),
        ],
        pl.BlockSpec((tile, features), here),
        [pltpu.VMEM((tile, values), jnp.bfloat16)],
        flops=2 * rows * features * (values + rmax),
        moved=2 * features * (rows + values),
        prefetch=3,
    )(plan, local, scales, *cots, weight, adapter_down, back)


def reduce_kernel(lay, cap, plan, *refs):
    groups, blocks = lay.groups, lay.blocks
    downs, ups = refs[:groups], refs[groups : 2 * groups]
    outs, (total,) = refs[2 * groups : 3 * groups], refs[3 * groups :]
    me = plan[0]
    small, slot = cap // groups, ups[0].shape[0]
    total[...] = jnp.zeros_like(total)
    sums = jnp.zeros((cap, ups[0].shape[1]), jnp.float32)
    for s in range(groups):
        place = iota((1, slot), 1)
        target = jnp.full((1, slot), -1, jnp.int32)
        for b in range(blocks):
            i = (me ^ s) * blocks + b
            rank, source = plan[lay.first + i], plan[lay.off + i]
            owner, into = plan[lay.owner + i], plan[lay.into + i]
            goal = owner * cap + into

            def add(k, carry, s=s, source=source, goal=goal):
                there = pl.ds(pl.multiple_of(goal + k * ALIGN, ALIGN), ALIGN)
                here = pl.ds(pl.multiple_of(source + k * ALIGN, ALIGN), ALIGN)
                total[there, :] += downs[s][here, :].astype(jnp.float32)
                return carry

            lax.fori_loop(0, lax.div(rank, jnp.int32(ALIGN)), add, 0)
            start = lax.div(source, jnp.int32(groups))
            inside = jnp.logical_and(place >= start, place < start + lax.div(rank, jnp.int32(groups)))
            shift = owner * small + lax.div(into, jnp.int32(groups)) - start
            target = jnp.where(inside, place + shift, target)
        pick = (iota((cap, slot), 0) == target).astype(jnp.bfloat16)
        sums += jnp.dot(pick, ups[s][...], preferred_element_type=jnp.float32)
    for s, out in enumerate(outs):
        owner = me ^ s
        out[:cap, :] = total[pl.ds(pl.multiple_of(owner * cap, ALIGN), cap), :].astype(out.dtype)
    total[:cap, :] = sums
    for s, out in enumerate(outs):
        out[cap:, :] = total[pl.ds(pl.multiple_of((me ^ s) * small, ALIGN), small), :].astype(out.dtype)


def reduce_terms(lay, cap, plan, downs, ups):
    part = downs[0].shape[1]
    small = cap // lay.groups
    return call(
        functools.partial(reduce_kernel, lay, cap),
        [jax.ShapeDtypeStruct((cap + small, part), jnp.bfloat16)] * lay.groups,
        (1,),
        [whole(v.shape) for v in downs] + [whole(v.shape) for v in ups],
        [whole((cap + small, part))] * lay.groups,
        [pltpu.VMEM((lay.groups * cap, part), jnp.float32)],
        flops=2 * cap * downs[0].shape[0] * part,
        moved=4 * lay.groups * cap * part,
    )(plan, *downs, *ups)


def unpack_kernel(lay, cap, plan, *refs):
    groups = lay.groups
    per = lay.npair // groups
    slots, (down, up, padded, cat) = refs[:groups], refs[groups:]
    me = plan[0]
    part, rmax, small = slots[0].shape[1], down.shape[2], cap // groups
    eye = (iota((part, part), 0) == iota((part, part), 1)).astype(jnp.bfloat16)
    for s, slot in enumerate(slots):
        padded[:cap, :] = slot[:cap, :]
        cat[s * small : (s + 1) * small, :] = slot[cap:, :]
        here = pl.ds(pl.multiple_of((me ^ s) * part, part), part)
        for k in range(per):
            pair = me * per + k
            start, rank = plan[lay.pair_into + pair], plan[lay.pair_rank + pair]
            rows = padded[pl.ds(pl.multiple_of(start, ALIGN), rmax), :]
            rows = jnp.where(iota(rows.shape, 0) < rank, rows, jnp.zeros_like(rows))
            down[k, here, :] = lax.dot_general(eye, rows, NT, preferred_element_type=jnp.float32).astype(down.dtype)
    for k in range(per):
        pair = me * per + k
        start, rank = plan[lay.pair_into + pair], plan[lay.pair_rank + pair]
        r = iota((rmax, cap), 0)
        place = ((r % groups) ^ me) * small + lax.div(start, jnp.int32(groups)) + r // groups
        pick = jnp.logical_and(iota((rmax, cap), 1) == place, r < rank).astype(jnp.bfloat16)
        up[k] = jnp.dot(pick, cat[...], preferred_element_type=jnp.float32).astype(up.dtype)


def unpack(lay, cap, plan, slots, features, rmax):
    part = slots[0].shape[1]
    per = lay.npair // lay.groups
    return call(
        functools.partial(unpack_kernel, lay, cap),
        [
            jax.ShapeDtypeStruct((per, features, rmax), jnp.bfloat16),
            jax.ShapeDtypeStruct((per, rmax, part), jnp.bfloat16),
        ],
        (1,),
        [whole(v.shape) for v in slots],
        [whole((per, features, rmax)), whole((per, rmax, part))],
        [pltpu.VMEM((cap + rmax, part), jnp.bfloat16), pltpu.VMEM((cap, part), jnp.bfloat16)],
        flops=2 * per * features * rmax * part,
        moved=2 * per * features * rmax,
    )(plan, *slots)


def exchange(parts, axis):
    return [parts[0]] + [swap(part, axis, s) for s, part in enumerate(parts) if s]


def gather_parts(x, axis):
    size = lax.axis_size(axis)
    parts = {0: x}
    bit = size // 2
    while bit:
        for k in sorted(parts):
            parts[k ^ bit] = swap(parts[k], axis, bit)
        bit //= 2
    return [parts[k] for k in range(size)]


def finish(lay, norm, bucket, plan, local, scales, tokens, cotangent, weight, adapter_down, back, low_part):
    width, cap = bucket
    downs = exchange(down_terms(lay, norm, width, plan, local, scales, tokens, back), "pair")
    low = sum_over(low_part, "fsdp")
    ups = exchange(up_terms(lay, norm, width, plan, local, scales, low, cotangent), "pair")
    cots = gather_parts(cotangent, "fsdp")
    input_grad = input_gradient(lay, plan, local, scales, cots, weight, adapter_down, back)
    slots = exchange(reduce_terms(lay, cap, plan, downs, ups), "pair")
    down_grad, up_grad = unpack(lay, cap, plan, slots, tokens.shape[1], back.shape[1])
    return input_grad, down_grad, up_grad


def per_device(tokens, cotangent, value_weight, adapter_down, adapter_up, pair_ids, ranks):
    rows = tokens.shape[0]
    blocks = pair_ids.shape[0]
    groups = lax.axis_size("pair")
    lay = Layout(groups, blocks, adapter_down.shape[0])
    norm = 1.0 / math.sqrt(rows * groups)
    me, mine = lax.axis_index("pair"), lax.axis_index("fsdp")
    own = (mine & 1) * (blocks // 2)
    block_ranks = ranks[pair_ids]
    scales = 32.0 / block_ranks.astype(jnp.float32)
    local = jnp.concatenate([pair_ids, block_ranks, own[None].astype(jnp.int32)])
    first = jnp.concatenate([pair_ids, own[None].astype(jnp.int32)])
    back_part = back_terms(first, cotangent, adapter_up, blocks)
    ids = gather_ids(pair_ids, "pair")
    plan = make_plan(lay, ids, ranks, jnp.stack([me, mine]).astype(jnp.int32))
    low_part = low_terms(first, tokens, adapter_down, blocks)
    back = sum_over(back_part, "fsdp")
    branches = [functools.partial(finish, lay, norm, bucket) for bucket in BUCKETS]
    return lax.switch(
        plan[2], branches, plan, local, scales, tokens, cotangent, value_weight, adapter_down, back, low_part
    )


def dense_per_device(tokens, cotangent, value_weight, adapter_down, adapter_up, pair_ids, ranks):
    rows, features = tokens.shape
    blocks = pair_ids.shape[0]
    length = rows // blocks
    npair, _, rmax = adapter_down.shape
    norm = 1.0 / math.sqrt(rows * lax.axis_size("pair"))
    mask = (jnp.arange(rmax, dtype=jnp.int32)[None, :] < ranks[:, None]).astype(jnp.float32)
    scale = 32.0 / ranks.astype(jnp.float32)
    x = tokens.reshape(blocks, length, features)
    c = cotangent.reshape(blocks, length, cotangent.shape[1])
    down, up = adapter_down[pair_ids], adapter_up[pair_ids]
    wide = {"preferred_element_type": jnp.float32}
    low = lax.psum(jnp.einsum("btd,bdr->btr", x, down, **wide).astype(jnp.bfloat16), "fsdp")
    back = lax.psum(jnp.einsum("btk,brk->btr", c, up, **wide).astype(jnp.bfloat16), "fsdp")
    rows_mask = mask[pair_ids][:, None, :]
    low = (low.astype(jnp.float32) * rows_mask).astype(jnp.bfloat16)
    back = (back.astype(jnp.float32) * rows_mask).astype(jnp.bfloat16)
    cots = lax.all_gather(cotangent, "fsdp", axis=1, tiled=True)
    base = jnp.einsum("tk,dk->td", cots, value_weight, **wide).reshape(blocks, length, features)
    factor = scale[pair_ids][:, None, None]
    input_grad = (base + factor * jnp.einsum("btr,bdr->btd", back, down, **wide)).astype(jnp.bfloat16)
    term_a = jnp.einsum("btd,btr->bdr", x, back, **wide) * (factor * norm)
    term_b = jnp.einsum("btr,btk->brk", low, c, **wide) * (factor * norm)
    onehot = (pair_ids[:, None] == jnp.arange(npair, dtype=jnp.int32)[None, :]).astype(jnp.float32)
    grads = [
        lax.psum_scatter(
            jnp.einsum("bp,bij->pij", onehot, term).astype(jnp.bfloat16), "pair", scatter_dimension=0, tiled=True
        )
        for term in (term_a, term_b)
    ]
    return input_grad.reshape(rows, features), grads[0], grads[1]


def per_shape(tokens, cotangent, value_weight, adapter_down, adapter_up, pair_ids, ranks):
    groups, shares = lax.axis_size("pair"), lax.axis_size("fsdp")
    blocks = pair_ids.shape[0]
    part = tokens.shape[1] // groups
    power = lambda v: v & (v - 1) == 0
    fits = (
        part % 128 == 0
        and part == cotangent.shape[1]
        and power(groups)
        and power(shares)
        and power(blocks)
        and min(shares, blocks) > 1
        and groups <= 8
        and BUCKETS[-1][0] >= blocks * adapter_down.shape[2]
        and BUCKETS[-1][1] >= adapter_down.shape[0] // groups * adapter_down.shape[2]
    )
    form = per_device if fits else dense_per_device
    return form(tokens, cotangent, value_weight, adapter_down, adapter_up, pair_ids, ranks)


def solution(mesh):
    placed = (
        P("pair", "fsdp"),
        P("pair", "fsdp"),
        P("fsdp", None),
        P(None, "fsdp", None),
        P(None, None, "fsdp"),
        P("pair"),
        P(),
    )
    return jax.shard_map(
        per_shape,
        mesh=mesh,
        in_specs=placed,
        out_specs=(P("pair", "fsdp"), P("pair", "fsdp", None), P("pair", None, "fsdp")),
        check_vma=False,
    )
```

```python
import functools
import math

import jax
import jax.numpy as jnp
from jax import lax
from jax.experimental import pallas as pl
from jax.experimental.pallas import tpu as pltpu
from jax.sharding import PartitionSpec as P

BUCKETS = ((256, 224), (320, 256), (352, 320), (384, 352), (448, 384), (512, 448), (512, 768))
ALIGN = 16
HEAD = 8
NT = (((1,), (1,)), ((), ()))
VMEM = 56 * 1024 * 1024
SIZES = (128, 64, 32, 16)


def call(kernel, out_shape, grid, in_specs, out_specs, scratch=(), flops=0, moved=0, prefetch=1):
    return pl.pallas_call(
        kernel,
        out_shape=out_shape,
        grid_spec=pltpu.PrefetchScalarGridSpec(
            num_scalar_prefetch=prefetch,
            grid=grid,
            in_specs=in_specs,
            out_specs=out_specs,
            scratch_shapes=list(scratch),
        ),
        compiler_params=pltpu.CompilerParams(vmem_limit_bytes=VMEM),
        cost_estimate=pl.CostEstimate(flops=flops, bytes_accessed=moved, transcendentals=0),
    )


def whole(shape):
    return pl.BlockSpec(shape, lambda i, *s: (0,) * len(shape))


def iota(shape, axis):
    return lax.broadcasted_iota(jnp.int32, shape, axis)


def aligned(index, unit=ALIGN):
    return pl.multiple_of(index, unit)


def swap(x, axis, bit):
    size = lax.axis_size(axis)
    return lax.ppermute(x, axis, [(i, i ^ bit) for i in range(size)])


def share(columns, groups):
    return -(-columns // (groups * ALIGN)) * ALIGN


class Layout:
    def __init__(self, groups, blocks, npair):
        self.groups, self.blocks, self.npair = groups, blocks, npair
        count = groups * blocks
        self.mine, self.own, self.choice = 1, 2, 3
        self.off = HEAD
        self.first = self.off + count
        self.owner = self.first + count
        self.into = self.owner + count
        self.pair = self.into + count
        self.rank = self.pair + count
        self.pair_into = self.rank + count
        self.pair_rank = self.pair_into + npair
        self.size = self.pair_rank + npair


def plan_kernel(lay, ids, ranks, where_ref, plan):
    groups, blocks, npair = lay.groups, lay.blocks, lay.npair
    per = npair // groups
    me = where_ref[0]
    for k in range(3):
        plan[k] = where_ref[k]

    def clear(p, carry):
        plan[lay.pair_rank + p] = 0
        return carry

    lax.fori_loop(0, npair, clear, 0)

    def group(g, widest):
        total = jnp.int32(0)
        pairs = [ids[(g ^ me) * blocks + b] for b in range(blocks)]
        places = []
        for b in range(blocks):
            i = g * blocks + b
            pair = pairs[b]
            rank = ranks[pair]
            plan[lay.pair_rank + pair] = rank
            place, new = total, rank
            for a in range(b):
                same = pairs[a] == pair
                place = jnp.where(same, places[a], place)
                new = jnp.where(same, 0, new)
            places.append(place)
            plan[lay.off + i] = place
            plan[lay.first + i] = new
            plan[lay.pair + i] = pair
            plan[lay.rank + i] = rank
            total = total + new
        return jnp.maximum(widest, total)

    widest = lax.fori_loop(0, groups, group, jnp.int32(0))

    def owner(o, fullest):
        total = jnp.int32(0)
        for k in range(per):
            p = o * per + k
            plan[lay.pair_into + p] = total
            total = total + plan[lay.pair_rank + p]
        return jnp.maximum(fullest, total)

    fullest = lax.fori_loop(0, groups, owner, jnp.int32(0))

    def block(i, carry):
        pair = plan[lay.pair + i]
        plan[lay.owner + i] = lax.div(pair, jnp.int32(per))
        plan[lay.into + i] = plan[lay.pair_into + pair]
        return carry

    lax.fori_loop(0, groups * blocks, block, 0)
    choice = jnp.int32(len(BUCKETS) - 1)
    for k in reversed(range(len(BUCKETS) - 1)):
        fits = jnp.logical_and(widest <= BUCKETS[k][0], fullest <= BUCKETS[k][1])
        choice = jnp.where(fits, k, choice)
    plan[lay.choice] = choice


def make_plan(lay, ids, ranks, where):
    smem = pl.BlockSpec(memory_space=pltpu.SMEM)
    return pl.pallas_call(
        functools.partial(plan_kernel, lay),
        out_shape=jax.ShapeDtypeStruct((lay.size,), jnp.int32),
        in_specs=[smem] * 3,
        out_specs=smem,
    )(ids, ranks, where)


def partial_kernel(half, dims, where_ref, ids, x, weight, kept, sent):
    step = pl.program_id(0)
    value = lax.dot_general(x[...], weight[0], dims, preferred_element_type=jnp.float32).astype(kept.dtype)

    @pl.when(step < half)
    def _():
        kept[...] = value

    @pl.when(step >= half)
    def _():
        sent[...] = value


def partial_sums(where, ids, x, weights, dims):
    rows, width = x.shape
    blocks = ids.shape[0]
    length, half = rows // blocks, blocks // 2
    rmax = math.prod(weights.shape[1:]) // width
    out = jax.ShapeDtypeStruct((rows // 2, rmax), jnp.bfloat16)
    return call(
        functools.partial(partial_kernel, half, dims),
        [out, out],
        (blocks,),
        [
            pl.BlockSpec((length, width), lambda i, w, s: (i ^ w[2], 0)),
            pl.BlockSpec((1,) + weights.shape[1:], lambda i, w, s: (s[i ^ w[2]], 0, 0)),
        ],
        [
            pl.BlockSpec((length, rmax), lambda i, w, s: (jnp.minimum(i, half - 1), 0)),
            pl.BlockSpec((length, rmax), lambda i, w, s: (jnp.maximum(i - half, 0), 0)),
        ],
        flops=2 * rows * width * rmax,
        moved=2 * rows * (width + rmax),
        prefetch=2,
    )(where, ids, x, weights)


def back_kernel(blocks, where_ref, ids, cot, *refs):
    ups, (kept, sent) = refs[:blocks], refs[blocks:]
    half, length = blocks // 2, cot.shape[0] // blocks
    for k in range(blocks):
        rows = pl.ds(aligned((k ^ where_ref[2]) * length, length), length)
        value = lax.dot_general(cot[rows, :], ups[k][0], NT, preferred_element_type=jnp.float32)
        out = kept if k < half else sent
        out[k % half * length : (k % half + 1) * length, :] = value.astype(out.dtype)


def back_sums(where, ids, cotangent, adapter_up):
    rows, width = cotangent.shape
    blocks, rmax = ids.shape[0], adapter_up.shape[1]
    shape = (rows // 2, rmax)
    adapter = lambda k: pl.BlockSpec((1, rmax, width), lambda i, w, s: (s[k ^ w[2]], 0, 0))
    return call(
        functools.partial(back_kernel, blocks),
        [jax.ShapeDtypeStruct(shape, jnp.bfloat16)] * 2,
        (1,),
        [whole(cotangent.shape)] + [adapter(k) for k in range(blocks)],
        [whole(shape)] * 2,
        flops=2 * rows * width * rmax,
        moved=2 * rows * (width + rmax),
        prefetch=2,
    )(where, ids, cotangent, *[adapter_up] * blocks)


def add(a, b):
    return (a.astype(jnp.float32) + b.astype(jnp.float32)).astype(a.dtype)


def turn(rank, value):
    shape = (value.shape[1], value.shape[1])
    eye = jnp.logical_and(iota(shape, 0) == iota(shape, 1), iota(shape, 0) < rank).astype(jnp.bfloat16)
    return lax.dot_general(eye, value, NT, preferred_element_type=jnp.float32).astype(jnp.bfloat16)


def row_factors(lay, plan, norm, width):
    me = plan[0]
    line = iota((width, 1), 0)
    each = jnp.zeros((width, 1), jnp.int32)
    for b in range(lay.blocks):
        i = me * lay.blocks + b
        begin, size = plan[lay.off + i], plan[lay.first + i]
        each = jnp.where(jnp.logical_and(line >= begin, line < begin + size), size, each)
    return jnp.where(each > 0, 32.0 / jnp.maximum(each, 1).astype(jnp.float32) * norm, 0.0)


def down_kernel(lay, norm, width, plan, x, backs, backo, *rest):
    groups, blocks = lay.groups, lay.blocks
    outs, (total, turned) = rest[:groups], rest[groups:]
    half = blocks // 2
    step = pl.program_id(0)
    length, rmax = turned.shape[2], turned.shape[1]
    me, own = plan[0], plan[lay.own]

    @pl.when(step == 0)
    def _():
        for k in range(blocks):
            rank = plan[lay.rank + me * blocks + (k ^ own)]
            source = backs if k < half else backo
            turned[k] = turn(rank, source[k % half * length : (k % half + 1) * length, :])

    total[...] = jnp.zeros_like(total)
    for k in range(blocks):
        b = k ^ own
        rows = pl.ds(aligned(plan[lay.off + me * blocks + b]), rmax)
        block = x[pl.ds(aligned(b * length, length), length), :]
        total[rows, :] += jnp.dot(turned[k], block, preferred_element_type=jnp.float32)
    term = (total[:width, :] * row_factors(lay, plan, norm, width)).astype(jnp.bfloat16)
    for s, out in enumerate(outs):

        @pl.when(step == s)
        def _(out=out):
            out[...] = term


def down_terms(lay, norm, width, plan, tokens, back):
    rows, features = tokens.shape
    part = features // lay.groups
    rmax = back[0].shape[1]
    shape = (width, part)
    return call(
        functools.partial(down_kernel, lay, norm, width),
        [jax.ShapeDtypeStruct(shape, jnp.bfloat16)] * lay.groups,
        (lay.groups,),
        [pl.BlockSpec((rows, part), lambda i, plan: (0, i ^ plan[0]))] + [whole(v.shape) for v in back],
        [whole(shape)] * lay.groups,
        [
            pltpu.VMEM((width + rmax, part), jnp.float32),
            pltpu.VMEM((lay.blocks, rmax, rows // lay.blocks), jnp.bfloat16),
        ],
        flops=2 * rows * features * rmax,
        moved=2 * features * (rows + width),
    )(plan, tokens, *back)


def up_kernel(lay, norm, width, plan, cot, lows, lowo, *rest):
    groups, blocks = lay.groups, lay.blocks
    outs, (total,) = rest[:groups], rest[groups:]
    half = blocks // 2
    length, rmax, slot = cot.shape[0] // blocks, lows.shape[1], outs[0].shape[0]
    me, own = plan[0], plan[lay.own]
    total[...] = jnp.zeros_like(total)
    for k in range(blocks):
        b = k ^ own
        i = me * blocks + b
        source = lows if k < half else lowo
        low = turn(plan[lay.rank + i], source[k % half * length : (k % half + 1) * length, :])
        block = cot[pl.ds(aligned(b * length, length), length), :]
        total[pl.ds(aligned(plan[lay.off + i]), rmax), :] += jnp.dot(low, block, preferred_element_type=jnp.float32)
    up = (total[:width, :] * row_factors(lay, plan, norm, width)).astype(jnp.bfloat16)
    column = iota((groups * slot, width), 1)
    target = ((column % groups) ^ me) * slot + column // groups
    pick = (iota((groups * slot, width), 0) == target).astype(jnp.bfloat16)
    moved = jnp.dot(pick, up, preferred_element_type=jnp.float32).astype(jnp.bfloat16)
    for s, out in enumerate(outs):
        out[...] = moved[s * slot : (s + 1) * slot, :]


def up_terms(lay, norm, width, plan, cotangent, low):
    rows, part = cotangent.shape
    shape = (share(width, lay.groups), part)
    rmax = low[0].shape[1]
    return call(
        functools.partial(up_kernel, lay, norm, width),
        [jax.ShapeDtypeStruct(shape, jnp.bfloat16)] * lay.groups,
        (1,),
        [whole(cotangent.shape)] + [whole(v.shape) for v in low],
        [whole(shape)] * lay.groups,
        [pltpu.VMEM((width + rmax, part), jnp.float32)],
        flops=2 * rows * part * rmax,
        moved=2 * part * (rows + width),
    )(plan, cotangent, *low)


def grad_kernel(lay, tiles, parts, plan, *refs):
    cots, (weight, down, backs, backo, out, cat) = refs[:parts], refs[parts:]
    step = pl.program_id(0)
    half = lay.blocks * tiles // 2
    block = lax.div(step, jnp.int32(tiles)) ^ plan[lay.own]
    mine = plan[lay.mine]
    width = cots[0].shape[1]
    for s, cot in enumerate(cots):
        cat[:, pl.ds(aligned((mine ^ s) * width, width), width)] = cot[...]
    rank = plan[lay.rank + plan[0] * lay.blocks + block]
    back = jnp.where(step < half, backs[...], backo[...])
    rows = jnp.where(iota(back.shape, 1) < rank, back, jnp.zeros_like(back))
    chunk = 512
    scale = 32.0 / jnp.full((1, chunk), rank, jnp.int32).astype(jnp.float32)
    for c in range(0, out.shape[1], chunk):
        base = lax.dot_general(cat[...], weight[c : c + chunk, :], NT, preferred_element_type=jnp.float32)
        extra = lax.dot_general(rows, down[0, c : c + chunk, :], NT, preferred_element_type=jnp.float32)
        out[:, c : c + chunk] = (base + scale * extra).astype(out.dtype)


def input_gradient(lay, plan, cots, weight, adapter_down, back):
    rows, width = cots[0].shape
    features, values = weight.shape
    blocks = lay.blocks
    tile = rows // blocks // 2
    tiles = 2
    half = blocks * tiles // 2
    rmax = back[0].shape[1]
    here = lambda i, plan: (i ^ (plan[lay.own] * tiles), 0)

    def adapter(i, plan):
        block = lax.div(i, jnp.int32(tiles)) ^ plan[lay.own]
        return (plan[lay.pair + plan[0] * blocks + block], 0, 0)

    return call(
        functools.partial(grad_kernel, lay, tiles, len(cots)),
        jax.ShapeDtypeStruct((rows, features), jnp.bfloat16),
        (rows // tile,),
        [pl.BlockSpec((tile, width), here)] * len(cots)
        + [
            whole(weight.shape),
            pl.BlockSpec((1, features, rmax), adapter),
            pl.BlockSpec((tile, rmax), lambda i, plan: (jnp.minimum(i, half - 1), 0)),
            pl.BlockSpec((tile, rmax), lambda i, plan: (jnp.maximum(i - half, 0), 0)),
        ],
        pl.BlockSpec((tile, features), here),
        [pltpu.VMEM((tile, values), jnp.bfloat16)],
        flops=2 * rows * features * (values + rmax),
        moved=2 * features * (rows + values),
    )(plan, *cots, weight, adapter_down, *back)


def reduce_kernel(lay, cap, plan, *refs):
    groups, blocks = lay.groups, lay.blocks
    parts, ups, outs = refs[:groups], refs[groups : 2 * groups], refs[2 * groups : 3 * groups]
    total, cat = refs[3 * groups :]
    me = plan[0]
    slot, small = ups[0].shape[0], outs[0].shape[0] - cap
    total[...] = jnp.zeros_like(total)
    place = iota((1, groups * slot), 1)
    target = jnp.full((1, groups * slot), -1, jnp.int32)
    for s in range(groups):
        cat[s * slot : (s + 1) * slot, :] = ups[s][...]
        for b in range(blocks):
            i = (me ^ s) * blocks + b
            rank, source = plan[lay.first + i], plan[lay.off + i]
            owner, into = plan[lay.owner + i], plan[lay.into + i]
            goal = owner * cap + into
            for size in SIZES:

                @pl.when(rank == size)
                def _(s=s, source=source, goal=goal, size=size):
                    total[pl.ds(aligned(goal), size), :] += parts[s][pl.ds(aligned(source), size), :].astype(jnp.float32)

            start = s * slot + lax.div(source, jnp.int32(groups))
            inside = jnp.logical_and(place >= start, place < start + lax.div(rank, jnp.int32(groups)))
            shift = owner * small + lax.div(into, jnp.int32(groups)) - start
            target = jnp.where(inside, place + shift, target)
    for s, out in enumerate(outs):
        owner = me ^ s
        out[:cap, :] = total[pl.ds(aligned(owner * cap), cap), :].astype(out.dtype)
    pick = (iota((groups * small, groups * slot), 0) == target).astype(jnp.bfloat16)
    total[: groups * small, :] = jnp.dot(pick, cat[...], preferred_element_type=jnp.float32)
    for s, out in enumerate(outs):
        out[cap:, :] = total[pl.ds(aligned((me ^ s) * small), small), :].astype(out.dtype)


def reduce_terms(lay, width, cap, plan, parts, ups):
    part = parts[0].shape[1]
    slot, small = share(width, lay.groups), share(cap, lay.groups)
    return call(
        functools.partial(reduce_kernel, lay, cap),
        [jax.ShapeDtypeStruct((cap + small, part), jnp.bfloat16)] * lay.groups,
        (1,),
        [whole(v.shape) for v in (*parts, *ups)],
        [whole((cap + small, part))] * lay.groups,
        [pltpu.VMEM((lay.groups * cap, part), jnp.float32), pltpu.VMEM((lay.groups * slot, part), jnp.bfloat16)],
        flops=2 * cap * width * part,
        moved=4 * lay.groups * cap * part,
    )(plan, *parts, *ups)


def unpack_kernel(lay, cap, plan, *refs):
    groups = lay.groups
    per = lay.npair // groups
    slots, (down, up, cat) = refs[:groups], refs[groups:]
    me = plan[0]
    part, rmax, small = slots[0].shape[1], down.shape[2], slots[0].shape[0] - cap
    eye = (iota((part, part), 0) == iota((part, part), 1)).astype(jnp.bfloat16)
    held = [(plan[lay.pair_into + me * per + k], plan[lay.pair_rank + me * per + k]) for k in range(per)]
    r, row = iota((cap, rmax), 1), iota((cap, rmax), 0)
    picks = [jnp.logical_and(row == r + start, r < rank).astype(jnp.bfloat16) for start, rank in held]
    pick = jnp.concatenate(picks, axis=1)
    for s, slot in enumerate(slots):
        cat[s * small : (s + 1) * small, :] = slot[cap:, :]
        here = pl.ds(aligned((me ^ s) * part, part), part)
        turned = lax.dot_general(eye, slot[:cap, :], NT, preferred_element_type=jnp.float32).astype(jnp.bfloat16)
        value = jnp.dot(turned, pick, preferred_element_type=jnp.float32).astype(down.dtype)
        for k in range(per):
            down[k, here, :] = value[:, k * rmax : (k + 1) * rmax]
    shape = (rmax, groups * small)
    r, column = iota(shape, 0), iota(shape, 1)
    place = ((r % groups) ^ me) * small + r // groups
    for k, (start, rank) in enumerate(held):
        match = column == place + lax.div(start, jnp.int32(groups))
        pick = jnp.logical_and(match, r < rank).astype(jnp.bfloat16)
        up[k] = jnp.dot(pick, cat[...], preferred_element_type=jnp.float32).astype(up.dtype)


def unpack(lay, cap, plan, slots, features, rmax):
    part = slots[0].shape[1]
    per = lay.npair // lay.groups
    shapes = [(per, features, rmax), (per, rmax, part)]
    return call(
        functools.partial(unpack_kernel, lay, cap),
        [jax.ShapeDtypeStruct(shape, jnp.bfloat16) for shape in shapes],
        (1,),
        [whole(v.shape) for v in slots],
        [whole(shape) for shape in shapes],
        [pltpu.VMEM((lay.groups * share(cap, lay.groups), part), jnp.bfloat16)],
        flops=2 * per * features * rmax * part,
        moved=2 * per * features * rmax,
    )(plan, *slots)


def exchange(parts, axis):
    return [parts[0]] + [swap(part, axis, s) for s, part in enumerate(parts) if s]


def finish(lay, norm, bucket, plan, tokens, cotangent, weight, adapter_down, back, low):
    width, cap = bucket
    parts = exchange(down_terms(lay, norm, width, plan, tokens, back), "pair")
    bit = 2
    while bit < lax.axis_size("fsdp"):
        theirs = swap(low, "fsdp", bit)
        theirs, parts[1] = lax.optimization_barrier((theirs, parts[1]))
        low = add(low, theirs)
        bit *= 2
    low = (low, swap(low, "fsdp", 1))
    ups = exchange(up_terms(lay, norm, width, plan, cotangent, low), "pair")
    features, parts[1] = lax.optimization_barrier((cotangent, parts[1]))
    cots = exchange([features] * lax.axis_size("fsdp"), "fsdp")
    sums = reduce_terms(lay, width, cap, plan, parts, ups)
    sums, cots = lax.optimization_barrier((sums, cots))
    input_grad = input_gradient(lay, plan, cots, weight, adapter_down, back)
    slots, input_grad = lax.optimization_barrier((exchange(sums, "pair"), input_grad))
    down_grad, up_grad = unpack(lay, cap, plan, slots, tokens.shape[1], back[0].shape[1])
    return input_grad, down_grad, up_grad


def per_device(tokens, cotangent, value_weight, adapter_down, adapter_up, pair_ids, ranks):
    rows = tokens.shape[0]
    blocks = pair_ids.shape[0]
    groups, shares = lax.axis_size("pair"), lax.axis_size("fsdp")
    lay = Layout(groups, blocks, adapter_down.shape[0])
    norm = 1.0 / math.sqrt(rows * groups)
    me, mine = lax.axis_index("pair"), lax.axis_index("fsdp")
    where = jnp.stack([me, mine, (mine & 1) * (blocks // 2)]).astype(jnp.int32)
    ids = jnp.concatenate([pair_ids, swap(pair_ids, "pair", 1)])
    back, back_sent = back_sums(where, pair_ids, cotangent, adapter_up)
    ids, back_sent = lax.optimization_barrier((ids, back_sent))
    back_other = swap(back_sent, "fsdp", 1)
    if groups > 2:
        ids = jnp.concatenate([ids, swap(ids, "pair", 2)])
    back, ids, tokens = lax.optimization_barrier((add(back, back_other), ids, tokens))
    bit = 4
    while bit < groups:
        ids = jnp.concatenate([ids, swap(ids, "pair", bit)])
        bit *= 2
    low, low_sent = partial_sums(where, pair_ids, tokens, adapter_down, (((1,), (0,)), ((), ())))
    plan = make_plan(lay, ids, ranks, where)
    low = add(low, swap(low_sent, "fsdp", 1))
    bit = 2
    while bit < shares:
        theirs = swap(back, "fsdp", bit)
        theirs, plan, low = lax.optimization_barrier((theirs, plan, low))
        back = add(back, theirs)
        bit *= 2
    back = (back, swap(back, "fsdp", 1))
    branches = [functools.partial(finish, lay, norm, bucket) for bucket in BUCKETS]
    return lax.switch(
        plan[lay.choice], branches, plan, tokens, cotangent, value_weight, adapter_down, back, low
    )


def dense_per_device(tokens, cotangent, value_weight, adapter_down, adapter_up, pair_ids, ranks):
    rows, features = tokens.shape
    blocks = pair_ids.shape[0]
    length = rows // blocks
    npair, _, rmax = adapter_down.shape
    norm = 1.0 / math.sqrt(rows * lax.axis_size("pair"))
    mask = (jnp.arange(rmax, dtype=jnp.int32)[None, :] < ranks[:, None]).astype(jnp.float32)
    scale = 32.0 / ranks.astype(jnp.float32)
    x = tokens.reshape(blocks, length, features)
    c = cotangent.reshape(blocks, length, cotangent.shape[1])
    down, up = adapter_down[pair_ids], adapter_up[pair_ids]
    wide = {"preferred_element_type": jnp.float32}
    low = lax.psum(jnp.einsum("btd,bdr->btr", x, down, **wide).astype(jnp.bfloat16), "fsdp")
    back = lax.psum(jnp.einsum("btk,brk->btr", c, up, **wide).astype(jnp.bfloat16), "fsdp")
    rows_mask = mask[pair_ids][:, None, :]
    low = (low.astype(jnp.float32) * rows_mask).astype(jnp.bfloat16)
    back = (back.astype(jnp.float32) * rows_mask).astype(jnp.bfloat16)
    cots = lax.all_gather(cotangent, "fsdp", axis=1, tiled=True)
    base = jnp.einsum("tk,dk->td", cots, value_weight, **wide).reshape(blocks, length, features)
    factor = scale[pair_ids][:, None, None]
    input_grad = (base + factor * jnp.einsum("btr,bdr->btd", back, down, **wide)).astype(jnp.bfloat16)
    term_a = jnp.einsum("btd,btr->bdr", x, back, **wide) * (factor * norm)
    term_b = jnp.einsum("btr,btk->brk", low, c, **wide) * (factor * norm)
    onehot = (pair_ids[:, None] == jnp.arange(npair, dtype=jnp.int32)[None, :]).astype(jnp.float32)
    grads = [
        lax.psum_scatter(
            jnp.einsum("bp,bij->pij", onehot, term).astype(jnp.bfloat16), "pair", scatter_dimension=0, tiled=True
        )
        for term in (term_a, term_b)
    ]
    return input_grad.reshape(rows, features), grads[0], grads[1]


def per_shape(tokens, cotangent, value_weight, adapter_down, adapter_up, pair_ids, ranks):
    groups, shares = lax.axis_size("pair"), lax.axis_size("fsdp")
    blocks = pair_ids.shape[0]
    part = tokens.shape[1] // groups
    power = lambda v: v & (v - 1) == 0
    fits = (
        part % 128 == 0
        and part == cotangent.shape[1]
        and power(groups)
        and power(shares)
        and power(blocks)
        and min(shares, blocks) > 1
        and groups <= 8
        and BUCKETS[-1][0] >= blocks * adapter_down.shape[2]
        and BUCKETS[-1][1] >= adapter_down.shape[0] // groups * adapter_down.shape[2]
    )
    form = per_device if fits else dense_per_device
    return form(tokens, cotangent, value_weight, adapter_down, adapter_up, pair_ids, ranks)


def solution(mesh):
    placed = (
        P("pair", "fsdp"),
        P("pair", "fsdp"),
        P("fsdp", None),
        P(None, "fsdp", None),
        P(None, None, "fsdp"),
        P("pair"),
        P(),
    )
    return jax.shard_map(
        per_shape,
        mesh=mesh,
        in_specs=placed,
        out_specs=(P("pair", "fsdp"), P("pair", "fsdp", None), P("pair", None, "fsdp")),
        check_vma=False,
    )
```

```python
import functools
import math

import jax
import jax.numpy as jnp
from jax import lax
from jax.experimental import pallas as pl
from jax.experimental.pallas import tpu as pltpu
from jax.sharding import PartitionSpec as P

BUCKETS = ((256, 224), (320, 256), (352, 320), (384, 352), (448, 384), (512, 448), (512, 768))
ALIGN = 16
HEAD = 8
NT = (((1,), (1,)), ((), ()))
VMEM = 56 * 1024 * 1024
SIZES = (128, 64, 32, 16)


def call(kernel, out_shape, grid, in_specs, out_specs, scratch=(), flops=0, moved=0, prefetch=1):
    return pl.pallas_call(
        kernel,
        out_shape=out_shape,
        grid_spec=pltpu.PrefetchScalarGridSpec(
            num_scalar_prefetch=prefetch,
            grid=grid,
            in_specs=in_specs,
            out_specs=out_specs,
            scratch_shapes=list(scratch),
        ),
        compiler_params=pltpu.CompilerParams(vmem_limit_bytes=VMEM),
        cost_estimate=pl.CostEstimate(flops=flops, bytes_accessed=moved, transcendentals=0),
    )


def whole(shape):
    return pl.BlockSpec(shape, lambda i, *s: (0,) * len(shape))


def iota(shape, axis):
    return lax.broadcasted_iota(jnp.int32, shape, axis)


def aligned(index, unit=ALIGN):
    return pl.multiple_of(index, unit)


def swap(x, axis, bit):
    size = lax.axis_size(axis)
    return lax.ppermute(x, axis, [(i, i ^ bit) for i in range(size)])


def share(columns, groups):
    return -(-columns // (groups * ALIGN)) * ALIGN


class Layout:
    def __init__(self, groups, blocks, npair):
        self.groups, self.blocks, self.npair = groups, blocks, npair
        count = groups * blocks
        self.mine, self.own, self.choice = 1, 2, 3
        self.off = HEAD
        self.first = self.off + count
        self.owner = self.first + count
        self.into = self.owner + count
        self.pair = self.into + count
        self.rank = self.pair + count
        self.pair_into = self.rank + count
        self.pair_rank = self.pair_into + npair
        self.size = self.pair_rank + npair


def plan_kernel(lay, ids, ranks, where_ref, plan):
    groups, blocks, npair = lay.groups, lay.blocks, lay.npair
    per = npair // groups
    me = where_ref[0]
    for k in range(3):
        plan[k] = where_ref[k]

    def clear(p, carry):
        plan[lay.pair_rank + p] = 0
        return carry

    lax.fori_loop(0, npair, clear, 0)

    def group(g, widest):
        total = jnp.int32(0)
        pairs = [ids[(g ^ me) * blocks + b] for b in range(blocks)]
        places = []
        for b in range(blocks):
            i = g * blocks + b
            pair = pairs[b]
            rank = ranks[pair]
            plan[lay.pair_rank + pair] = rank
            place, new = total, rank
            for a in range(b):
                same = pairs[a] == pair
                place = jnp.where(same, places[a], place)
                new = jnp.where(same, 0, new)
            places.append(place)
            plan[lay.off + i] = place
            plan[lay.first + i] = new
            plan[lay.pair + i] = pair
            plan[lay.rank + i] = rank
            total = total + new
        return jnp.maximum(widest, total)

    widest = lax.fori_loop(0, groups, group, jnp.int32(0))

    def owner(o, fullest):
        total = jnp.int32(0)
        for k in range(per):
            p = o * per + k
            plan[lay.pair_into + p] = total
            total = total + plan[lay.pair_rank + p]
        return jnp.maximum(fullest, total)

    fullest = lax.fori_loop(0, groups, owner, jnp.int32(0))

    def block(i, carry):
        pair = plan[lay.pair + i]
        plan[lay.owner + i] = lax.div(pair, jnp.int32(per))
        plan[lay.into + i] = plan[lay.pair_into + pair]
        return carry

    lax.fori_loop(0, groups * blocks, block, 0)
    choice = jnp.int32(len(BUCKETS) - 1)
    for k in reversed(range(len(BUCKETS) - 1)):
        fits = jnp.logical_and(widest <= BUCKETS[k][0], fullest <= BUCKETS[k][1])
        choice = jnp.where(fits, k, choice)
    plan[lay.choice] = choice


def make_plan(lay, ids, ranks, where):
    smem = pl.BlockSpec(memory_space=pltpu.SMEM)
    return pl.pallas_call(
        functools.partial(plan_kernel, lay),
        out_shape=jax.ShapeDtypeStruct((lay.size,), jnp.int32),
        in_specs=[smem] * 3,
        out_specs=smem,
    )(ids, ranks, where)


def rank_kernel(half, where_ref, ids, cot, up, x, down, kept, sent):
    step = pl.program_id(0)
    rmax = up.shape[1]
    back = lax.dot_general(cot[...], up[0], NT, preferred_element_type=jnp.float32).astype(kept.dtype)
    low = jnp.dot(x[...], down[0], preferred_element_type=jnp.float32).astype(kept.dtype)

    @pl.when(step < half)
    def _():
        kept[:, :rmax] = back
        kept[:, rmax:] = low

    @pl.when(step >= half)
    def _():
        sent[:, :rmax] = back
        sent[:, rmax:] = low


def rank_sums(where, ids, cotangent, adapter_up, tokens, adapter_down):
    rows, width = cotangent.shape
    features = tokens.shape[1]
    blocks, rmax = ids.shape[0], adapter_up.shape[1]
    length, half = rows // blocks, blocks // 2
    out = jax.ShapeDtypeStruct((rows // 2, 2 * rmax), jnp.bfloat16)
    rows_of = lambda i, w, s: (i ^ w[2], 0)
    pair_of = lambda i, w, s: (s[i ^ w[2]], 0, 0)
    return call(
        functools.partial(rank_kernel, half),
        [out, out],
        (blocks,),
        [
            pl.BlockSpec((length, width), rows_of),
            pl.BlockSpec((1, rmax, width), pair_of),
            pl.BlockSpec((length, features), rows_of),
            pl.BlockSpec((1, features, rmax), pair_of),
        ],
        [
            pl.BlockSpec((length, 2 * rmax), lambda i, w, s: (jnp.minimum(i, half - 1), 0)),
            pl.BlockSpec((length, 2 * rmax), lambda i, w, s: (jnp.maximum(i - half, 0), 0)),
        ],
        flops=2 * rows * (width + features) * rmax,
        moved=2 * rows * (width + features + 2 * rmax),
        prefetch=2,
    )(where, ids, cotangent, adapter_up, tokens, adapter_down)


def add(a, b):
    return (a.astype(jnp.float32) + b.astype(jnp.float32)).astype(a.dtype)


def turn(rank, value):
    shape = (value.shape[1], value.shape[1])
    eye = jnp.logical_and(iota(shape, 0) == iota(shape, 1), iota(shape, 0) < rank).astype(jnp.bfloat16)
    return lax.dot_general(eye, value, NT, preferred_element_type=jnp.float32).astype(jnp.bfloat16)


def terms_kernel(lay, norm, width, plan, x, cot, own_sums, other_sums, out, total, turned, moved):
    groups, blocks = lay.groups, lay.blocks
    half = blocks // 2
    step = pl.program_id(0)
    length, rmax, slot = turned.shape[2], turned.shape[1], out.shape[1] - width
    part = out.shape[2]
    me, own = plan[0], plan[lay.own]

    def place(k):
        i = me * blocks + (k ^ own)
        factor = 32.0 / jnp.full((1, part), plan[lay.rank + i], jnp.int32).astype(jnp.float32) * norm
        return pl.ds(aligned(plan[lay.off + i]), rmax), factor

    @pl.when(step == 0)
    def _():
        total[...] = jnp.zeros_like(total)
        for k in range(blocks):
            b = k ^ own
            rank = plan[lay.rank + me * blocks + b]
            source = own_sums if k < half else other_sums
            lines = slice(k % half * length, (k % half + 1) * length)
            turned[k] = turn(rank, source[lines, :rmax])
            low = turn(rank, source[lines, rmax:])
            rows, factor = place(k)
            block = cot[pl.ds(aligned(b * length, length), length), :]
            total[rows, :] += factor * jnp.dot(low, block, preferred_element_type=jnp.float32)
        column = iota((groups * slot, width), 1)
        target = (column % groups) * slot + column // groups
        pick = (iota((groups * slot, width), 0) == target).astype(jnp.bfloat16)
        up = total[:width, :].astype(jnp.bfloat16)
        moved[...] = jnp.dot(pick, up, preferred_element_type=jnp.float32).astype(jnp.bfloat16)

    total[...] = jnp.zeros_like(total)
    for k in range(blocks):
        rows, factor = place(k)
        block = x[pl.ds(aligned((k ^ own) * length, length), length), :]
        total[rows, :] += factor * jnp.dot(turned[k], block, preferred_element_type=jnp.float32)
    out[0, :width, :] = total[:width, :].astype(jnp.bfloat16)
    out[0, width:, :] = moved[pl.ds(aligned(step * slot), slot), :]


def group_terms(lay, norm, width, plan, tokens, cotangent, sums):
    rows, features = tokens.shape
    part = cotangent.shape[1]
    rmax = sums[0].shape[1] // 2
    slot = share(width, lay.groups)
    shape = (lay.groups, width + slot, part)
    return call(
        functools.partial(terms_kernel, lay, norm, width),
        jax.ShapeDtypeStruct(shape, jnp.bfloat16),
        (lay.groups,),
        [pl.BlockSpec((rows, part), lambda i, plan: (0, i)), whole(cotangent.shape)] + [whole(v.shape) for v in sums],
        pl.BlockSpec((1,) + shape[1:], lambda i, plan: (i, 0, 0)),
        [
            pltpu.VMEM((width + rmax, part), jnp.float32),
            pltpu.VMEM((lay.blocks, rmax, rows // lay.blocks), jnp.bfloat16),
            pltpu.VMEM((lay.groups * slot, part), jnp.bfloat16),
        ],
        flops=2 * rows * (features + part) * rmax,
        moved=2 * features * (rows + width),
    )(plan, tokens, cotangent, *sums)


def grad_kernel(lay, tiles, parts, plan, *refs):
    cots, (weight, down, backs, backo, out, cat) = refs[:parts], refs[parts:]
    step = pl.program_id(0)
    half = lay.blocks * tiles // 2
    block = lax.div(step, jnp.int32(tiles)) ^ plan[lay.own]
    mine = plan[lay.mine]
    width = cots[0].shape[1]
    for s, cot in enumerate(cots):
        cat[:, pl.ds(aligned((mine ^ s) * width, width), width)] = cot[...]
    rank = plan[lay.rank + plan[0] * lay.blocks + block]
    back = jnp.where(step < half, backs[...], backo[...])
    rows = jnp.where(iota(back.shape, 1) < rank, back, jnp.zeros_like(back))
    chunk = 512
    scale = 32.0 / jnp.full((1, chunk), rank, jnp.int32).astype(jnp.float32)
    for c in range(0, out.shape[1], chunk):
        base = lax.dot_general(cat[...], weight[c : c + chunk, :], NT, preferred_element_type=jnp.float32)
        extra = lax.dot_general(rows, down[0, c : c + chunk, :], NT, preferred_element_type=jnp.float32)
        out[:, c : c + chunk] = (base + scale * extra).astype(out.dtype)


def input_gradient(lay, plan, cots, weight, adapter_down, sums):
    rows, width = cots[0].shape
    features, values = weight.shape
    blocks = lay.blocks
    tile = rows // blocks // 2
    tiles = 2
    half = blocks * tiles // 2
    rmax = sums[0].shape[1] // 2
    here = lambda i, plan: (i ^ (plan[lay.own] * tiles), 0)

    def adapter(i, plan):
        block = lax.div(i, jnp.int32(tiles)) ^ plan[lay.own]
        return (plan[lay.pair + plan[0] * blocks + block], 0, 0)

    return call(
        functools.partial(grad_kernel, lay, tiles, len(cots)),
        jax.ShapeDtypeStruct((rows, features), jnp.bfloat16),
        (rows // tile,),
        [pl.BlockSpec((tile, width), here)] * len(cots)
        + [
            whole(weight.shape),
            pl.BlockSpec((1, features, rmax), adapter),
            pl.BlockSpec((tile, rmax), lambda i, plan: (jnp.minimum(i, half - 1), 0)),
            pl.BlockSpec((tile, rmax), lambda i, plan: (jnp.maximum(i - half, 0), 0)),
        ],
        pl.BlockSpec((tile, features), here),
        [pltpu.VMEM((tile, values), jnp.bfloat16)],
        flops=2 * rows * features * (values + rmax),
        moved=2 * features * (rows + values),
    )(plan, *cots, weight, adapter_down, *sums)


def reduce_kernel(lay, width, cap, plan, parts, *refs):
    groups, blocks = lay.groups, lay.blocks
    outs, (total, cat) = refs[:groups], refs[groups:]
    me = plan[0]
    slot, small = parts.shape[1] - width, outs[0].shape[0] - cap
    total[...] = jnp.zeros_like(total)
    place = iota((1, groups * slot), 1)
    target = jnp.full((1, groups * slot), -1, jnp.int32)
    for g in range(groups):
        cat[g * slot : (g + 1) * slot, :] = parts[g, width:, :]
        for b in range(blocks):
            i = g * blocks + b
            rank, source = plan[lay.first + i], plan[lay.off + i]
            owner, into = plan[lay.owner + i], plan[lay.into + i]
            goal = owner * cap + into
            for size in SIZES:

                @pl.when(rank == size)
                def _(g=g, source=source, goal=goal, size=size):
                    here = pl.ds(aligned(source), size)
                    total[pl.ds(aligned(goal), size), :] += parts[g, here, :].astype(jnp.float32)

            start = g * slot + lax.div(source, jnp.int32(groups))
            inside = jnp.logical_and(place >= start, place < start + lax.div(rank, jnp.int32(groups)))
            shift = owner * small + lax.div(into, jnp.int32(groups)) - start
            target = jnp.where(inside, place + shift, target)
    for s, out in enumerate(outs):
        owner = me ^ s
        out[:cap, :] = total[pl.ds(aligned(owner * cap), cap), :].astype(out.dtype)
    pick = (iota((groups * small, groups * slot), 0) == target).astype(jnp.bfloat16)
    total[: groups * small, :] = jnp.dot(pick, cat[...], preferred_element_type=jnp.float32)
    for s, out in enumerate(outs):
        out[cap:, :] = total[pl.ds(aligned((me ^ s) * small), small), :].astype(out.dtype)


def reduce_terms(lay, width, cap, plan, parts):
    part = parts.shape[2]
    slot, small = share(width, lay.groups), share(cap, lay.groups)
    return call(
        functools.partial(reduce_kernel, lay, width, cap),
        [jax.ShapeDtypeStruct((cap + small, part), jnp.bfloat16)] * lay.groups,
        (1,),
        [whole(parts.shape)],
        [whole((cap + small, part))] * lay.groups,
        [pltpu.VMEM((lay.groups * cap, part), jnp.float32), pltpu.VMEM((lay.groups * slot, part), jnp.bfloat16)],
        flops=2 * cap * width * part,
        moved=4 * lay.groups * cap * part,
    )(plan, parts)


def unpack_kernel(lay, cap, plan, *refs):
    groups = lay.groups
    per = lay.npair // groups
    slots, (down, up, cat) = refs[:groups], refs[groups:]
    me = plan[0]
    part, rmax, small = slots[0].shape[1], down.shape[2], slots[0].shape[0] - cap
    eye = (iota((part, part), 0) == iota((part, part), 1)).astype(jnp.bfloat16)
    held = [(plan[lay.pair_into + me * per + k], plan[lay.pair_rank + me * per + k]) for k in range(per)]
    r, row = iota((cap, rmax), 1), iota((cap, rmax), 0)
    picks = [jnp.logical_and(row == r + start, r < rank).astype(jnp.bfloat16) for start, rank in held]
    pick = jnp.concatenate(picks, axis=1)
    for s, slot in enumerate(slots):
        cat[s * small : (s + 1) * small, :] = slot[cap:, :]
        here = pl.ds(aligned((me ^ s) * part, part), part)
        turned = lax.dot_general(eye, slot[:cap, :], NT, preferred_element_type=jnp.float32).astype(jnp.bfloat16)
        value = jnp.dot(turned, pick, preferred_element_type=jnp.float32).astype(down.dtype)
        for k in range(per):
            down[k, here, :] = value[:, k * rmax : (k + 1) * rmax]
    shape = (rmax, groups * small)
    r, column = iota(shape, 0), iota(shape, 1)
    place = ((r % groups) ^ me) * small + r // groups
    for k, (start, rank) in enumerate(held):
        match = column == place + lax.div(start, jnp.int32(groups))
        pick = jnp.logical_and(match, r < rank).astype(jnp.bfloat16)
        up[k] = jnp.dot(pick, cat[...], preferred_element_type=jnp.float32).astype(up.dtype)


def unpack(lay, cap, plan, slots, features, rmax):
    part = slots[0].shape[1]
    per = lay.npair // lay.groups
    shapes = [(per, features, rmax), (per, rmax, part)]
    return call(
        functools.partial(unpack_kernel, lay, cap),
        [jax.ShapeDtypeStruct(shape, jnp.bfloat16) for shape in shapes],
        (1,),
        [whole(v.shape) for v in slots],
        [whole(shape) for shape in shapes],
        [pltpu.VMEM((lay.groups * share(cap, lay.groups), part), jnp.bfloat16)],
        flops=2 * per * features * rmax * part,
        moved=2 * per * features * rmax,
    )(plan, *slots)


def exchange(parts, axis):
    return [parts[0]] + [swap(part, axis, s) for s, part in enumerate(parts) if s]


def finish(lay, norm, bucket, plan, tokens, cotangent, weight, adapter_down, sums):
    width, cap = bucket
    parts = group_terms(lay, norm, width, plan, tokens, cotangent, sums)
    cots = exchange([cotangent] * lax.axis_size("fsdp"), "fsdp")
    parts = lax.all_to_all(parts, "pair", split_axis=0, concat_axis=0, tiled=True)
    terms = reduce_terms(lay, width, cap, plan, parts)
    terms, cots = lax.optimization_barrier((terms, cots))
    input_grad = input_gradient(lay, plan, cots, weight, adapter_down, sums)
    slots, input_grad = lax.optimization_barrier((exchange(terms, "pair"), input_grad))
    down_grad, up_grad = unpack(lay, cap, plan, slots, tokens.shape[1], adapter_down.shape[2])
    return input_grad, down_grad, up_grad


def per_device(tokens, cotangent, value_weight, adapter_down, adapter_up, pair_ids, ranks):
    rows = tokens.shape[0]
    blocks = pair_ids.shape[0]
    groups, shares = lax.axis_size("pair"), lax.axis_size("fsdp")
    lay = Layout(groups, blocks, adapter_down.shape[0])
    norm = 1.0 / math.sqrt(rows * groups)
    me, mine = lax.axis_index("pair"), lax.axis_index("fsdp")
    where = jnp.stack([me, mine, (mine & 1) * (blocks // 2)]).astype(jnp.int32)
    ids = jnp.concatenate([pair_ids, swap(pair_ids, "pair", 1)])
    kept, sent = rank_sums(where, pair_ids, cotangent, adapter_up, tokens, adapter_down)
    ids, sent = lax.optimization_barrier((ids, sent))
    sums = add(kept, swap(sent, "fsdp", 1))
    if groups > 2:
        ids = jnp.concatenate([ids, swap(ids, "pair", 2)])
    sums, ids = lax.optimization_barrier((sums, ids))
    bit = 4
    while bit < groups:
        ids = jnp.concatenate([ids, swap(ids, "pair", bit)])
        bit *= 2
    plan = make_plan(lay, ids, ranks, where)
    bit = 2
    while bit < shares:
        theirs = swap(sums, "fsdp", bit)
        theirs, plan = lax.optimization_barrier((theirs, plan))
        sums = add(sums, theirs)
        bit *= 2
    sums = (sums, swap(sums, "fsdp", 1))
    branches = [functools.partial(finish, lay, norm, bucket) for bucket in BUCKETS]
    return lax.switch(plan[lay.choice], branches, plan, tokens, cotangent, value_weight, adapter_down, sums)


def dense_per_device(tokens, cotangent, value_weight, adapter_down, adapter_up, pair_ids, ranks):
    rows, features = tokens.shape
    blocks = pair_ids.shape[0]
    length = rows // blocks
    npair, _, rmax = adapter_down.shape
    norm = 1.0 / math.sqrt(rows * lax.axis_size("pair"))
    mask = (jnp.arange(rmax, dtype=jnp.int32)[None, :] < ranks[:, None]).astype(jnp.float32)
    scale = 32.0 / ranks.astype(jnp.float32)
    x = tokens.reshape(blocks, length, features)
    c = cotangent.reshape(blocks, length, cotangent.shape[1])
    down, up = adapter_down[pair_ids], adapter_up[pair_ids]
    wide = {"preferred_element_type": jnp.float32}
    low = lax.psum(jnp.einsum("btd,bdr->btr", x, down, **wide).astype(jnp.bfloat16), "fsdp")
    back = lax.psum(jnp.einsum("btk,brk->btr", c, up, **wide).astype(jnp.bfloat16), "fsdp")
    rows_mask = mask[pair_ids][:, None, :]
    low = (low.astype(jnp.float32) * rows_mask).astype(jnp.bfloat16)
    back = (back.astype(jnp.float32) * rows_mask).astype(jnp.bfloat16)
    cots = lax.all_gather(cotangent, "fsdp", axis=1, tiled=True)
    base = jnp.einsum("tk,dk->td", cots, value_weight, **wide).reshape(blocks, length, features)
    factor = scale[pair_ids][:, None, None]
    input_grad = (base + factor * jnp.einsum("btr,bdr->btd", back, down, **wide)).astype(jnp.bfloat16)
    term_a = jnp.einsum("btd,btr->bdr", x, back, **wide) * (factor * norm)
    term_b = jnp.einsum("btr,btk->brk", low, c, **wide) * (factor * norm)
    onehot = (pair_ids[:, None] == jnp.arange(npair, dtype=jnp.int32)[None, :]).astype(jnp.float32)
    grads = [
        lax.psum_scatter(
            jnp.einsum("bp,bij->pij", onehot, term).astype(jnp.bfloat16), "pair", scatter_dimension=0, tiled=True
        )
        for term in (term_a, term_b)
    ]
    return input_grad.reshape(rows, features), grads[0], grads[1]


def per_shape(tokens, cotangent, value_weight, adapter_down, adapter_up, pair_ids, ranks):
    groups, shares = lax.axis_size("pair"), lax.axis_size("fsdp")
    blocks = pair_ids.shape[0]
    part = tokens.shape[1] // groups
    power = lambda v: v & (v - 1) == 0
    fits = (
        part % 128 == 0
        and part == cotangent.shape[1]
        and power(groups)
        and power(shares)
        and power(blocks)
        and min(shares, blocks) > 1
        and groups <= 8
        and BUCKETS[-1][0] >= blocks * adapter_down.shape[2]
        and BUCKETS[-1][1] >= adapter_down.shape[0] // groups * adapter_down.shape[2]
    )
    form = per_device if fits else dense_per_device
    return form(tokens, cotangent, value_weight, adapter_down, adapter_up, pair_ids, ranks)


def solution(mesh):
    placed = (
        P("pair", "fsdp"),
        P("pair", "fsdp"),
        P("fsdp", None),
        P(None, "fsdp", None),
        P(None, None, "fsdp"),
        P("pair"),
        P(),
    )
    return jax.shard_map(
        per_shape,
        mesh=mesh,
        in_specs=placed,
        out_specs=(P("pair", "fsdp"), P("pair", "fsdp", None), P("pair", None, "fsdp")),
        check_vma=False,
    )
```

```python
import functools
import math

import jax
import jax.numpy as jnp
from jax import lax
from jax.experimental import pallas as pl
from jax.experimental.pallas import tpu as pltpu
from jax.sharding import PartitionSpec as P

BUCKETS = ((256, 224), (320, 256), (352, 320), (384, 352), (448, 384), (512, 448), (512, 768))
ALIGN = 16
HEAD = 8
NT = (((1,), (1,)), ((), ()))
VMEM = 56 * 1024 * 1024
SIZES = (128, 64, 32, 16)


def call(kernel, out_shape, grid, in_specs, out_specs, scratch=(), flops=0, moved=0, prefetch=1):
    return pl.pallas_call(
        kernel,
        out_shape=out_shape,
        grid_spec=pltpu.PrefetchScalarGridSpec(
            num_scalar_prefetch=prefetch,
            grid=grid,
            in_specs=in_specs,
            out_specs=out_specs,
            scratch_shapes=list(scratch),
        ),
        compiler_params=pltpu.CompilerParams(vmem_limit_bytes=VMEM),
        cost_estimate=pl.CostEstimate(flops=flops, bytes_accessed=moved, transcendentals=0),
    )


def whole(shape):
    return pl.BlockSpec(shape, lambda i, *s: (0,) * len(shape))


def iota(shape, axis):
    return lax.broadcasted_iota(jnp.int32, shape, axis)


def aligned(index, unit=ALIGN):
    return pl.multiple_of(index, unit)


def swap(x, axis, bit):
    size = lax.axis_size(axis)
    return lax.ppermute(x, axis, [(i, i ^ bit) for i in range(size)])


def share(columns, groups):
    return -(-columns // (groups * ALIGN)) * ALIGN


class Layout:
    def __init__(self, groups, blocks, npair):
        self.groups, self.blocks, self.npair = groups, blocks, npair
        count = groups * blocks
        self.mine, self.own, self.choice = 1, 2, 3
        self.off = HEAD
        self.first = self.off + count
        self.owner = self.first + count
        self.into = self.owner + count
        self.pair = self.into + count
        self.rank = self.pair + count
        self.pair_into = self.rank + count
        self.pair_rank = self.pair_into + npair
        self.size = self.pair_rank + npair


def plan_kernel(lay, ids, ranks, where_ref, plan):
    groups, blocks, npair = lay.groups, lay.blocks, lay.npair
    per = npair // groups
    me = where_ref[0]
    for k in range(3):
        plan[k] = where_ref[k]

    def clear(p, carry):
        plan[lay.pair_rank + p] = 0
        return carry

    lax.fori_loop(0, npair, clear, 0)

    def group(g, widest):
        total = jnp.int32(0)
        pairs = [ids[(g ^ me) * blocks + b] for b in range(blocks)]
        places = []
        for b in range(blocks):
            i = g * blocks + b
            pair = pairs[b]
            rank = ranks[pair]
            plan[lay.pair_rank + pair] = rank
            place, new = total, rank
            for a in range(b):
                same = pairs[a] == pair
                place = jnp.where(same, places[a], place)
                new = jnp.where(same, 0, new)
            places.append(place)
            plan[lay.off + i] = place
            plan[lay.first + i] = new
            plan[lay.pair + i] = pair
            plan[lay.rank + i] = rank
            total = total + new
        return jnp.maximum(widest, total)

    widest = lax.fori_loop(0, groups, group, jnp.int32(0))

    def owner(o, fullest):
        total = jnp.int32(0)
        for k in range(per):
            p = o * per + k
            plan[lay.pair_into + p] = total
            total = total + plan[lay.pair_rank + p]
        return jnp.maximum(fullest, total)

    fullest = lax.fori_loop(0, groups, owner, jnp.int32(0))

    def block(i, carry):
        pair = plan[lay.pair + i]
        plan[lay.owner + i] = lax.div(pair, jnp.int32(per))
        plan[lay.into + i] = plan[lay.pair_into + pair]
        return carry

    lax.fori_loop(0, groups * blocks, block, 0)
    choice = jnp.int32(len(BUCKETS) - 1)
    for k in reversed(range(len(BUCKETS) - 1)):
        fits = jnp.logical_and(widest <= BUCKETS[k][0], fullest <= BUCKETS[k][1])
        choice = jnp.where(fits, k, choice)
    plan[lay.choice] = choice


def make_plan(lay, ids, ranks, where):
    smem = pl.BlockSpec(memory_space=pltpu.SMEM)
    return pl.pallas_call(
        functools.partial(plan_kernel, lay),
        out_shape=jax.ShapeDtypeStruct((lay.size,), jnp.int32),
        in_specs=[smem] * 3,
        out_specs=smem,
    )(ids, ranks, where)


def rank_kernel(half, where_ref, ids, cot, up, x, down, kept, sent):
    step = pl.program_id(0)
    rmax = up.shape[1]
    back = lax.dot_general(cot[...], up[0], NT, preferred_element_type=jnp.float32).astype(kept.dtype)
    low = jnp.dot(x[...], down[0], preferred_element_type=jnp.float32).astype(kept.dtype)

    @pl.when(step < half)
    def _():
        kept[:, :rmax] = back
        kept[:, rmax:] = low

    @pl.when(step >= half)
    def _():
        sent[:, :rmax] = back
        sent[:, rmax:] = low


def rank_sums(where, ids, cotangent, adapter_up, tokens, adapter_down):
    rows, width = cotangent.shape
    features = tokens.shape[1]
    blocks, rmax = ids.shape[0], adapter_up.shape[1]
    length, half = rows // blocks, blocks // 2
    out = jax.ShapeDtypeStruct((rows // 2, 2 * rmax), jnp.bfloat16)
    rows_of = lambda i, w, s: (i ^ w[2], 0)
    pair_of = lambda i, w, s: (s[i ^ w[2]], 0, 0)
    return call(
        functools.partial(rank_kernel, half),
        [out, out],
        (blocks,),
        [
            pl.BlockSpec((length, width), rows_of),
            pl.BlockSpec((1, rmax, width), pair_of),
            pl.BlockSpec((length, features), rows_of),
            pl.BlockSpec((1, features, rmax), pair_of),
        ],
        [
            pl.BlockSpec((length, 2 * rmax), lambda i, w, s: (jnp.minimum(i, half - 1), 0)),
            pl.BlockSpec((length, 2 * rmax), lambda i, w, s: (jnp.maximum(i - half, 0), 0)),
        ],
        flops=2 * rows * (width + features) * rmax,
        moved=2 * rows * (width + features + 2 * rmax),
        prefetch=2,
    )(where, ids, cotangent, adapter_up, tokens, adapter_down)


def add(a, b):
    return (a.astype(jnp.float32) + b.astype(jnp.float32)).astype(a.dtype)


def turn(rank, value):
    shape = (value.shape[1], value.shape[1])
    eye = jnp.logical_and(iota(shape, 0) == iota(shape, 1), iota(shape, 0) < rank).astype(jnp.bfloat16)
    return lax.dot_general(eye, value, NT, preferred_element_type=jnp.float32).astype(jnp.bfloat16)


def terms_kernel(lay, norm, width, plan, x, cot, own_sums, other_sums, out, total, turned, moved):
    groups, blocks = lay.groups, lay.blocks
    half = blocks // 2
    step = pl.program_id(0)
    length, rmax, slot = turned.shape[2], turned.shape[1], out.shape[1] - width
    part = out.shape[2]
    me, own = plan[0], plan[lay.own]

    def place(k):
        i = me * blocks + (k ^ own)
        factor = 32.0 / jnp.full((1, part), plan[lay.rank + i], jnp.int32).astype(jnp.float32) * norm
        return pl.ds(aligned(plan[lay.off + i]), rmax), factor

    @pl.when(step == 0)
    def _():
        total[...] = jnp.zeros_like(total)
        for k in range(blocks):
            b = k ^ own
            rank = plan[lay.rank + me * blocks + b]
            source = own_sums if k < half else other_sums
            lines = slice(k % half * length, (k % half + 1) * length)
            turned[k] = turn(rank, source[lines, :rmax])
            low = turn(rank, source[lines, rmax:])
            rows, factor = place(k)
            block = cot[pl.ds(aligned(b * length, length), length), :]
            total[rows, :] += factor * jnp.dot(low, block, preferred_element_type=jnp.float32)
        column = iota((groups * slot, width), 1)
        target = (column % groups) * slot + column // groups
        pick = (iota((groups * slot, width), 0) == target).astype(jnp.bfloat16)
        up = total[:width, :].astype(jnp.bfloat16)
        moved[...] = jnp.dot(pick, up, preferred_element_type=jnp.float32).astype(jnp.bfloat16)

    total[...] = jnp.zeros_like(total)
    for k in range(blocks):
        rows, factor = place(k)
        block = x[pl.ds(aligned((k ^ own) * length, length), length), :]
        total[rows, :] += factor * jnp.dot(turned[k], block, preferred_element_type=jnp.float32)
    out[0, :width, :] = total[:width, :].astype(jnp.bfloat16)
    out[0, width:, :] = moved[pl.ds(aligned(step * slot), slot), :]


def group_terms(lay, norm, width, plan, tokens, cotangent, sums):
    rows, features = tokens.shape
    part = cotangent.shape[1]
    rmax = sums[0].shape[1] // 2
    slot = share(width, lay.groups)
    shape = (lay.groups, width + slot, part)
    return call(
        functools.partial(terms_kernel, lay, norm, width),
        jax.ShapeDtypeStruct(shape, jnp.bfloat16),
        (lay.groups,),
        [pl.BlockSpec((rows, part), lambda i, plan: (0, i)), whole(cotangent.shape)] + [whole(v.shape) for v in sums],
        pl.BlockSpec((1,) + shape[1:], lambda i, plan: (i, 0, 0)),
        [
            pltpu.VMEM((width + rmax, part), jnp.float32),
            pltpu.VMEM((lay.blocks, rmax, rows // lay.blocks), jnp.bfloat16),
            pltpu.VMEM((lay.groups * slot, part), jnp.bfloat16),
        ],
        flops=2 * rows * (features + part) * rmax,
        moved=2 * features * (rows + width),
    )(plan, tokens, cotangent, *sums)


def grad_kernel(lay, tiles, parts, plan, *refs):
    cots, (weight, down, backs, backo, out, cat) = refs[:parts], refs[parts:]
    step = pl.program_id(0)
    half = lay.blocks * tiles // 2
    block = lax.div(step, jnp.int32(tiles)) ^ plan[lay.own]
    mine = plan[lay.mine]
    width = cots[0].shape[1]
    for s, cot in enumerate(cots):
        cat[:, pl.ds(aligned((mine ^ s) * width, width), width)] = cot[...]
    rank = plan[lay.rank + plan[0] * lay.blocks + block]
    back = jnp.where(step < half, backs[...], backo[...])
    rows = jnp.where(iota(back.shape, 1) < rank, back, jnp.zeros_like(back))
    chunk = 512
    scale = 32.0 / jnp.full((1, chunk), rank, jnp.int32).astype(jnp.float32)
    for c in range(0, out.shape[1], chunk):
        base = lax.dot_general(cat[...], weight[c : c + chunk, :], NT, preferred_element_type=jnp.float32)
        extra = lax.dot_general(rows, down[0, c : c + chunk, :], NT, preferred_element_type=jnp.float32)
        out[:, c : c + chunk] = (base + scale * extra).astype(out.dtype)


def input_gradient(lay, plan, cots, weight, adapter_down, sums):
    rows, width = cots[0].shape
    features, values = weight.shape
    blocks = lay.blocks
    tile = rows // blocks // 2
    tiles = 2
    half = blocks * tiles // 2
    rmax = sums[0].shape[1] // 2
    here = lambda i, plan: (i ^ (plan[lay.own] * tiles), 0)

    def adapter(i, plan):
        block = lax.div(i, jnp.int32(tiles)) ^ plan[lay.own]
        return (plan[lay.pair + plan[0] * blocks + block], 0, 0)

    return call(
        functools.partial(grad_kernel, lay, tiles, len(cots)),
        jax.ShapeDtypeStruct((rows, features), jnp.bfloat16),
        (rows // tile,),
        [pl.BlockSpec((tile, width), here)] * len(cots)
        + [
            whole(weight.shape),
            pl.BlockSpec((1, features, rmax), adapter),
            pl.BlockSpec((tile, rmax), lambda i, plan: (jnp.minimum(i, half - 1), 0)),
            pl.BlockSpec((tile, rmax), lambda i, plan: (jnp.maximum(i - half, 0), 0)),
        ],
        pl.BlockSpec((tile, features), here),
        [pltpu.VMEM((tile, values), jnp.bfloat16)],
        flops=2 * rows * features * (values + rmax),
        moved=2 * features * (rows + values),
    )(plan, *cots, weight, adapter_down, *sums)


def reduce_kernel(lay, width, cap, plan, parts, out, total, cat):
    groups, blocks = lay.groups, lay.blocks
    slot, small = parts.shape[1] - width, out.shape[1] - cap
    total[...] = jnp.zeros_like(total)
    place = iota((1, groups * slot), 1)
    target = jnp.full((1, groups * slot), -1, jnp.int32)
    for g in range(groups):
        cat[g * slot : (g + 1) * slot, :] = parts[g, width:, :]
        for b in range(blocks):
            i = g * blocks + b
            rank, source = plan[lay.first + i], plan[lay.off + i]
            owner, into = plan[lay.owner + i], plan[lay.into + i]
            goal = owner * cap + into
            for size in SIZES:

                @pl.when(rank == size)
                def _(g=g, source=source, goal=goal, size=size):
                    here = pl.ds(aligned(source), size)
                    total[pl.ds(aligned(goal), size), :] += parts[g, here, :].astype(jnp.float32)

            start = g * slot + lax.div(source, jnp.int32(groups))
            inside = jnp.logical_and(place >= start, place < start + lax.div(rank, jnp.int32(groups)))
            shift = owner * small + lax.div(into, jnp.int32(groups)) - start
            target = jnp.where(inside, place + shift, target)
    for o in range(groups):
        out[o, :cap, :] = total[o * cap : (o + 1) * cap, :].astype(out.dtype)
    pick = (iota((groups * small, groups * slot), 0) == target).astype(jnp.bfloat16)
    sums = jnp.dot(pick, cat[...], preferred_element_type=jnp.float32).astype(out.dtype)
    for o in range(groups):
        out[o, cap:, :] = sums[o * small : (o + 1) * small, :]


def reduce_terms(lay, width, cap, plan, parts):
    part = parts.shape[2]
    slot, small = share(width, lay.groups), share(cap, lay.groups)
    return call(
        functools.partial(reduce_kernel, lay, width, cap),
        jax.ShapeDtypeStruct((lay.groups, cap + small, part), jnp.bfloat16),
        (1,),
        [whole(parts.shape)],
        whole((lay.groups, cap + small, part)),
        [pltpu.VMEM((lay.groups * cap, part), jnp.float32), pltpu.VMEM((lay.groups * slot, part), jnp.bfloat16)],
        flops=2 * cap * width * part,
        moved=4 * lay.groups * cap * part,
    )(plan, parts)


def unpack_kernel(lay, cap, plan, slots, down, up, cat):
    groups = lay.groups
    per = lay.npair // groups
    me = plan[0]
    part, rmax, small = slots.shape[2], down.shape[2], slots.shape[1] - cap
    eye = (iota((part, part), 0) == iota((part, part), 1)).astype(jnp.bfloat16)
    held = [(plan[lay.pair_into + me * per + k], plan[lay.pair_rank + me * per + k]) for k in range(per)]
    r, row = iota((cap, rmax), 1), iota((cap, rmax), 0)
    picks = [jnp.logical_and(row == r + start, r < rank).astype(jnp.bfloat16) for start, rank in held]
    pick = jnp.concatenate(picks, axis=1)
    for s in range(groups):
        cat[s * small : (s + 1) * small, :] = slots[s, cap:, :]
        here = slice(s * part, (s + 1) * part)
        turned = lax.dot_general(eye, slots[s, :cap, :], NT, preferred_element_type=jnp.float32).astype(jnp.bfloat16)
        value = jnp.dot(turned, pick, preferred_element_type=jnp.float32).astype(down.dtype)
        for k in range(per):
            down[k, here, :] = value[:, k * rmax : (k + 1) * rmax]
    shape = (rmax, groups * small)
    r, column = iota(shape, 0), iota(shape, 1)
    place = (r % groups) * small + r // groups
    for k, (start, rank) in enumerate(held):
        match = column == place + lax.div(start, jnp.int32(groups))
        pick = jnp.logical_and(match, r < rank).astype(jnp.bfloat16)
        up[k] = jnp.dot(pick, cat[...], preferred_element_type=jnp.float32).astype(up.dtype)


def unpack(lay, cap, plan, slots, features, rmax):
    part = slots.shape[2]
    per = lay.npair // lay.groups
    shapes = [(per, features, rmax), (per, rmax, part)]
    return call(
        functools.partial(unpack_kernel, lay, cap),
        [jax.ShapeDtypeStruct(shape, jnp.bfloat16) for shape in shapes],
        (1,),
        [whole(slots.shape)],
        [whole(shape) for shape in shapes],
        [pltpu.VMEM((lay.groups * share(cap, lay.groups), part), jnp.bfloat16)],
        flops=2 * per * features * rmax * part,
        moved=2 * per * features * rmax,
    )(plan, slots)


def exchange(parts, axis):
    return [parts[0]] + [swap(part, axis, s) for s, part in enumerate(parts) if s]


def spread(parts):
    return lax.all_to_all(parts, "pair", split_axis=0, concat_axis=0, tiled=True)


def finish(lay, norm, bucket, plan, tokens, cotangent, weight, adapter_down, sums):
    width, cap = bucket
    parts = group_terms(lay, norm, width, plan, tokens, cotangent, sums)
    cots = exchange([cotangent] * lax.axis_size("fsdp"), "fsdp")
    terms = reduce_terms(lay, width, cap, plan, spread(parts))
    _, cots = lax.optimization_barrier((terms, cots))
    input_grad = input_gradient(lay, plan, cots, weight, adapter_down, sums)
    slots, input_grad = lax.optimization_barrier((spread(terms), input_grad))
    down_grad, up_grad = unpack(lay, cap, plan, slots, tokens.shape[1], adapter_down.shape[2])
    return input_grad, down_grad, up_grad


def per_device(tokens, cotangent, value_weight, adapter_down, adapter_up, pair_ids, ranks):
    rows = tokens.shape[0]
    blocks = pair_ids.shape[0]
    groups, shares = lax.axis_size("pair"), lax.axis_size("fsdp")
    lay = Layout(groups, blocks, adapter_down.shape[0])
    norm = 1.0 / math.sqrt(rows * groups)
    me, mine = lax.axis_index("pair"), lax.axis_index("fsdp")
    where = jnp.stack([me, mine, (mine & 1) * (blocks // 2)]).astype(jnp.int32)
    ids = jnp.concatenate([pair_ids, swap(pair_ids, "pair", 1)])
    kept, sent = rank_sums(where, pair_ids, cotangent, adapter_up, tokens, adapter_down)
    ids, sent = lax.optimization_barrier((ids, sent))
    sums = add(kept, swap(sent, "fsdp", 1))
    if groups > 2:
        ids = jnp.concatenate([ids, swap(ids, "pair", 2)])
    sums, ids = lax.optimization_barrier((sums, ids))
    bit = 4
    while bit < groups:
        ids = jnp.concatenate([ids, swap(ids, "pair", bit)])
        bit *= 2
    plan = make_plan(lay, ids, ranks, where)
    bit = 2
    while bit < shares:
        theirs = swap(sums, "fsdp", bit)
        theirs, plan = lax.optimization_barrier((theirs, plan))
        sums = add(sums, theirs)
        bit *= 2
    sums = (sums, swap(sums, "fsdp", 1))
    branches = [functools.partial(finish, lay, norm, bucket) for bucket in BUCKETS]
    return lax.switch(plan[lay.choice], branches, plan, tokens, cotangent, value_weight, adapter_down, sums)


def dense_per_device(tokens, cotangent, value_weight, adapter_down, adapter_up, pair_ids, ranks):
    rows, features = tokens.shape
    blocks = pair_ids.shape[0]
    length = rows // blocks
    npair, _, rmax = adapter_down.shape
    norm = 1.0 / math.sqrt(rows * lax.axis_size("pair"))
    mask = (jnp.arange(rmax, dtype=jnp.int32)[None, :] < ranks[:, None]).astype(jnp.float32)
    scale = 32.0 / ranks.astype(jnp.float32)
    x = tokens.reshape(blocks, length, features)
    c = cotangent.reshape(blocks, length, cotangent.shape[1])
    down, up = adapter_down[pair_ids], adapter_up[pair_ids]
    wide = {"preferred_element_type": jnp.float32}
    low = lax.psum(jnp.einsum("btd,bdr->btr", x, down, **wide).astype(jnp.bfloat16), "fsdp")
    back = lax.psum(jnp.einsum("btk,brk->btr", c, up, **wide).astype(jnp.bfloat16), "fsdp")
    rows_mask = mask[pair_ids][:, None, :]
    low = (low.astype(jnp.float32) * rows_mask).astype(jnp.bfloat16)
    back = (back.astype(jnp.float32) * rows_mask).astype(jnp.bfloat16)
    cots = lax.all_gather(cotangent, "fsdp", axis=1, tiled=True)
    base = jnp.einsum("tk,dk->td", cots, value_weight, **wide).reshape(blocks, length, features)
    factor = scale[pair_ids][:, None, None]
    input_grad = (base + factor * jnp.einsum("btr,bdr->btd", back, down, **wide)).astype(jnp.bfloat16)
    term_a = jnp.einsum("btd,btr->bdr", x, back, **wide) * (factor * norm)
    term_b = jnp.einsum("btr,btk->brk", low, c, **wide) * (factor * norm)
    onehot = (pair_ids[:, None] == jnp.arange(npair, dtype=jnp.int32)[None, :]).astype(jnp.float32)
    grads = [
        lax.psum_scatter(
            jnp.einsum("bp,bij->pij", onehot, term).astype(jnp.bfloat16), "pair", scatter_dimension=0, tiled=True
        )
        for term in (term_a, term_b)
    ]
    return input_grad.reshape(rows, features), grads[0], grads[1]


def per_shape(tokens, cotangent, value_weight, adapter_down, adapter_up, pair_ids, ranks):
    groups, shares = lax.axis_size("pair"), lax.axis_size("fsdp")
    blocks = pair_ids.shape[0]
    part = tokens.shape[1] // groups
    power = lambda v: v & (v - 1) == 0
    fits = (
        part % 128 == 0
        and part == cotangent.shape[1]
        and power(groups)
        and power(shares)
        and power(blocks)
        and min(shares, blocks) > 1
        and groups <= 8
        and BUCKETS[-1][0] >= blocks * adapter_down.shape[2]
        and BUCKETS[-1][1] >= adapter_down.shape[0] // groups * adapter_down.shape[2]
    )
    form = per_device if fits else dense_per_device
    return form(tokens, cotangent, value_weight, adapter_down, adapter_up, pair_ids, ranks)


def solution(mesh):
    placed = (
        P("pair", "fsdp"),
        P("pair", "fsdp"),
        P("fsdp", None),
        P(None, "fsdp", None),
        P(None, None, "fsdp"),
        P("pair"),
        P(),
    )
    return jax.shard_map(
        per_shape,
        mesh=mesh,
        in_specs=placed,
        out_specs=(P("pair", "fsdp"), P("pair", "fsdp", None), P("pair", None, "fsdp")),
        check_vma=False,
    )
```

```python
import functools
import math

import jax
import jax.numpy as jnp
from jax import lax
from jax.experimental import pallas as pl
from jax.experimental.pallas import tpu as pltpu
from jax.sharding import PartitionSpec as P

BUCKETS = ((256, 224), (320, 256), (352, 320), (384, 352), (448, 384), (512, 448), (512, 768))
ALIGN = 16
HEAD = 8
NT = (((1,), (1,)), ((), ()))
VMEM = 56 * 1024 * 1024
SIZES = (128, 64, 32, 16)


def call(kernel, out_shape, grid, in_specs, out_specs, scratch=(), flops=0, moved=0, prefetch=1):
    return pl.pallas_call(
        kernel,
        out_shape=out_shape,
        grid_spec=pltpu.PrefetchScalarGridSpec(
            num_scalar_prefetch=prefetch,
            grid=grid,
            in_specs=in_specs,
            out_specs=out_specs,
            scratch_shapes=list(scratch),
        ),
        compiler_params=pltpu.CompilerParams(vmem_limit_bytes=VMEM),
        cost_estimate=pl.CostEstimate(flops=flops, bytes_accessed=moved, transcendentals=0),
    )


def whole(shape):
    return pl.BlockSpec(shape, lambda i, *s: (0,) * len(shape))


def iota(shape, axis):
    return lax.broadcasted_iota(jnp.int32, shape, axis)


def aligned(index, unit=ALIGN):
    return pl.multiple_of(index, unit)


def swap(x, axis, bit):
    size = lax.axis_size(axis)
    return lax.ppermute(x, axis, [(i, i ^ bit) for i in range(size)])


def share(columns, groups):
    return -(-columns // (groups * ALIGN)) * ALIGN


class Layout:
    def __init__(self, groups, blocks, npair):
        self.groups, self.blocks, self.npair = groups, blocks, npair
        count = groups * blocks
        self.mine, self.own, self.choice = 1, 2, 3
        self.off = HEAD
        self.first = self.off + count
        self.owner = self.first + count
        self.into = self.owner + count
        self.pair = self.into + count
        self.rank = self.pair + count
        self.pair_into = self.rank + count
        self.pair_rank = self.pair_into + npair
        self.size = self.pair_rank + npair


def plan_kernel(lay, ids, ranks, where_ref, plan):
    groups, blocks, npair = lay.groups, lay.blocks, lay.npair
    per = npair // groups
    me = where_ref[0]
    for k in range(3):
        plan[k] = where_ref[k]

    def clear(p, carry):
        plan[lay.pair_rank + p] = 0
        return carry

    lax.fori_loop(0, npair, clear, 0)

    def group(g, widest):
        total = jnp.int32(0)
        pairs = [ids[(g ^ me) * blocks + b] for b in range(blocks)]
        places = []
        for b in range(blocks):
            i = g * blocks + b
            pair = pairs[b]
            rank = ranks[pair]
            plan[lay.pair_rank + pair] = rank
            place, new = total, rank
            for a in range(b):
                same = pairs[a] == pair
                place = jnp.where(same, places[a], place)
                new = jnp.where(same, 0, new)
            places.append(place)
            plan[lay.off + i] = place
            plan[lay.first + i] = new
            plan[lay.pair + i] = pair
            plan[lay.rank + i] = rank
            total = total + new
        return jnp.maximum(widest, total)

    widest = lax.fori_loop(0, groups, group, jnp.int32(0))

    def owner(o, fullest):
        total = jnp.int32(0)
        for k in range(per):
            p = o * per + k
            plan[lay.pair_into + p] = total
            total = total + plan[lay.pair_rank + p]
        return jnp.maximum(fullest, total)

    fullest = lax.fori_loop(0, groups, owner, jnp.int32(0))

    def block(i, carry):
        pair = plan[lay.pair + i]
        plan[lay.owner + i] = lax.div(pair, jnp.int32(per))
        plan[lay.into + i] = plan[lay.pair_into + pair]
        return carry

    lax.fori_loop(0, groups * blocks, block, 0)
    choice = jnp.int32(len(BUCKETS) - 1)
    for k in reversed(range(len(BUCKETS) - 1)):
        fits = jnp.logical_and(widest <= BUCKETS[k][0], fullest <= BUCKETS[k][1])
        choice = jnp.where(fits, k, choice)
    plan[lay.choice] = choice


def make_plan(lay, ids, ranks, where):
    smem = pl.BlockSpec(memory_space=pltpu.SMEM)
    return pl.pallas_call(
        functools.partial(plan_kernel, lay),
        out_shape=jax.ShapeDtypeStruct((lay.size,), jnp.int32),
        in_specs=[smem] * 3,
        out_specs=smem,
    )(ids, ranks, where)


def rank_kernel(half, where_ref, ids, cot, up, x, down, kept, sent):
    step = pl.program_id(0)
    rmax = up.shape[1]
    back = lax.dot_general(cot[...], up[0], NT, preferred_element_type=jnp.float32).astype(kept.dtype)
    low = jnp.dot(x[...], down[0], preferred_element_type=jnp.float32).astype(kept.dtype)

    @pl.when(step < half)
    def _():
        kept[:, :rmax] = back
        kept[:, rmax:] = low

    @pl.when(step >= half)
    def _():
        sent[:, :rmax] = back
        sent[:, rmax:] = low


def rank_sums(where, ids, cotangent, adapter_up, tokens, adapter_down):
    rows, width = cotangent.shape
    features = tokens.shape[1]
    blocks, rmax = ids.shape[0], adapter_up.shape[1]
    length, half = rows // blocks, blocks // 2
    out = jax.ShapeDtypeStruct((rows // 2, 2 * rmax), jnp.bfloat16)
    rows_of = lambda i, w, s: (i ^ w[2], 0)
    pair_of = lambda i, w, s: (s[i ^ w[2]], 0, 0)
    return call(
        functools.partial(rank_kernel, half),
        [out, out],
        (blocks,),
        [
            pl.BlockSpec((length, width), rows_of),
            pl.BlockSpec((1, rmax, width), pair_of),
            pl.BlockSpec((length, features), rows_of),
            pl.BlockSpec((1, features, rmax), pair_of),
        ],
        [
            pl.BlockSpec((length, 2 * rmax), lambda i, w, s: (jnp.minimum(i, half - 1), 0)),
            pl.BlockSpec((length, 2 * rmax), lambda i, w, s: (jnp.maximum(i - half, 0), 0)),
        ],
        flops=2 * rows * (width + features) * rmax,
        moved=2 * rows * (width + features + 2 * rmax),
        prefetch=2,
    )(where, ids, cotangent, adapter_up, tokens, adapter_down)


def add(a, b):
    return (a.astype(jnp.float32) + b.astype(jnp.float32)).astype(a.dtype)


def turn(rank, value):
    shape = (value.shape[1], value.shape[1])
    eye = jnp.logical_and(iota(shape, 0) == iota(shape, 1), iota(shape, 0) < rank).astype(jnp.bfloat16)
    return lax.dot_general(eye, value, NT, preferred_element_type=jnp.float32).astype(jnp.bfloat16)


def terms_kernel(lay, norm, width, plan, x, cot, own_sums, other_sums, out, total, turned, moved):
    groups, blocks = lay.groups, lay.blocks
    half = blocks // 2
    step = pl.program_id(0)
    length, rmax, slot = turned.shape[2], turned.shape[1], out.shape[1] - width
    part = out.shape[2]
    me, own = plan[0], plan[lay.own]

    def place(k):
        i = me * blocks + (k ^ own)
        factor = 32.0 / jnp.full((1, part), plan[lay.rank + i], jnp.int32).astype(jnp.float32) * norm
        return pl.ds(aligned(plan[lay.off + i]), rmax), factor

    @pl.when(step == 0)
    def _():
        total[...] = jnp.zeros_like(total)
        for k in range(blocks):
            b = k ^ own
            rank = plan[lay.rank + me * blocks + b]
            source = own_sums if k < half else other_sums
            lines = slice(k % half * length, (k % half + 1) * length)
            turned[k] = turn(rank, source[lines, :rmax])
            low = turn(rank, source[lines, rmax:])
            rows, factor = place(k)
            block = cot[pl.ds(aligned(b * length, length), length), :]
            total[rows, :] += factor * jnp.dot(low, block, preferred_element_type=jnp.float32)
        column = iota((groups * slot, width), 1)
        target = (column % groups) * slot + column // groups
        pick = (iota((groups * slot, width), 0) == target).astype(jnp.bfloat16)
        up = total[:width, :].astype(jnp.bfloat16)
        moved[...] = jnp.dot(pick, up, preferred_element_type=jnp.float32).astype(jnp.bfloat16)

    total[...] = jnp.zeros_like(total)
    for k in range(blocks):
        rows, factor = place(k)
        block = x[pl.ds(aligned((k ^ own) * length, length), length), :]
        total[rows, :] += factor * jnp.dot(turned[k], block, preferred_element_type=jnp.float32)
    out[0, :width, :] = total[:width, :].astype(jnp.bfloat16)
    out[0, width:, :] = moved[pl.ds(aligned(step * slot), slot), :]


def group_terms(lay, norm, width, plan, tokens, cotangent, sums):
    rows, features = tokens.shape
    part = cotangent.shape[1]
    rmax = sums[0].shape[1] // 2
    slot = share(width, lay.groups)
    shape = (lay.groups, width + slot, part)
    return call(
        functools.partial(terms_kernel, lay, norm, width),
        jax.ShapeDtypeStruct(shape, jnp.bfloat16),
        (lay.groups,),
        [pl.BlockSpec((rows, part), lambda i, plan: (0, i)), whole(cotangent.shape)] + [whole(v.shape) for v in sums],
        pl.BlockSpec((1,) + shape[1:], lambda i, plan: (i, 0, 0)),
        [
            pltpu.VMEM((width + rmax, part), jnp.float32),
            pltpu.VMEM((lay.blocks, rmax, rows // lay.blocks), jnp.bfloat16),
            pltpu.VMEM((lay.groups * slot, part), jnp.bfloat16),
        ],
        flops=2 * rows * (features + part) * rmax,
        moved=2 * features * (rows + width),
    )(plan, tokens, cotangent, *sums)


def grad_kernel(lay, tiles, parts, plan, *refs):
    cots, (weight, down, backs, backo, out, cat) = refs[:parts], refs[parts:]
    step = pl.program_id(0)
    half = lay.blocks * tiles // 2
    block = lax.div(step, jnp.int32(tiles)) ^ plan[lay.own]
    mine = plan[lay.mine]
    width = cots[0].shape[1]
    for s, cot in enumerate(cots):
        cat[:, pl.ds(aligned((mine ^ s) * width, width), width)] = cot[...]
    rank = plan[lay.rank + plan[0] * lay.blocks + block]
    back = jnp.where(step < half, backs[...], backo[...])
    rows = jnp.where(iota(back.shape, 1) < rank, back, jnp.zeros_like(back))
    chunk = 512
    scale = 32.0 / jnp.full((1, chunk), rank, jnp.int32).astype(jnp.float32)
    for c in range(0, out.shape[1], chunk):
        base = lax.dot_general(cat[...], weight[c : c + chunk, :], NT, preferred_element_type=jnp.float32)
        extra = lax.dot_general(rows, down[0, c : c + chunk, :], NT, preferred_element_type=jnp.float32)
        out[:, c : c + chunk] = (base + scale * extra).astype(out.dtype)


def input_gradient(lay, plan, cots, weight, adapter_down, sums):
    rows, width = cots[0].shape
    features, values = weight.shape
    blocks = lay.blocks
    tile = rows // blocks // 2
    tiles = 2
    half = blocks * tiles // 2
    rmax = sums[0].shape[1] // 2
    here = lambda i, plan: (i ^ (plan[lay.own] * tiles), 0)

    def adapter(i, plan):
        block = lax.div(i, jnp.int32(tiles)) ^ plan[lay.own]
        return (plan[lay.pair + plan[0] * blocks + block], 0, 0)

    return call(
        functools.partial(grad_kernel, lay, tiles, len(cots)),
        jax.ShapeDtypeStruct((rows, features), jnp.bfloat16),
        (rows // tile,),
        [pl.BlockSpec((tile, width), here)] * len(cots)
        + [
            whole(weight.shape),
            pl.BlockSpec((1, features, rmax), adapter),
            pl.BlockSpec((tile, rmax), lambda i, plan: (jnp.minimum(i, half - 1), 0)),
            pl.BlockSpec((tile, rmax), lambda i, plan: (jnp.maximum(i - half, 0), 0)),
        ],
        pl.BlockSpec((tile, features), here),
        [pltpu.VMEM((tile, values), jnp.bfloat16)],
        flops=2 * rows * features * (values + rmax),
        moved=2 * features * (rows + values),
    )(plan, *cots, weight, adapter_down, *sums)


def reduce_kernel(lay, width, cap, plan, parts, out, total, cat):
    groups, blocks = lay.groups, lay.blocks
    slot, small = parts.shape[1] - width, out.shape[1] - cap
    total[...] = jnp.zeros_like(total)
    place = iota((1, groups * slot), 1)
    target = jnp.full((1, groups * slot), -1, jnp.int32)
    for g in range(groups):
        cat[g * slot : (g + 1) * slot, :] = parts[g, width:, :]
        for b in range(blocks):
            i = g * blocks + b
            rank, source = plan[lay.first + i], plan[lay.off + i]
            owner, into = plan[lay.owner + i], plan[lay.into + i]
            goal = owner * cap + into
            for size in SIZES:

                @pl.when(rank == size)
                def _(g=g, source=source, goal=goal, size=size):
                    here = pl.ds(aligned(source), size)
                    total[pl.ds(aligned(goal), size), :] += parts[g, here, :].astype(jnp.float32)

            start = g * slot + lax.div(source, jnp.int32(groups))
            inside = jnp.logical_and(place >= start, place < start + lax.div(rank, jnp.int32(groups)))
            shift = owner * small + lax.div(into, jnp.int32(groups)) - start
            target = jnp.where(inside, place + shift, target)
    for o in range(groups):
        out[o, :cap, :] = total[o * cap : (o + 1) * cap, :].astype(out.dtype)
    pick = (iota((groups * small, groups * slot), 0) == target).astype(jnp.bfloat16)
    sums = jnp.dot(pick, cat[...], preferred_element_type=jnp.float32).astype(out.dtype)
    for o in range(groups):
        out[o, cap:, :] = sums[o * small : (o + 1) * small, :]


def reduce_terms(lay, width, cap, plan, parts):
    part = parts.shape[2]
    slot, small = share(width, lay.groups), share(cap, lay.groups)
    return call(
        functools.partial(reduce_kernel, lay, width, cap),
        jax.ShapeDtypeStruct((lay.groups, cap + small, part), jnp.bfloat16),
        (1,),
        [whole(parts.shape)],
        whole((lay.groups, cap + small, part)),
        [pltpu.VMEM((lay.groups * cap, part), jnp.float32), pltpu.VMEM((lay.groups * slot, part), jnp.bfloat16)],
        flops=2 * cap * width * part,
        moved=4 * lay.groups * cap * part,
    )(plan, parts)


def unpack_kernel(lay, cap, plan, slots, down, up, cat):
    groups = lay.groups
    per = lay.npair // groups
    me = plan[0]
    part, rmax, small = slots.shape[2], down.shape[2], slots.shape[1] - cap
    eye = (iota((part, part), 0) == iota((part, part), 1)).astype(jnp.bfloat16)
    held = [(plan[lay.pair_into + me * per + k], plan[lay.pair_rank + me * per + k]) for k in range(per)]
    r, row = iota((cap, rmax), 1), iota((cap, rmax), 0)
    picks = [jnp.logical_and(row == r + start, r < rank).astype(jnp.bfloat16) for start, rank in held]
    pick = jnp.concatenate(picks, axis=1)
    for s in range(groups):
        cat[s * small : (s + 1) * small, :] = slots[s, cap:, :]
        here = slice(s * part, (s + 1) * part)
        turned = lax.dot_general(eye, slots[s, :cap, :], NT, preferred_element_type=jnp.float32).astype(jnp.bfloat16)
        value = jnp.dot(turned, pick, preferred_element_type=jnp.float32).astype(down.dtype)
        for k in range(per):
            down[k, here, :] = value[:, k * rmax : (k + 1) * rmax]
    shape = (rmax, groups * small)
    r, column = iota(shape, 0), iota(shape, 1)
    place = (r % groups) * small + r // groups
    for k, (start, rank) in enumerate(held):
        match = column == place + lax.div(start, jnp.int32(groups))
        pick = jnp.logical_and(match, r < rank).astype(jnp.bfloat16)
        up[k] = jnp.dot(pick, cat[...], preferred_element_type=jnp.float32).astype(up.dtype)


def unpack(lay, cap, plan, slots, features, rmax):
    part = slots.shape[2]
    per = lay.npair // lay.groups
    shapes = [(per, features, rmax), (per, rmax, part)]
    return call(
        functools.partial(unpack_kernel, lay, cap),
        [jax.ShapeDtypeStruct(shape, jnp.bfloat16) for shape in shapes],
        (1,),
        [whole(slots.shape)],
        [whole(shape) for shape in shapes],
        [pltpu.VMEM((lay.groups * share(cap, lay.groups), part), jnp.bfloat16)],
        flops=2 * per * features * rmax * part,
        moved=2 * per * features * rmax,
    )(plan, slots)


def gather_parts(x, axis, after_far):
    size = lax.axis_size(axis)
    parts = {0: x}
    bit = size // 2
    while bit > 1:
        for k in sorted(parts):
            parts[k ^ bit] = swap(parts[k], axis, bit)
        bit //= 2
    near = swap(x, axis, 1)
    held, far = after_far([parts[k] for k in sorted(parts) if k] + [near])
    near, far = far[-1], far[:-1]
    out = {0: x, 1: near}
    for k, part in zip([k for k in sorted(parts) if k], far):
        out[k] = part
        out[k ^ 1] = swap(part, axis, 1)
    return held, [out[k] for k in range(size)]


def spread(parts):
    return lax.all_to_all(parts, "pair", split_axis=0, concat_axis=0, tiled=True)


def finish(lay, norm, bucket, plan, tokens, cotangent, weight, adapter_down, sums):
    width, cap = bucket
    parts = group_terms(lay, norm, width, plan, tokens, cotangent, sums)
    received = spread(parts)
    cots = gather_parts(cotangent, "fsdp", lambda far: lax.optimization_barrier((received, far)))
    received, cots = cots
    terms = reduce_terms(lay, width, cap, plan, received)
    _, cots = lax.optimization_barrier((terms, cots))
    input_grad = input_gradient(lay, plan, cots, weight, adapter_down, sums)
    slots, input_grad = lax.optimization_barrier((spread(terms), input_grad))
    down_grad, up_grad = unpack(lay, cap, plan, slots, tokens.shape[1], adapter_down.shape[2])
    return input_grad, down_grad, up_grad


def per_device(tokens, cotangent, value_weight, adapter_down, adapter_up, pair_ids, ranks):
    rows = tokens.shape[0]
    blocks = pair_ids.shape[0]
    groups, shares = lax.axis_size("pair"), lax.axis_size("fsdp")
    lay = Layout(groups, blocks, adapter_down.shape[0])
    norm = 1.0 / math.sqrt(rows * groups)
    me, mine = lax.axis_index("pair"), lax.axis_index("fsdp")
    where = jnp.stack([me, mine, (mine & 1) * (blocks // 2)]).astype(jnp.int32)
    ids = jnp.concatenate([pair_ids, swap(pair_ids, "pair", 1)])
    kept, sent = rank_sums(where, pair_ids, cotangent, adapter_up, tokens, adapter_down)
    ids, sent = lax.optimization_barrier((ids, sent))
    sums = add(kept, swap(sent, "fsdp", 1))
    if groups > 2:
        ids = jnp.concatenate([ids, swap(ids, "pair", 2)])
    sums, ids = lax.optimization_barrier((sums, ids))
    bit = 4
    while bit < groups:
        ids = jnp.concatenate([ids, swap(ids, "pair", bit)])
        bit *= 2
    plan = make_plan(lay, ids, ranks, where)
    bit = 2
    while bit < shares:
        theirs = swap(sums, "fsdp", bit)
        theirs, plan = lax.optimization_barrier((theirs, plan))
        sums = add(sums, theirs)
        bit *= 2
    sums = (sums, swap(sums, "fsdp", 1))
    branches = [functools.partial(finish, lay, norm, bucket) for bucket in BUCKETS]
    return lax.switch(plan[lay.choice], branches, plan, tokens, cotangent, value_weight, adapter_down, sums)


def dense_per_device(tokens, cotangent, value_weight, adapter_down, adapter_up, pair_ids, ranks):
    rows, features = tokens.shape
    blocks = pair_ids.shape[0]
    length = rows // blocks
    npair, _, rmax = adapter_down.shape
    norm = 1.0 / math.sqrt(rows * lax.axis_size("pair"))
    mask = (jnp.arange(rmax, dtype=jnp.int32)[None, :] < ranks[:, None]).astype(jnp.float32)
    scale = 32.0 / ranks.astype(jnp.float32)
    x = tokens.reshape(blocks, length, features)
    c = cotangent.reshape(blocks, length, cotangent.shape[1])
    down, up = adapter_down[pair_ids], adapter_up[pair_ids]
    wide = {"preferred_element_type": jnp.float32}
    low = lax.psum(jnp.einsum("btd,bdr->btr", x, down, **wide).astype(jnp.bfloat16), "fsdp")
    back = lax.psum(jnp.einsum("btk,brk->btr", c, up, **wide).astype(jnp.bfloat16), "fsdp")
    rows_mask = mask[pair_ids][:, None, :]
    low = (low.astype(jnp.float32) * rows_mask).astype(jnp.bfloat16)
    back = (back.astype(jnp.float32) * rows_mask).astype(jnp.bfloat16)
    cots = lax.all_gather(cotangent, "fsdp", axis=1, tiled=True)
    base = jnp.einsum("tk,dk->td", cots, value_weight, **wide).reshape(blocks, length, features)
    factor = scale[pair_ids][:, None, None]
    input_grad = (base + factor * jnp.einsum("btr,bdr->btd", back, down, **wide)).astype(jnp.bfloat16)
    term_a = jnp.einsum("btd,btr->bdr", x, back, **wide) * (factor * norm)
    term_b = jnp.einsum("btr,btk->brk", low, c, **wide) * (factor * norm)
    onehot = (pair_ids[:, None] == jnp.arange(npair, dtype=jnp.int32)[None, :]).astype(jnp.float32)
    grads = [
        lax.psum_scatter(
            jnp.einsum("bp,bij->pij", onehot, term).astype(jnp.bfloat16), "pair", scatter_dimension=0, tiled=True
        )
        for term in (term_a, term_b)
    ]
    return input_grad.reshape(rows, features), grads[0], grads[1]


def per_shape(tokens, cotangent, value_weight, adapter_down, adapter_up, pair_ids, ranks):
    groups, shares = lax.axis_size("pair"), lax.axis_size("fsdp")
    blocks = pair_ids.shape[0]
    part = tokens.shape[1] // groups
    power = lambda v: v & (v - 1) == 0
    fits = (
        part % 128 == 0
        and part == cotangent.shape[1]
        and power(groups)
        and power(shares)
        and power(blocks)
        and min(shares, blocks) > 1
        and groups <= 8
        and BUCKETS[-1][0] >= blocks * adapter_down.shape[2]
        and BUCKETS[-1][1] >= adapter_down.shape[0] // groups * adapter_down.shape[2]
    )
    form = per_device if fits else dense_per_device
    return form(tokens, cotangent, value_weight, adapter_down, adapter_up, pair_ids, ranks)


def solution(mesh):
    placed = (
        P("pair", "fsdp"),
        P("pair", "fsdp"),
        P("fsdp", None),
        P(None, "fsdp", None),
        P(None, None, "fsdp"),
        P("pair"),
        P(),
    )
    return jax.shard_map(
        per_shape,
        mesh=mesh,
        in_specs=placed,
        out_specs=(P("pair", "fsdp"), P("pair", "fsdp", None), P("pair", None, "fsdp")),
        check_vma=False,
    )
```

```python
import functools
import math

import jax
import jax.numpy as jnp
from jax import lax
from jax.experimental import pallas as pl
from jax.experimental.pallas import tpu as pltpu
from jax.sharding import PartitionSpec as P

WIDTHS = (224, 256, 288, 320, 352, 384, 416, 448, 512)
CAPS = (160, 192, 224, 256, 288, 320, 352, 384, 448, 768)
ALIGN = 16
HEAD = 16
NT = (((1,), (1,)), ((), ()))
VMEM = 56 * 1024 * 1024
SIZES = (128, 64, 32, 16)


def call(kernel, out_shape, grid, in_specs, out_specs, scratch=(), flops=0, moved=0, prefetch=1):
    return pl.pallas_call(
        kernel,
        out_shape=out_shape,
        grid_spec=pltpu.PrefetchScalarGridSpec(
            num_scalar_prefetch=prefetch,
            grid=grid,
            in_specs=in_specs,
            out_specs=out_specs,
            scratch_shapes=list(scratch),
        ),
        compiler_params=pltpu.CompilerParams(vmem_limit_bytes=VMEM),
        cost_estimate=pl.CostEstimate(flops=flops, bytes_accessed=moved, transcendentals=0),
    )


def whole(shape):
    return pl.BlockSpec(shape, lambda i, *s: (0,) * len(shape))


def iota(shape, axis):
    return lax.broadcasted_iota(jnp.int32, shape, axis)


def aligned(index, unit=ALIGN):
    return pl.multiple_of(index, unit)


def swap(x, axis, bit):
    size = lax.axis_size(axis)
    return lax.ppermute(x, axis, [(i, i ^ bit) for i in range(size)])


def share(columns, groups):
    return -(-columns // (groups * ALIGN)) * ALIGN


class Layout:
    def __init__(self, groups, blocks, npair):
        self.groups, self.blocks, self.npair = groups, blocks, npair
        count = groups * blocks
        self.mine, self.own = 1, 2
        self.width_at, self.width, self.slot, self.cap_at, self.cap, self.small = 3, 4, 5, 6, 7, 8
        self.off = HEAD
        self.first = self.off + count
        self.owner = self.first + count
        self.into = self.owner + count
        self.pair = self.into + count
        self.rank = self.pair + count
        self.pair_into = self.rank + count
        self.pair_rank = self.pair_into + npair
        self.size = self.pair_rank + npair


def plan_kernel(lay, ids, ranks, where_ref, plan):
    groups, blocks, npair = lay.groups, lay.blocks, lay.npair
    per = npair // groups
    me = where_ref[0]
    for k in range(3):
        plan[k] = where_ref[k]

    def clear(p, carry):
        plan[lay.pair_rank + p] = 0
        return carry

    lax.fori_loop(0, npair, clear, 0)

    def group(g, widest):
        total = jnp.int32(0)
        pairs = [ids[(g ^ me) * blocks + b] for b in range(blocks)]
        places = []
        for b in range(blocks):
            i = g * blocks + b
            pair = pairs[b]
            rank = ranks[pair]
            plan[lay.pair_rank + pair] = rank
            place, new = total, rank
            for a in range(b):
                same = pairs[a] == pair
                place = jnp.where(same, places[a], place)
                new = jnp.where(same, 0, new)
            places.append(place)
            plan[lay.off + i] = place
            plan[lay.first + i] = new
            plan[lay.pair + i] = pair
            plan[lay.rank + i] = rank
            total = total + new
        return jnp.maximum(widest, total)

    widest = lax.fori_loop(0, groups, group, jnp.int32(0))

    def owner(o, fullest):
        total = jnp.int32(0)
        for k in range(per):
            p = o * per + k
            plan[lay.pair_into + p] = total
            total = total + plan[lay.pair_rank + p]
        return jnp.maximum(fullest, total)

    fullest = lax.fori_loop(0, groups, owner, jnp.int32(0))

    def block(i, carry):
        pair = plan[lay.pair + i]
        plan[lay.owner + i] = lax.div(pair, jnp.int32(per))
        plan[lay.into + i] = plan[lay.pair_into + pair]
        return carry

    lax.fori_loop(0, groups * blocks, block, 0)
    for need, sizes, at in ((widest, WIDTHS, lay.width_at), (fullest, CAPS, lay.cap_at)):
        values = [(k, size, share(size, groups)) for k, size in enumerate(sizes)]
        chosen = [jnp.int32(v) for v in values[-1]]
        for k, size, rows in reversed(values[:-1]):
            fits = need <= size
            chosen = [jnp.where(fits, v, c) for v, c in zip((k, size, rows), chosen)]
        for k in range(3):
            plan[at + k] = chosen[k]


def make_plan(lay, ids, ranks, where):
    smem = pl.BlockSpec(memory_space=pltpu.SMEM)
    return pl.pallas_call(
        functools.partial(plan_kernel, lay),
        out_shape=jax.ShapeDtypeStruct((lay.size,), jnp.int32),
        in_specs=[smem] * 3,
        out_specs=smem,
    )(ids, ranks, where)


def rank_kernel(half, where_ref, ids, cot, up, x, down, kept, sent):
    step = pl.program_id(0)
    rmax = up.shape[1]
    back = lax.dot_general(cot[...], up[0], NT, preferred_element_type=jnp.float32).astype(kept.dtype)
    low = jnp.dot(x[...], down[0], preferred_element_type=jnp.float32).astype(kept.dtype)

    @pl.when(step < half)
    def _():
        kept[:, :rmax] = back
        kept[:, rmax:] = low

    @pl.when(step >= half)
    def _():
        sent[:, :rmax] = back
        sent[:, rmax:] = low


def rank_sums(where, ids, cotangent, adapter_up, tokens, adapter_down):
    rows, width = cotangent.shape
    features = tokens.shape[1]
    blocks, rmax = ids.shape[0], adapter_up.shape[1]
    length, half = rows // blocks, blocks // 2
    out = jax.ShapeDtypeStruct((rows // 2, 2 * rmax), jnp.bfloat16)
    rows_of = lambda i, w, s: (i ^ w[2], 0)
    pair_of = lambda i, w, s: (s[i ^ w[2]], 0, 0)
    return call(
        functools.partial(rank_kernel, half),
        [out, out],
        (blocks,),
        [
            pl.BlockSpec((length, width), rows_of),
            pl.BlockSpec((1, rmax, width), pair_of),
            pl.BlockSpec((length, features), rows_of),
            pl.BlockSpec((1, features, rmax), pair_of),
        ],
        [
            pl.BlockSpec((length, 2 * rmax), lambda i, w, s: (jnp.minimum(i, half - 1), 0)),
            pl.BlockSpec((length, 2 * rmax), lambda i, w, s: (jnp.maximum(i - half, 0), 0)),
        ],
        flops=2 * rows * (width + features) * rmax,
        moved=2 * rows * (width + features + 2 * rmax),
        prefetch=2,
    )(where, ids, cotangent, adapter_up, tokens, adapter_down)


def add(a, b):
    return (a.astype(jnp.float32) + b.astype(jnp.float32)).astype(a.dtype)


def turn(rank, value):
    shape = (value.shape[1], value.shape[1])
    eye = jnp.logical_and(iota(shape, 0) == iota(shape, 1), iota(shape, 0) < rank).astype(jnp.bfloat16)
    return lax.dot_general(eye, value, NT, preferred_element_type=jnp.float32).astype(jnp.bfloat16)


def terms_kernel(lay, norm, plan, x, cot, own_sums, other_sums, out, total, turned, moved):
    groups, blocks = lay.groups, lay.blocks
    half = blocks // 2
    step = pl.program_id(0)
    length, rmax, part = turned.shape[2], turned.shape[1], out.shape[2]
    most, room = WIDTHS[-1], share(WIDTHS[-1], groups)
    pieces = out.shape[0]
    me, own = plan[0], plan[lay.own]
    width, slot = plan[lay.width], plan[lay.slot]

    def place(k, columns):
        i = me * blocks + (k ^ own)
        factor = 32.0 / jnp.full((1, columns), plan[lay.rank + i], jnp.int32).astype(jnp.float32) * norm
        return pl.ds(aligned(plan[lay.off + i]), rmax), factor

    @pl.when(step == 0)
    def _():
        total[:, :part] = jnp.zeros((total.shape[0], part), total.dtype)
        for k in range(blocks):
            b = k ^ own
            rank = plan[lay.rank + me * blocks + b]
            source = own_sums if k < half else other_sums
            lines = slice(k % half * length, (k % half + 1) * length)
            turned[k] = turn(rank, source[lines, :rmax])
            low = turn(rank, source[lines, rmax:])
            rows, factor = place(k, part)
            block = cot[pl.ds(aligned(b * length, length), length), :]
            total[rows, :part] += factor * jnp.dot(low, block, preferred_element_type=jnp.float32)
        column = iota((groups * room, most), 1)
        target = (column % groups) * slot + column // groups
        pick = (iota((groups * room, most), 0) == target).astype(jnp.bfloat16)
        up = total[:most, :part].astype(jnp.bfloat16)
        moved[...] = jnp.dot(pick, up, preferred_element_type=jnp.float32).astype(jnp.bfloat16)

    total[...] = jnp.zeros_like(total)
    for k in range(blocks):
        rows, factor = place(k, pieces * part)
        block = x[pl.ds(aligned((k ^ own) * length, length), length), :]
        total[rows, :] += factor * jnp.dot(turned[k], block, preferred_element_type=jnp.float32)
    for p in range(pieces):
        out[p, :most, :] = total[:most, p * part : (p + 1) * part].astype(jnp.bfloat16)
        out[p, pl.ds(aligned(width), room), :] = moved[pl.ds(aligned((step * pieces + p) * slot), room), :]


def group_terms(lay, norm, plan, tokens, cotangent, sums):
    rows, features = tokens.shape
    part = cotangent.shape[1]
    rmax = sums[0].shape[1] // 2
    most, room = WIDTHS[-1], share(WIDTHS[-1], lay.groups)
    pieces = 2
    shape = (lay.groups, most + room, part)
    return call(
        functools.partial(terms_kernel, lay, norm),
        jax.ShapeDtypeStruct(shape, jnp.bfloat16),
        (lay.groups // pieces,),
        [pl.BlockSpec((rows, pieces * part), lambda i, plan: (0, i)), whole(cotangent.shape)]
        + [whole(v.shape) for v in sums],
        pl.BlockSpec((pieces,) + shape[1:], lambda i, plan: (i, 0, 0)),
        [
            pltpu.VMEM((most + rmax, pieces * part), jnp.float32),
            pltpu.VMEM((lay.blocks, rmax, rows // lay.blocks), jnp.bfloat16),
            pltpu.VMEM((lay.groups * room, part), jnp.bfloat16),
        ],
        flops=2 * rows * (features + part) * rmax,
        moved=2 * features * (rows + most),
    )(plan, tokens, cotangent, *sums)


def grad_kernel(lay, tiles, parts, plan, *refs):
    cots, (weight, down, backs, backo, out, cat) = refs[:parts], refs[parts:]
    step = pl.program_id(0)
    half = lay.blocks * tiles // 2
    block = lax.div(step, jnp.int32(tiles)) ^ plan[lay.own]
    mine = plan[lay.mine]
    width = cots[0].shape[1]
    for s, cot in enumerate(cots):
        cat[:, pl.ds(aligned((mine ^ s) * width, width), width)] = cot[...]
    rank = plan[lay.rank + plan[0] * lay.blocks + block]
    back = jnp.where(step < half, backs[...], backo[...])
    rows = jnp.where(iota(back.shape, 1) < rank, back, jnp.zeros_like(back))
    chunk = 512
    scale = 32.0 / jnp.full((1, chunk), rank, jnp.int32).astype(jnp.float32)

    def columns(c, carry):
        here = pl.ds(aligned(c * chunk, chunk), chunk)
        base = lax.dot_general(cat[...], weight[here, :], NT, preferred_element_type=jnp.float32)
        extra = lax.dot_general(rows, down[0, here, :], NT, preferred_element_type=jnp.float32)
        out[:, here] = (base + scale * extra).astype(out.dtype)
        return carry

    lax.fori_loop(0, out.shape[1] // chunk, columns, 0)


def input_gradient(lay, plan, cots, weight, adapter_down, sums):
    rows, width = cots[0].shape
    features, values = weight.shape
    blocks = lay.blocks
    tile = rows // blocks
    tiles = 1
    half = blocks * tiles // 2
    rmax = sums[0].shape[1] // 2
    here = lambda i, plan: (i ^ (plan[lay.own] * tiles), 0)

    def adapter(i, plan):
        block = lax.div(i, jnp.int32(tiles)) ^ plan[lay.own]
        return (plan[lay.pair + plan[0] * blocks + block], 0, 0)

    return call(
        functools.partial(grad_kernel, lay, tiles, len(cots)),
        jax.ShapeDtypeStruct((rows, features), jnp.bfloat16),
        (rows // tile,),
        [pl.BlockSpec((tile, width), here)] * len(cots)
        + [
            whole(weight.shape),
            pl.BlockSpec((1, features, rmax), adapter),
            pl.BlockSpec((tile, rmax), lambda i, plan: (jnp.minimum(i, half - 1), 0)),
            pl.BlockSpec((tile, rmax), lambda i, plan: (jnp.maximum(i - half, 0), 0)),
        ],
        pl.BlockSpec((tile, features), here),
        [pltpu.VMEM((tile, values), jnp.bfloat16)],
        flops=2 * rows * features * (values + rmax),
        moved=2 * features * (rows + values),
    )(plan, *cots, weight, adapter_down, *sums)


def reduce_kernel(lay, plan, parts, out, total, cat):
    groups, blocks = lay.groups, lay.blocks
    room, space = share(WIDTHS[-1], groups), share(CAPS[-1], groups)
    width, cap, small = plan[lay.width], plan[lay.cap], plan[lay.small]
    chunk = 128

    def clear(c, carry):
        total[pl.ds(aligned(c * chunk, chunk), chunk), :] = jnp.zeros((chunk, total.shape[1]), total.dtype)
        return carry

    lax.fori_loop(0, lax.div(groups * cap + chunk - 1, jnp.int32(chunk)), clear, 0)
    place = iota((1, groups * room), 1)
    target = jnp.full((1, groups * room), -1, jnp.int32)
    for g in range(groups):
        cat[g * room : (g + 1) * room, :] = parts[g, pl.ds(aligned(width), room), :]
        for b in range(blocks):
            i = g * blocks + b
            rank, source = plan[lay.first + i], plan[lay.off + i]
            owner, into = plan[lay.owner + i], plan[lay.into + i]
            goal = owner * cap + into
            for size in SIZES:

                @pl.when(rank == size)
                def _(g=g, source=source, goal=goal, size=size):
                    here = pl.ds(aligned(source), size)
                    total[pl.ds(aligned(goal), size), :] += parts[g, here, :].astype(jnp.float32)

            start = g * room + lax.div(source, jnp.int32(groups))
            inside = jnp.logical_and(place >= start, place < start + lax.div(rank, jnp.int32(groups)))
            shift = owner * small + lax.div(into, jnp.int32(groups)) - start
            target = jnp.where(inside, place + shift, target)
    line = iota((space, groups * room), 0)

    def owner_rows(o, carry):
        def copy(c, carry):
            here = pl.ds(aligned(c * chunk, chunk), chunk)
            out[o, here, :] = total[pl.ds(aligned(o * cap + c * chunk), chunk), :].astype(out.dtype)
            return carry

        lax.fori_loop(0, lax.div(cap + chunk - 1, jnp.int32(chunk)), copy, 0)
        pick = (line + o * small == target).astype(jnp.bfloat16)
        rows = jnp.dot(pick, cat[...], preferred_element_type=jnp.float32).astype(out.dtype)
        out[o, pl.ds(aligned(cap), space), :] = rows
        return carry

    lax.fori_loop(0, groups, owner_rows, 0)


def reduce_terms(lay, rmax, plan, parts):
    part = parts.shape[2]
    groups, most = lay.groups, CAPS[-1]
    shape = (groups, most + rmax, part)
    return call(
        functools.partial(reduce_kernel, lay),
        jax.ShapeDtypeStruct(shape, jnp.bfloat16),
        (1,),
        [whole(parts.shape)],
        whole(shape),
        [
            pltpu.VMEM((groups * most + 128, part), jnp.float32),
            pltpu.VMEM((groups * share(WIDTHS[-1], groups), part), jnp.bfloat16),
        ],
        flops=2 * most * WIDTHS[-1] * part,
        moved=4 * groups * most * part,
    )(plan, parts)


def unpack_kernel(lay, plan, slots, down, up, cat):
    groups = lay.groups
    per = lay.npair // groups
    me, cap = plan[0], plan[lay.cap]
    part, rmax, space = slots.shape[2], down.shape[2], share(CAPS[-1], groups)
    eye = (iota((part, part), 0) == iota((part, part), 1)).astype(jnp.bfloat16)
    for s in range(groups):
        cat[s * space : (s + 1) * space, :] = slots[s, pl.ds(aligned(cap), space), :]
    shape = (rmax, groups * space)
    r, column = iota(shape, 0), iota(shape, 1)
    place = (r % groups) * space + r // groups
    for k in range(per):
        start, rank = plan[lay.pair_into + me * per + k], plan[lay.pair_rank + me * per + k]

        @pl.when(rank > 0)
        def _(k=k, start=start, rank=rank):
            for s in range(groups):
                rows = slots[s, pl.ds(aligned(start), rmax), :]
                rows = jnp.where(iota(rows.shape, 0) < rank, rows, jnp.zeros_like(rows))
                value = lax.dot_general(eye, rows, NT, preferred_element_type=jnp.float32)
                down[k, s * part : (s + 1) * part, :] = value.astype(down.dtype)
            match = column == place + lax.div(start, jnp.int32(groups))
            pick = jnp.logical_and(match, r < rank).astype(jnp.bfloat16)
            up[k] = jnp.dot(pick, cat[...], preferred_element_type=jnp.float32).astype(up.dtype)

        @pl.when(rank == 0)
        def _(k=k):
            down[k] = jnp.zeros_like(down[k])
            up[k] = jnp.zeros_like(up[k])


def unpack(lay, plan, slots, features, rmax):
    part = slots.shape[2]
    per = lay.npair // lay.groups
    shapes = [(per, features, rmax), (per, rmax, part)]
    return call(
        functools.partial(unpack_kernel, lay),
        [jax.ShapeDtypeStruct(shape, jnp.bfloat16) for shape in shapes],
        (1,),
        [whole(slots.shape)],
        [whole(shape) for shape in shapes],
        [pltpu.VMEM((lay.groups * share(CAPS[-1], lay.groups), part), jnp.bfloat16)],
        flops=2 * per * features * rmax * part,
        moved=2 * per * features * rmax,
    )(plan, slots)


def far_parts(x, axis):
    size = lax.axis_size(axis)
    parts = {0: x}
    bit = size // 2
    while bit > 1:
        for k in sorted(parts):
            parts[k ^ bit] = swap(parts[k], axis, bit)
        bit //= 2
    return [parts[k] for k in sorted(parts) if k], swap(x, axis, 1)


def all_parts(x, far, near, axis):
    out = [x, near]
    for part in far:
        out += [part, swap(part, axis, 1)]
    return out


def spread(rows, parts):
    sent = lax.all_to_all(parts[:, :rows, :], "pair", split_axis=0, concat_axis=0, tiled=True)
    return jnp.pad(sent, ((0, 0), (0, parts.shape[1] - rows), (0, 0)))


def first_exchange(rows, terms, cotangent):
    return spread(rows, terms), *far_parts(cotangent, "fsdp")


def second_exchange(lay, rows, plan, sums, cotangent, far, near, weight, adapter_down, ranked):
    cots = all_parts(cotangent, far, near, "fsdp")
    return spread(rows, sums), input_gradient(lay, plan, cots, weight, adapter_down, ranked)


def per_device(tokens, cotangent, value_weight, adapter_down, adapter_up, pair_ids, ranks):
    rows = tokens.shape[0]
    blocks = pair_ids.shape[0]
    groups, shares = lax.axis_size("pair"), lax.axis_size("fsdp")
    lay = Layout(groups, blocks, adapter_down.shape[0])
    norm = 1.0 / math.sqrt(rows * groups)
    me, mine = lax.axis_index("pair"), lax.axis_index("fsdp")
    where = jnp.stack([me, mine, (mine & 1) * (blocks // 2)]).astype(jnp.int32)
    ids = jnp.concatenate([pair_ids, swap(pair_ids, "pair", 1)])
    kept, sent = rank_sums(where, pair_ids, cotangent, adapter_up, tokens, adapter_down)
    ids, sent = lax.optimization_barrier((ids, sent))
    sums = add(kept, swap(sent, "fsdp", 1))
    if groups > 2:
        ids = jnp.concatenate([ids, swap(ids, "pair", 2)])
    sums, ids = lax.optimization_barrier((sums, ids))
    bit = 4
    while bit < groups:
        ids = jnp.concatenate([ids, swap(ids, "pair", bit)])
        bit *= 2
    plan = make_plan(lay, ids, ranks, where)
    bit = 2
    while bit < shares:
        theirs = swap(sums, "fsdp", bit)
        theirs, plan = lax.optimization_barrier((theirs, plan))
        sums = add(sums, theirs)
        bit *= 2
    sums = (sums, swap(sums, "fsdp", 1))
    terms = group_terms(lay, norm, plan, tokens, cotangent, sums)
    branches = [functools.partial(first_exchange, size + share(size, groups)) for size in WIDTHS]
    received, far, near = lax.switch(plan[lay.width_at], branches, terms, cotangent)
    reduced = reduce_terms(lay, adapter_down.shape[2], plan, received)
    branches = [functools.partial(second_exchange, lay, size + share(size, groups)) for size in CAPS]
    slots, input_grad = lax.switch(
        plan[lay.cap_at], branches, plan, reduced, cotangent, far, near, value_weight, adapter_down, sums
    )
    down_grad, up_grad = unpack(lay, plan, slots, tokens.shape[1], adapter_down.shape[2])
    return input_grad, down_grad, up_grad


def dense_per_device(tokens, cotangent, value_weight, adapter_down, adapter_up, pair_ids, ranks):
    rows, features = tokens.shape
    blocks = pair_ids.shape[0]
    length = rows // blocks
    npair, _, rmax = adapter_down.shape
    norm = 1.0 / math.sqrt(rows * lax.axis_size("pair"))
    mask = (jnp.arange(rmax, dtype=jnp.int32)[None, :] < ranks[:, None]).astype(jnp.float32)
    scale = 32.0 / ranks.astype(jnp.float32)
    x = tokens.reshape(blocks, length, features)
    c = cotangent.reshape(blocks, length, cotangent.shape[1])
    down, up = adapter_down[pair_ids], adapter_up[pair_ids]
    wide = {"preferred_element_type": jnp.float32}
    low = lax.psum(jnp.einsum("btd,bdr->btr", x, down, **wide).astype(jnp.bfloat16), "fsdp")
    back = lax.psum(jnp.einsum("btk,brk->btr", c, up, **wide).astype(jnp.bfloat16), "fsdp")
    rows_mask = mask[pair_ids][:, None, :]
    low = (low.astype(jnp.float32) * rows_mask).astype(jnp.bfloat16)
    back = (back.astype(jnp.float32) * rows_mask).astype(jnp.bfloat16)
    cots = lax.all_gather(cotangent, "fsdp", axis=1, tiled=True)
    base = jnp.einsum("tk,dk->td", cots, value_weight, **wide).reshape(blocks, length, features)
    factor = scale[pair_ids][:, None, None]
    input_grad = (base + factor * jnp.einsum("btr,bdr->btd", back, down, **wide)).astype(jnp.bfloat16)
    term_a = jnp.einsum("btd,btr->bdr", x, back, **wide) * (factor * norm)
    term_b = jnp.einsum("btr,btk->brk", low, c, **wide) * (factor * norm)
    onehot = (pair_ids[:, None] == jnp.arange(npair, dtype=jnp.int32)[None, :]).astype(jnp.float32)
    grads = [
        lax.psum_scatter(
            jnp.einsum("bp,bij->pij", onehot, term).astype(jnp.bfloat16), "pair", scatter_dimension=0, tiled=True
        )
        for term in (term_a, term_b)
    ]
    return input_grad.reshape(rows, features), grads[0], grads[1]


def per_shape(tokens, cotangent, value_weight, adapter_down, adapter_up, pair_ids, ranks):
    groups, shares = lax.axis_size("pair"), lax.axis_size("fsdp")
    blocks = pair_ids.shape[0]
    part = tokens.shape[1] // groups
    power = lambda v: v & (v - 1) == 0
    fits = (
        part % 128 == 0
        and part == cotangent.shape[1]
        and power(groups)
        and power(shares)
        and power(blocks)
        and min(shares, blocks) > 1
        and groups <= 8
        and WIDTHS[-1] >= blocks * adapter_down.shape[2]
        and CAPS[-1] >= adapter_down.shape[0] // groups * adapter_down.shape[2]
    )
    form = per_device if fits else dense_per_device
    return form(tokens, cotangent, value_weight, adapter_down, adapter_up, pair_ids, ranks)


def solution(mesh):
    placed = (
        P("pair", "fsdp"),
        P("pair", "fsdp"),
        P("fsdp", None),
        P(None, "fsdp", None),
        P(None, None, "fsdp"),
        P("pair"),
        P(),
    )
    return jax.shard_map(
        per_shape,
        mesh=mesh,
        in_specs=placed,
        out_specs=(P("pair", "fsdp"), P("pair", "fsdp", None), P("pair", None, "fsdp")),
        check_vma=False,
    )
```

```python
import functools
import math

import jax
import jax.numpy as jnp
from jax import lax
from jax.experimental import pallas as pl
from jax.experimental.pallas import tpu as pltpu
from jax.sharding import PartitionSpec as P

WIDTHS = (224, 256, 288, 320, 352, 384, 416, 448, 512)
CAPS = (160, 192, 224, 256, 288, 320, 352, 384, 448, 768)
ALIGN = 16
HEAD = 16
NT = (((1,), (1,)), ((), ()))
MIB = 1024 * 1024
SIZES = (128, 64, 32, 16)


def call(kernel, out_shape, grid, in_specs, out_specs, scratch=(), flops=0, moved=0, prefetch=1, room=24):
    return pl.pallas_call(
        kernel,
        out_shape=out_shape,
        grid_spec=pltpu.PrefetchScalarGridSpec(
            num_scalar_prefetch=prefetch,
            grid=grid,
            in_specs=in_specs,
            out_specs=out_specs,
            scratch_shapes=list(scratch),
        ),
        compiler_params=pltpu.CompilerParams(vmem_limit_bytes=room * MIB),
        cost_estimate=pl.CostEstimate(flops=flops, bytes_accessed=moved, transcendentals=0),
    )


def whole(shape):
    return pl.BlockSpec(shape, lambda i, *s: (0,) * len(shape))


def iota(shape, axis):
    return lax.broadcasted_iota(jnp.int32, shape, axis)


def aligned(index, unit=ALIGN):
    return pl.multiple_of(index, unit)


def swap(x, axis, bit):
    size = lax.axis_size(axis)
    return lax.ppermute(x, axis, [(i, i ^ bit) for i in range(size)])


def share(columns, groups):
    return -(-columns // (groups * ALIGN)) * ALIGN


class Layout:
    def __init__(self, groups, blocks, npair):
        self.groups, self.blocks, self.npair = groups, blocks, npair
        count = groups * blocks
        self.mine, self.own = 1, 2
        self.width_at, self.width, self.slot, self.cap_at, self.cap, self.small = 3, 4, 5, 6, 7, 8
        self.off = HEAD
        self.first = self.off + count
        self.owner = self.first + count
        self.into = self.owner + count
        self.pair = self.into + count
        self.rank = self.pair + count
        self.pair_into = self.rank + count
        self.pair_rank = self.pair_into + npair
        self.size = self.pair_rank + npair


def plan_kernel(lay, ids, ranks, where_ref, plan):
    groups, blocks, npair = lay.groups, lay.blocks, lay.npair
    per = npair // groups
    me = where_ref[0]
    for k in range(3):
        plan[k] = where_ref[k]

    def clear(p, carry):
        plan[lay.pair_rank + p] = 0
        return carry

    lax.fori_loop(0, npair, clear, 0)

    def group(g, widest):
        total = jnp.int32(0)
        pairs = [ids[(g ^ me) * blocks + b] for b in range(blocks)]
        places = []
        for b in range(blocks):
            i = g * blocks + b
            pair = pairs[b]
            rank = ranks[pair]
            plan[lay.pair_rank + pair] = rank
            place, new = total, rank
            for a in range(b):
                same = pairs[a] == pair
                place = jnp.where(same, places[a], place)
                new = jnp.where(same, 0, new)
            places.append(place)
            plan[lay.off + i] = place
            plan[lay.first + i] = new
            plan[lay.pair + i] = pair
            plan[lay.rank + i] = rank
            total = total + new
        return jnp.maximum(widest, total)

    widest = lax.fori_loop(0, groups, group, jnp.int32(0))

    def owner(o, fullest):
        total = jnp.int32(0)
        for k in range(per):
            p = o * per + k
            plan[lay.pair_into + p] = total
            total = total + plan[lay.pair_rank + p]
        return jnp.maximum(fullest, total)

    fullest = lax.fori_loop(0, groups, owner, jnp.int32(0))

    def block(i, carry):
        pair = plan[lay.pair + i]
        plan[lay.owner + i] = lax.div(pair, jnp.int32(per))
        plan[lay.into + i] = plan[lay.pair_into + pair]
        return carry

    lax.fori_loop(0, groups * blocks, block, 0)
    for need, sizes, at in ((widest, WIDTHS, lay.width_at), (fullest, CAPS, lay.cap_at)):
        values = [(k, size, share(size, groups)) for k, size in enumerate(sizes)]
        chosen = [jnp.int32(v) for v in values[-1]]
        for k, size, rows in reversed(values[:-1]):
            fits = need <= size
            chosen = [jnp.where(fits, v, c) for v, c in zip((k, size, rows), chosen)]
        for k in range(3):
            plan[at + k] = chosen[k]


def make_plan(lay, ids, ranks, where):
    smem = pl.BlockSpec(memory_space=pltpu.SMEM)
    return pl.pallas_call(
        functools.partial(plan_kernel, lay),
        out_shape=jax.ShapeDtypeStruct((lay.size,), jnp.int32),
        in_specs=[smem] * 3,
        out_specs=smem,
    )(ids, ranks, where)


def rank_kernel(half, where_ref, ids, cot, up, x, down, kept, sent):
    step = pl.program_id(0)
    rmax = up.shape[1]
    back = lax.dot_general(cot[...], up[0], NT, preferred_element_type=jnp.float32).astype(kept.dtype)
    low = jnp.dot(x[...], down[0], preferred_element_type=jnp.float32).astype(kept.dtype)

    @pl.when(step < half)
    def _():
        kept[:, :rmax] = back
        kept[:, rmax:] = low

    @pl.when(step >= half)
    def _():
        sent[:, :rmax] = back
        sent[:, rmax:] = low


def rank_sums(where, ids, cotangent, adapter_up, tokens, adapter_down):
    rows, width = cotangent.shape
    features = tokens.shape[1]
    blocks, rmax = ids.shape[0], adapter_up.shape[1]
    length, half = rows // blocks, blocks // 2
    out = jax.ShapeDtypeStruct((rows // 2, 2 * rmax), jnp.bfloat16)
    rows_of = lambda i, w, s: (i ^ w[2], 0)
    pair_of = lambda i, w, s: (s[i ^ w[2]], 0, 0)
    return call(
        functools.partial(rank_kernel, half),
        [out, out],
        (blocks,),
        [
            pl.BlockSpec((length, width), rows_of),
            pl.BlockSpec((1, rmax, width), pair_of),
            pl.BlockSpec((length, features), rows_of),
            pl.BlockSpec((1, features, rmax), pair_of),
        ],
        [
            pl.BlockSpec((length, 2 * rmax), lambda i, w, s: (jnp.minimum(i, half - 1), 0)),
            pl.BlockSpec((length, 2 * rmax), lambda i, w, s: (jnp.maximum(i - half, 0), 0)),
        ],
        flops=2 * rows * (width + features) * rmax,
        moved=2 * rows * (width + features + 2 * rmax),
        prefetch=2,
        room=56,
    )(where, ids, cotangent, adapter_up, tokens, adapter_down)


def add(a, b):
    return (a.astype(jnp.float32) + b.astype(jnp.float32)).astype(a.dtype)


def turn(rank, value):
    shape = (value.shape[1], value.shape[1])
    eye = jnp.logical_and(iota(shape, 0) == iota(shape, 1), iota(shape, 0) < rank).astype(jnp.bfloat16)
    return lax.dot_general(eye, value, NT, preferred_element_type=jnp.float32).astype(jnp.bfloat16)


def terms_kernel(lay, norm, plan, x, cot, own_sums, other_sums, out, total, turned, moved):
    groups, blocks = lay.groups, lay.blocks
    half = blocks // 2
    step = pl.program_id(0)
    length, rmax, part = turned.shape[2], turned.shape[1], out.shape[2]
    most, room = WIDTHS[-1], share(WIDTHS[-1], groups)
    pieces = out.shape[0]
    me, own = plan[0], plan[lay.own]
    width, slot = plan[lay.width], plan[lay.slot]

    def place(k, columns):
        i = me * blocks + (k ^ own)
        factor = 32.0 / jnp.full((1, columns), plan[lay.rank + i], jnp.int32).astype(jnp.float32) * norm
        return pl.ds(aligned(plan[lay.off + i]), rmax), factor

    @pl.when(step == 0)
    def _():
        total[:, :part] = jnp.zeros((total.shape[0], part), total.dtype)
        for k in range(blocks):
            b = k ^ own
            rank = plan[lay.rank + me * blocks + b]
            source = own_sums if k < half else other_sums
            lines = slice(k % half * length, (k % half + 1) * length)
            turned[k] = turn(rank, source[lines, :rmax])
            low = turn(rank, source[lines, rmax:])
            rows, factor = place(k, part)
            block = cot[pl.ds(aligned(b * length, length), length), :]
            total[rows, :part] += factor * jnp.dot(low, block, preferred_element_type=jnp.float32)
        column = iota((groups * room, most), 1)
        target = (column % groups) * slot + column // groups
        pick = (iota((groups * room, most), 0) == target).astype(jnp.bfloat16)
        up = total[:most, :part].astype(jnp.bfloat16)
        moved[...] = jnp.dot(pick, up, preferred_element_type=jnp.float32).astype(jnp.bfloat16)

    total[...] = jnp.zeros_like(total)
    for k in range(blocks):
        rows, factor = place(k, pieces * part)
        block = x[pl.ds(aligned((k ^ own) * length, length), length), :]
        total[rows, :] += factor * jnp.dot(turned[k], block, preferred_element_type=jnp.float32)
    for p in range(pieces):
        out[p, :most, :] = total[:most, p * part : (p + 1) * part].astype(jnp.bfloat16)
        out[p, pl.ds(aligned(width), room), :] = moved[pl.ds(aligned((step * pieces + p) * slot), room), :]


def group_terms(lay, norm, plan, tokens, cotangent, sums):
    rows, features = tokens.shape
    part = cotangent.shape[1]
    rmax = sums[0].shape[1] // 2
    most, room = WIDTHS[-1], share(WIDTHS[-1], lay.groups)
    pieces = 2
    shape = (lay.groups, most + room, part)
    return call(
        functools.partial(terms_kernel, lay, norm),
        jax.ShapeDtypeStruct(shape, jnp.bfloat16),
        (lay.groups // pieces,),
        [pl.BlockSpec((rows, pieces * part), lambda i, plan: (0, i)), whole(cotangent.shape)]
        + [whole(v.shape) for v in sums],
        pl.BlockSpec((pieces,) + shape[1:], lambda i, plan: (i, 0, 0)),
        [
            pltpu.VMEM((most + rmax, pieces * part), jnp.float32),
            pltpu.VMEM((lay.blocks, rmax, rows // lay.blocks), jnp.bfloat16),
            pltpu.VMEM((lay.groups * room, part), jnp.bfloat16),
        ],
        flops=2 * rows * (features + part) * rmax,
        moved=2 * features * (rows + most),
    )(plan, tokens, cotangent, *sums)


def grad_kernel(lay, tiles, parts, plan, *refs):
    cots, (weight, down, backs, backo, out, cat) = refs[:parts], refs[parts:]
    step = pl.program_id(0)
    half = lay.blocks * tiles // 2
    block = lax.div(step, jnp.int32(tiles)) ^ plan[lay.own]
    mine = plan[lay.mine]
    width = cots[0].shape[1]
    for s, cot in enumerate(cots):
        cat[:, pl.ds(aligned((mine ^ s) * width, width), width)] = cot[...]
    rank = plan[lay.rank + plan[0] * lay.blocks + block]
    back = jnp.where(step < half, backs[...], backo[...])
    rows = jnp.where(iota(back.shape, 1) < rank, back, jnp.zeros_like(back))
    chunk = 512
    scale = 32.0 / jnp.full((1, chunk), rank, jnp.int32).astype(jnp.float32)

    def columns(c, carry):
        here = pl.ds(aligned(c * chunk, chunk), chunk)
        base = lax.dot_general(cat[...], weight[here, :], NT, preferred_element_type=jnp.float32)
        extra = lax.dot_general(rows, down[0, here, :], NT, preferred_element_type=jnp.float32)
        out[:, here] = (base + scale * extra).astype(out.dtype)
        return carry

    lax.fori_loop(0, out.shape[1] // chunk, columns, 0)


def input_gradient(lay, plan, cots, weight, adapter_down, sums):
    rows, width = cots[0].shape
    features, values = weight.shape
    blocks = lay.blocks
    tile = rows // blocks
    tiles = 1
    half = blocks * tiles // 2
    rmax = sums[0].shape[1] // 2
    here = lambda i, plan: (i ^ (plan[lay.own] * tiles), 0)

    def adapter(i, plan):
        block = lax.div(i, jnp.int32(tiles)) ^ plan[lay.own]
        return (plan[lay.pair + plan[0] * blocks + block], 0, 0)

    return call(
        functools.partial(grad_kernel, lay, tiles, len(cots)),
        jax.ShapeDtypeStruct((rows, features), jnp.bfloat16),
        (rows // tile,),
        [pl.BlockSpec((tile, width), here)] * len(cots)
        + [
            whole(weight.shape),
            pl.BlockSpec((1, features, rmax), adapter),
            pl.BlockSpec((tile, rmax), lambda i, plan: (jnp.minimum(i, half - 1), 0)),
            pl.BlockSpec((tile, rmax), lambda i, plan: (jnp.maximum(i - half, 0), 0)),
        ],
        pl.BlockSpec((tile, features), here),
        [pltpu.VMEM((tile, values), jnp.bfloat16)],
        flops=2 * rows * features * (values + rmax),
        moved=2 * features * (rows + values),
        room=32,
    )(plan, *cots, weight, adapter_down, *sums)


def reduce_kernel(lay, plan, parts, out, total, cat):
    groups, blocks = lay.groups, lay.blocks
    room, space = share(WIDTHS[-1], groups), share(CAPS[-1], groups)
    width, cap, small = plan[lay.width], plan[lay.cap], plan[lay.small]
    chunk = 128

    def clear(c, carry):
        total[pl.ds(aligned(c * chunk, chunk), chunk), :] = jnp.zeros((chunk, total.shape[1]), total.dtype)
        return carry

    lax.fori_loop(0, lax.div(groups * cap + chunk - 1, jnp.int32(chunk)), clear, 0)
    place = iota((1, groups * room), 1)
    target = jnp.full((1, groups * room), -1, jnp.int32)
    for g in range(groups):
        cat[g * room : (g + 1) * room, :] = parts[g, pl.ds(aligned(width), room), :]
        for b in range(blocks):
            i = g * blocks + b
            rank, source = plan[lay.first + i], plan[lay.off + i]
            owner, into = plan[lay.owner + i], plan[lay.into + i]
            goal = owner * cap + into
            for size in SIZES:

                @pl.when(rank == size)
                def _(g=g, source=source, goal=goal, size=size):
                    here = pl.ds(aligned(source), size)
                    total[pl.ds(aligned(goal), size), :] += parts[g, here, :].astype(jnp.float32)

            start = g * room + lax.div(source, jnp.int32(groups))
            inside = jnp.logical_and(place >= start, place < start + lax.div(rank, jnp.int32(groups)))
            shift = owner * small + lax.div(into, jnp.int32(groups)) - start
            target = jnp.where(inside, place + shift, target)
    line = iota((space, groups * room), 0)

    def owner_rows(o, carry):
        def copy(c, carry):
            here = pl.ds(aligned(c * chunk, chunk), chunk)
            out[o, here, :] = total[pl.ds(aligned(o * cap + c * chunk), chunk), :].astype(out.dtype)
            return carry

        lax.fori_loop(0, lax.div(cap + chunk - 1, jnp.int32(chunk)), copy, 0)
        pick = (line + o * small == target).astype(jnp.bfloat16)
        rows = jnp.dot(pick, cat[...], preferred_element_type=jnp.float32).astype(out.dtype)
        out[o, pl.ds(aligned(cap), space), :] = rows
        return carry

    lax.fori_loop(0, groups, owner_rows, 0)


def reduce_terms(lay, rmax, plan, parts):
    part = parts.shape[2]
    groups, most = lay.groups, CAPS[-1]
    shape = (groups, most + rmax, part)
    return call(
        functools.partial(reduce_kernel, lay),
        jax.ShapeDtypeStruct(shape, jnp.bfloat16),
        (1,),
        [whole(parts.shape)],
        whole(shape),
        [
            pltpu.VMEM((groups * most + 128, part), jnp.float32),
            pltpu.VMEM((groups * share(WIDTHS[-1], groups), part), jnp.bfloat16),
        ],
        flops=2 * most * WIDTHS[-1] * part,
        moved=4 * groups * most * part,
        room=30,
    )(plan, parts)


def unpack_kernel(lay, plan, slots, down, up, cat):
    groups = lay.groups
    per = lay.npair // groups
    me, cap = plan[0], plan[lay.cap]
    part, rmax, space = slots.shape[2], down.shape[2], share(CAPS[-1], groups)
    eye = (iota((part, part), 0) == iota((part, part), 1)).astype(jnp.bfloat16)
    for s in range(groups):
        cat[s * space : (s + 1) * space, :] = slots[s, pl.ds(aligned(cap), space), :]
    shape = (rmax, groups * space)
    r, column = iota(shape, 0), iota(shape, 1)
    place = (r % groups) * space + r // groups
    for k in range(per):
        start, rank = plan[lay.pair_into + me * per + k], plan[lay.pair_rank + me * per + k]

        @pl.when(rank > 0)
        def _(k=k, start=start, rank=rank):
            for s in range(groups):
                rows = slots[s, pl.ds(aligned(start), rmax), :]
                rows = jnp.where(iota(rows.shape, 0) < rank, rows, jnp.zeros_like(rows))
                value = lax.dot_general(eye, rows, NT, preferred_element_type=jnp.float32)
                down[k, s * part : (s + 1) * part, :] = value.astype(down.dtype)
            match = column == place + lax.div(start, jnp.int32(groups))
            pick = jnp.logical_and(match, r < rank).astype(jnp.bfloat16)
            up[k] = jnp.dot(pick, cat[...], preferred_element_type=jnp.float32).astype(up.dtype)

        @pl.when(rank == 0)
        def _(k=k):
            down[k] = jnp.zeros_like(down[k])
            up[k] = jnp.zeros_like(up[k])


def unpack(lay, plan, slots, features, rmax):
    part = slots.shape[2]
    per = lay.npair // lay.groups
    shapes = [(per, features, rmax), (per, rmax, part)]
    return call(
        functools.partial(unpack_kernel, lay),
        [jax.ShapeDtypeStruct(shape, jnp.bfloat16) for shape in shapes],
        (1,),
        [whole(slots.shape)],
        [whole(shape) for shape in shapes],
        [pltpu.VMEM((lay.groups * share(CAPS[-1], lay.groups), part), jnp.bfloat16)],
        flops=2 * per * features * rmax * part,
        moved=2 * per * features * rmax,
    )(plan, slots)


def far_parts(x, axis):
    size = lax.axis_size(axis)
    parts = {0: x}
    bit = size // 2
    while bit > 1:
        for k in sorted(parts):
            parts[k ^ bit] = swap(parts[k], axis, bit)
        bit //= 2
    return [parts[k] for k in sorted(parts) if k], swap(x, axis, 1)


def all_parts(x, far, near, axis):
    out = [x, near]
    for part in far:
        out += [part, swap(part, axis, 1)]
    return out


def spread(rows, parts):
    sent = lax.all_to_all(parts[:, :rows, :], "pair", split_axis=0, concat_axis=0, tiled=True)
    return jnp.pad(sent, ((0, 0), (0, parts.shape[1] - rows), (0, 0)))


def first_exchange(rows, terms, cotangent):
    return spread(rows, terms), *far_parts(cotangent, "fsdp")


def second_exchange(lay, rows, plan, sums, cotangent, far, near, weight, adapter_down, ranked):
    cots = all_parts(cotangent, far, near, "fsdp")
    return spread(rows, sums), input_gradient(lay, plan, cots, weight, adapter_down, ranked)


def per_device(tokens, cotangent, value_weight, adapter_down, adapter_up, pair_ids, ranks):
    rows = tokens.shape[0]
    blocks = pair_ids.shape[0]
    groups, shares = lax.axis_size("pair"), lax.axis_size("fsdp")
    lay = Layout(groups, blocks, adapter_down.shape[0])
    norm = 1.0 / math.sqrt(rows * groups)
    me, mine = lax.axis_index("pair"), lax.axis_index("fsdp")
    where = jnp.stack([me, mine, (mine & 1) * (blocks // 2)]).astype(jnp.int32)
    ids = jnp.concatenate([pair_ids, swap(pair_ids, "pair", 1)])
    kept, sent = rank_sums(where, pair_ids, cotangent, adapter_up, tokens, adapter_down)
    ids, sent = lax.optimization_barrier((ids, sent))
    sums = add(kept, swap(sent, "fsdp", 1))
    if groups > 2:
        ids = jnp.concatenate([ids, swap(ids, "pair", 2)])
    sums, ids = lax.optimization_barrier((sums, ids))
    bit = 4
    while bit < groups:
        ids = jnp.concatenate([ids, swap(ids, "pair", bit)])
        bit *= 2
    plan = make_plan(lay, ids, ranks, where)
    bit = 2
    while bit < shares:
        theirs = swap(sums, "fsdp", bit)
        theirs, plan = lax.optimization_barrier((theirs, plan))
        sums = add(sums, theirs)
        bit *= 2
    sums = (sums, swap(sums, "fsdp", 1))
    terms = group_terms(lay, norm, plan, tokens, cotangent, sums)
    branches = [functools.partial(first_exchange, size + share(size, groups)) for size in WIDTHS]
    received, far, near = lax.switch(plan[lay.width_at], branches, terms, cotangent)
    reduced = reduce_terms(lay, adapter_down.shape[2], plan, received)
    branches = [functools.partial(second_exchange, lay, size + share(size, groups)) for size in CAPS]
    slots, input_grad = lax.switch(
        plan[lay.cap_at], branches, plan, reduced, cotangent, far, near, value_weight, adapter_down, sums
    )
    down_grad, up_grad = unpack(lay, plan, slots, tokens.shape[1], adapter_down.shape[2])
    return input_grad, down_grad, up_grad


def dense_per_device(tokens, cotangent, value_weight, adapter_down, adapter_up, pair_ids, ranks):
    rows, features = tokens.shape
    blocks = pair_ids.shape[0]
    length = rows // blocks
    npair, _, rmax = adapter_down.shape
    norm = 1.0 / math.sqrt(rows * lax.axis_size("pair"))
    mask = (jnp.arange(rmax, dtype=jnp.int32)[None, :] < ranks[:, None]).astype(jnp.float32)
    scale = 32.0 / ranks.astype(jnp.float32)
    x = tokens.reshape(blocks, length, features)
    c = cotangent.reshape(blocks, length, cotangent.shape[1])
    down, up = adapter_down[pair_ids], adapter_up[pair_ids]
    wide = {"preferred_element_type": jnp.float32}
    low = lax.psum(jnp.einsum("btd,bdr->btr", x, down, **wide).astype(jnp.bfloat16), "fsdp")
    back = lax.psum(jnp.einsum("btk,brk->btr", c, up, **wide).astype(jnp.bfloat16), "fsdp")
    rows_mask = mask[pair_ids][:, None, :]
    low = (low.astype(jnp.float32) * rows_mask).astype(jnp.bfloat16)
    back = (back.astype(jnp.float32) * rows_mask).astype(jnp.bfloat16)
    cots = lax.all_gather(cotangent, "fsdp", axis=1, tiled=True)
    base = jnp.einsum("tk,dk->td", cots, value_weight, **wide).reshape(blocks, length, features)
    factor = scale[pair_ids][:, None, None]
    input_grad = (base + factor * jnp.einsum("btr,bdr->btd", back, down, **wide)).astype(jnp.bfloat16)
    term_a = jnp.einsum("btd,btr->bdr", x, back, **wide) * (factor * norm)
    term_b = jnp.einsum("btr,btk->brk", low, c, **wide) * (factor * norm)
    onehot = (pair_ids[:, None] == jnp.arange(npair, dtype=jnp.int32)[None, :]).astype(jnp.float32)
    grads = [
        lax.psum_scatter(
            jnp.einsum("bp,bij->pij", onehot, term).astype(jnp.bfloat16), "pair", scatter_dimension=0, tiled=True
        )
        for term in (term_a, term_b)
    ]
    return input_grad.reshape(rows, features), grads[0], grads[1]


def per_shape(tokens, cotangent, value_weight, adapter_down, adapter_up, pair_ids, ranks):
    groups, shares = lax.axis_size("pair"), lax.axis_size("fsdp")
    blocks = pair_ids.shape[0]
    part = tokens.shape[1] // groups
    power = lambda v: v & (v - 1) == 0
    fits = (
        part % 128 == 0
        and part == cotangent.shape[1]
        and power(groups)
        and power(shares)
        and power(blocks)
        and min(shares, blocks) > 1
        and groups <= 8
        and WIDTHS[-1] >= blocks * adapter_down.shape[2]
        and CAPS[-1] >= adapter_down.shape[0] // groups * adapter_down.shape[2]
    )
    form = per_device if fits else dense_per_device
    return form(tokens, cotangent, value_weight, adapter_down, adapter_up, pair_ids, ranks)


def solution(mesh):
    placed = (
        P("pair", "fsdp"),
        P("pair", "fsdp"),
        P("fsdp", None),
        P(None, "fsdp", None),
        P(None, None, "fsdp"),
        P("pair"),
        P(),
    )
    return jax.shard_map(
        per_shape,
        mesh=mesh,
        in_specs=placed,
        out_specs=(P("pair", "fsdp"), P("pair", "fsdp", None), P("pair", None, "fsdp")),
        check_vma=False,
    )
```

```python
import functools
import math

import jax
import jax.numpy as jnp
from jax import lax
from jax.experimental import pallas as pl
from jax.experimental.pallas import tpu as pltpu
from jax.sharding import PartitionSpec as P

WIDTHS = (224, 256, 288, 320, 352, 384, 416, 448, 512)
CAPS = (160, 192, 224, 256, 288, 320, 352, 384, 448, 768)
ALIGN = 16
HEAD = 16
NT = (((1,), (1,)), ((), ()))
MIB = 1024 * 1024
SIZES = (128, 64, 32, 16)


def call(kernel, out_shape, grid, in_specs, out_specs, scratch=(), flops=0, moved=0, prefetch=1, room=40):
    return pl.pallas_call(
        kernel,
        out_shape=out_shape,
        grid_spec=pltpu.PrefetchScalarGridSpec(
            num_scalar_prefetch=prefetch,
            grid=grid,
            in_specs=in_specs,
            out_specs=out_specs,
            scratch_shapes=list(scratch),
        ),
        compiler_params=pltpu.CompilerParams(vmem_limit_bytes=room * MIB),
        cost_estimate=pl.CostEstimate(flops=flops, bytes_accessed=moved, transcendentals=0),
    )


def whole(shape):
    return pl.BlockSpec(shape, lambda i, *s: (0,) * len(shape))


def iota(shape, axis):
    return lax.broadcasted_iota(jnp.int32, shape, axis)


def aligned(index, unit=ALIGN):
    return pl.multiple_of(index, unit)


def swap(x, axis, bit):
    size = lax.axis_size(axis)
    return lax.ppermute(x, axis, [(i, i ^ bit) for i in range(size)])


def share(columns, groups):
    return -(-columns // (groups * ALIGN)) * ALIGN


class Layout:
    def __init__(self, groups, blocks, npair):
        self.groups, self.blocks, self.npair = groups, blocks, npair
        count = groups * blocks
        self.mine, self.own = 1, 2
        self.width_at, self.width, self.slot, self.cap_at, self.cap, self.small = 3, 4, 5, 6, 7, 8
        self.off = HEAD
        self.first = self.off + count
        self.owner = self.first + count
        self.into = self.owner + count
        self.pair = self.into + count
        self.rank = self.pair + count
        self.pair_into = self.rank + count
        self.pair_rank = self.pair_into + npair
        self.size = self.pair_rank + npair


def plan_kernel(lay, ids, ranks, where_ref, plan):
    groups, blocks, npair = lay.groups, lay.blocks, lay.npair
    per = npair // groups
    me = where_ref[0]
    for k in range(3):
        plan[k] = where_ref[k]

    def clear(p, carry):
        plan[lay.pair_rank + p] = 0
        return carry

    lax.fori_loop(0, npair, clear, 0)

    def group(g, widest):
        total = jnp.int32(0)
        pairs = [ids[(g ^ me) * blocks + b] for b in range(blocks)]
        places = []
        for b in range(blocks):
            i = g * blocks + b
            pair = pairs[b]
            rank = ranks[pair]
            plan[lay.pair_rank + pair] = rank
            place, new = total, rank
            for a in range(b):
                same = pairs[a] == pair
                place = jnp.where(same, places[a], place)
                new = jnp.where(same, 0, new)
            places.append(place)
            plan[lay.off + i] = place
            plan[lay.first + i] = new
            plan[lay.pair + i] = pair
            plan[lay.rank + i] = rank
            total = total + new
        return jnp.maximum(widest, total)

    widest = lax.fori_loop(0, groups, group, jnp.int32(0))

    def owner(o, fullest):
        total = jnp.int32(0)
        for k in range(per):
            p = o * per + k
            plan[lay.pair_into + p] = total
            total = total + plan[lay.pair_rank + p]
        return jnp.maximum(fullest, total)

    fullest = lax.fori_loop(0, groups, owner, jnp.int32(0))

    def block(i, carry):
        pair = plan[lay.pair + i]
        plan[lay.owner + i] = lax.div(pair, jnp.int32(per))
        plan[lay.into + i] = plan[lay.pair_into + pair]
        return carry

    lax.fori_loop(0, groups * blocks, block, 0)
    for need, sizes, at in ((widest, WIDTHS, lay.width_at), (fullest, CAPS, lay.cap_at)):
        values = [(k, size, share(size, groups)) for k, size in enumerate(sizes)]
        chosen = [jnp.int32(v) for v in values[-1]]
        for k, size, rows in reversed(values[:-1]):
            fits = need <= size
            chosen = [jnp.where(fits, v, c) for v, c in zip((k, size, rows), chosen)]
        for k in range(3):
            plan[at + k] = chosen[k]


def make_plan(lay, ids, ranks, where):
    smem = pl.BlockSpec(memory_space=pltpu.SMEM)
    return pl.pallas_call(
        functools.partial(plan_kernel, lay),
        out_shape=jax.ShapeDtypeStruct((lay.size,), jnp.int32),
        in_specs=[smem] * 3,
        out_specs=smem,
    )(ids, ranks, where)


def rank_kernel(half, where_ref, ids, cot, up, x, down, kept, sent):
    step = pl.program_id(0)
    rmax = up.shape[1]
    back = lax.dot_general(cot[...], up[0], NT, preferred_element_type=jnp.float32).astype(kept.dtype)
    low = jnp.dot(x[...], down[0], preferred_element_type=jnp.float32).astype(kept.dtype)

    @pl.when(step < half)
    def _():
        kept[:, :rmax] = back
        kept[:, rmax:] = low

    @pl.when(step >= half)
    def _():
        sent[:, :rmax] = back
        sent[:, rmax:] = low


def rank_sums(where, ids, cotangent, adapter_up, tokens, adapter_down):
    rows, width = cotangent.shape
    features = tokens.shape[1]
    blocks, rmax = ids.shape[0], adapter_up.shape[1]
    length, half = rows // blocks, blocks // 2
    out = jax.ShapeDtypeStruct((rows // 2, 2 * rmax), jnp.bfloat16)
    rows_of = lambda i, w, s: (i ^ w[2], 0)
    pair_of = lambda i, w, s: (s[i ^ w[2]], 0, 0)
    return call(
        functools.partial(rank_kernel, half),
        [out, out],
        (blocks,),
        [
            pl.BlockSpec((length, width), rows_of),
            pl.BlockSpec((1, rmax, width), pair_of),
            pl.BlockSpec((length, features), rows_of),
            pl.BlockSpec((1, features, rmax), pair_of),
        ],
        [
            pl.BlockSpec((length, 2 * rmax), lambda i, w, s: (jnp.minimum(i, half - 1), 0)),
            pl.BlockSpec((length, 2 * rmax), lambda i, w, s: (jnp.maximum(i - half, 0), 0)),
        ],
        flops=2 * rows * (width + features) * rmax,
        moved=2 * rows * (width + features + 2 * rmax),
        prefetch=2,
        room=56,
    )(where, ids, cotangent, adapter_up, tokens, adapter_down)


def add(a, b):
    return (a.astype(jnp.float32) + b.astype(jnp.float32)).astype(a.dtype)


def turn(rank, value):
    shape = (value.shape[1], value.shape[1])
    eye = jnp.logical_and(iota(shape, 0) == iota(shape, 1), iota(shape, 0) < rank).astype(jnp.bfloat16)
    return lax.dot_general(eye, value, NT, preferred_element_type=jnp.float32).astype(jnp.bfloat16)


def terms_kernel(lay, norm, plan, x, cot, own_sums, other_sums, out, total, turned, moved):
    groups, blocks = lay.groups, lay.blocks
    half = blocks // 2
    step = pl.program_id(0)
    length, rmax, part = turned.shape[2], turned.shape[1], out.shape[2]
    most, room = WIDTHS[-1], share(WIDTHS[-1], groups)
    pieces = out.shape[0]
    me, own = plan[0], plan[lay.own]
    width, slot = plan[lay.width], plan[lay.slot]

    def place(k, columns):
        i = me * blocks + (k ^ own)
        factor = 32.0 / jnp.full((1, columns), plan[lay.rank + i], jnp.int32).astype(jnp.float32) * norm
        return pl.ds(aligned(plan[lay.off + i]), rmax), factor

    @pl.when(step == 0)
    def _():
        total[:, :part] = jnp.zeros((total.shape[0], part), total.dtype)
        for k in range(blocks):
            b = k ^ own
            rank = plan[lay.rank + me * blocks + b]
            source = own_sums if k < half else other_sums
            lines = slice(k % half * length, (k % half + 1) * length)
            turned[k] = turn(rank, source[lines, :rmax])
            low = turn(rank, source[lines, rmax:])
            rows, factor = place(k, part)
            block = cot[pl.ds(aligned(b * length, length), length), :]
            total[rows, :part] += factor * jnp.dot(low, block, preferred_element_type=jnp.float32)
        column = iota((groups * room, most), 1)
        target = (column % groups) * slot + column // groups
        pick = (iota((groups * room, most), 0) == target).astype(jnp.bfloat16)
        up = total[:most, :part].astype(jnp.bfloat16)
        moved[...] = jnp.dot(pick, up, preferred_element_type=jnp.float32).astype(jnp.bfloat16)

    total[...] = jnp.zeros_like(total)
    for k in range(blocks):
        rows, factor = place(k, pieces * part)
        block = x[pl.ds(aligned((k ^ own) * length, length), length), :]
        total[rows, :] += factor * jnp.dot(turned[k], block, preferred_element_type=jnp.float32)
    for p in range(pieces):
        out[p, :most, :] = total[:most, p * part : (p + 1) * part].astype(jnp.bfloat16)
        out[p, pl.ds(aligned(width), room), :] = moved[pl.ds(aligned((step * pieces + p) * slot), room), :]


def group_terms(lay, norm, plan, tokens, cotangent, sums):
    rows, features = tokens.shape
    part = cotangent.shape[1]
    rmax = sums[0].shape[1] // 2
    most, room = WIDTHS[-1], share(WIDTHS[-1], lay.groups)
    pieces = 2
    shape = (lay.groups, most + room, part)
    return call(
        functools.partial(terms_kernel, lay, norm),
        pltpu.VMEM(shape, jnp.bfloat16),
        (lay.groups // pieces,),
        [pl.BlockSpec((rows, pieces * part), lambda i, plan: (0, i)), whole(cotangent.shape)]
        + [whole(v.shape) for v in sums],
        pl.BlockSpec((pieces,) + shape[1:], lambda i, plan: (i, 0, 0)),
        [
            pltpu.VMEM((most + rmax, pieces * part), jnp.float32),
            pltpu.VMEM((lay.blocks, rmax, rows // lay.blocks), jnp.bfloat16),
            pltpu.VMEM((lay.groups * room, part), jnp.bfloat16),
        ],
        flops=2 * rows * (features + part) * rmax,
        moved=2 * features * (rows + most),
    )(plan, tokens, cotangent, *sums)


def grad_kernel(lay, tiles, parts, plan, *refs):
    cots, (weight, down, backs, backo, out, cat) = refs[:parts], refs[parts:]
    step = pl.program_id(0)
    half = lay.blocks * tiles // 2
    block = lax.div(step, jnp.int32(tiles)) ^ plan[lay.own]
    mine = plan[lay.mine]
    width = cots[0].shape[1]
    for s, cot in enumerate(cots):
        cat[:, pl.ds(aligned((mine ^ s) * width, width), width)] = cot[...]
    rank = plan[lay.rank + plan[0] * lay.blocks + block]
    back = jnp.where(step < half, backs[...], backo[...])
    rows = jnp.where(iota(back.shape, 1) < rank, back, jnp.zeros_like(back))
    chunk = 512
    scale = 32.0 / jnp.full((1, chunk), rank, jnp.int32).astype(jnp.float32)

    def columns(c, carry):
        here = pl.ds(aligned(c * chunk, chunk), chunk)
        base = lax.dot_general(cat[...], weight[here, :], NT, preferred_element_type=jnp.float32)
        extra = lax.dot_general(rows, down[0, here, :], NT, preferred_element_type=jnp.float32)
        out[:, here] = (base + scale * extra).astype(out.dtype)
        return carry

    lax.fori_loop(0, out.shape[1] // chunk, columns, 0)


def input_gradient(lay, plan, cots, weight, adapter_down, sums):
    rows, width = cots[0].shape
    features, values = weight.shape
    blocks = lay.blocks
    tile = rows // blocks
    tiles = 1
    half = blocks * tiles // 2
    rmax = sums[0].shape[1] // 2
    here = lambda i, plan: (i ^ (plan[lay.own] * tiles), 0)

    def adapter(i, plan):
        block = lax.div(i, jnp.int32(tiles)) ^ plan[lay.own]
        return (plan[lay.pair + plan[0] * blocks + block], 0, 0)

    return call(
        functools.partial(grad_kernel, lay, tiles, len(cots)),
        jax.ShapeDtypeStruct((rows, features), jnp.bfloat16),
        (rows // tile,),
        [pl.BlockSpec((tile, width), here)] * len(cots)
        + [
            whole(weight.shape),
            pl.BlockSpec((1, features, rmax), adapter),
            pl.BlockSpec((tile, rmax), lambda i, plan: (jnp.minimum(i, half - 1), 0)),
            pl.BlockSpec((tile, rmax), lambda i, plan: (jnp.maximum(i - half, 0), 0)),
        ],
        pl.BlockSpec((tile, features), here),
        [pltpu.VMEM((tile, values), jnp.bfloat16)],
        flops=2 * rows * features * (values + rmax),
        moved=2 * features * (rows + values),
        room=32,
    )(plan, *cots, weight, adapter_down, *sums)


def reduce_kernel(lay, plan, parts, out, total, cat):
    groups, blocks = lay.groups, lay.blocks
    room, space = share(WIDTHS[-1], groups), share(CAPS[-1], groups)
    width, slot, cap, small = plan[lay.width], plan[lay.slot], plan[lay.cap], plan[lay.small]
    chunk = 128

    def clear(c, carry):
        total[pl.ds(aligned(c * chunk, chunk), chunk), :] = jnp.zeros((chunk, total.shape[1]), total.dtype)
        return carry

    lax.fori_loop(0, lax.div(groups * cap + chunk - 1, jnp.int32(chunk)), clear, 0)
    place = iota((1, groups * room), 1)
    target = jnp.full((1, groups * room), -1, jnp.int32)
    for g in range(groups):
        held = parts[g, pl.ds(aligned(width), room), :]
        cat[g * room : (g + 1) * room, :] = jnp.where(iota(held.shape, 0) < slot, held, jnp.zeros_like(held))
        for b in range(blocks):
            i = g * blocks + b
            rank, source = plan[lay.first + i], plan[lay.off + i]
            owner, into = plan[lay.owner + i], plan[lay.into + i]
            goal = owner * cap + into
            for size in SIZES:

                @pl.when(rank == size)
                def _(g=g, source=source, goal=goal, size=size):
                    here = pl.ds(aligned(source), size)
                    total[pl.ds(aligned(goal), size), :] += parts[g, here, :].astype(jnp.float32)

            start = g * room + lax.div(source, jnp.int32(groups))
            inside = jnp.logical_and(place >= start, place < start + lax.div(rank, jnp.int32(groups)))
            shift = owner * small + lax.div(into, jnp.int32(groups)) - start
            target = jnp.where(inside, place + shift, target)
    line = iota((space, groups * room), 0)

    def owner_rows(o, carry):
        def copy(c, carry):
            here = pl.ds(aligned(c * chunk, chunk), chunk)
            out[o, here, :] = total[pl.ds(aligned(o * cap + c * chunk), chunk), :].astype(out.dtype)
            return carry

        lax.fori_loop(0, lax.div(cap + chunk - 1, jnp.int32(chunk)), copy, 0)
        pick = (line + o * small == target).astype(jnp.bfloat16)
        rows = jnp.dot(pick, cat[...], preferred_element_type=jnp.float32).astype(out.dtype)
        out[o, pl.ds(aligned(cap), space), :] = rows
        return carry

    lax.fori_loop(0, groups, owner_rows, 0)


def reduce_terms(lay, rmax, plan, parts):
    part = parts.shape[2]
    groups, most = lay.groups, CAPS[-1]
    shape = (groups, most + rmax, part)
    return call(
        functools.partial(reduce_kernel, lay),
        pltpu.VMEM(shape, jnp.bfloat16),
        (1,),
        [whole(parts.shape)],
        whole(shape),
        [
            pltpu.VMEM((groups * most + 128, part), jnp.float32),
            pltpu.VMEM((groups * share(WIDTHS[-1], groups), part), jnp.bfloat16),
        ],
        flops=2 * most * WIDTHS[-1] * part,
        moved=4 * groups * most * part,
        room=30,
    )(plan, parts)


def unpack_kernel(lay, plan, slots, down, up, cat):
    groups = lay.groups
    per = lay.npair // groups
    me, cap = plan[0], plan[lay.cap]
    part, rmax, space = slots.shape[2], down.shape[2], share(CAPS[-1], groups)
    eye = (iota((part, part), 0) == iota((part, part), 1)).astype(jnp.bfloat16)
    for s in range(groups):
        held = slots[s, pl.ds(aligned(cap), space), :]
        cat[s * space : (s + 1) * space, :] = jnp.where(iota(held.shape, 0) < plan[lay.small], held, jnp.zeros_like(held))
    shape = (rmax, groups * space)
    r, column = iota(shape, 0), iota(shape, 1)
    place = (r % groups) * space + r // groups
    for k in range(per):
        start, rank = plan[lay.pair_into + me * per + k], plan[lay.pair_rank + me * per + k]

        @pl.when(rank > 0)
        def _(k=k, start=start, rank=rank):
            for s in range(groups):
                rows = slots[s, pl.ds(aligned(start), rmax), :]
                rows = jnp.where(iota(rows.shape, 0) < rank, rows, jnp.zeros_like(rows))
                value = lax.dot_general(eye, rows, NT, preferred_element_type=jnp.float32)
                down[k, s * part : (s + 1) * part, :] = value.astype(down.dtype)
            match = column == place + lax.div(start, jnp.int32(groups))
            pick = jnp.logical_and(match, r < rank).astype(jnp.bfloat16)
            up[k] = jnp.dot(pick, cat[...], preferred_element_type=jnp.float32).astype(up.dtype)

        @pl.when(rank == 0)
        def _(k=k):
            down[k] = jnp.zeros_like(down[k])
            up[k] = jnp.zeros_like(up[k])


def unpack(lay, plan, slots, features, rmax):
    part = slots.shape[2]
    per = lay.npair // lay.groups
    shapes = [(per, features, rmax), (per, rmax, part)]
    return call(
        functools.partial(unpack_kernel, lay),
        [jax.ShapeDtypeStruct(shape, jnp.bfloat16) for shape in shapes],
        (1,),
        [whole(slots.shape)],
        [whole(shape) for shape in shapes],
        [pltpu.VMEM((lay.groups * share(CAPS[-1], lay.groups), part), jnp.bfloat16)],
        flops=2 * per * features * rmax * part,
        moved=2 * per * features * rmax,
    )(plan, slots)


def far_parts(x, axis):
    size = lax.axis_size(axis)
    parts = {0: x}
    bit = size // 2
    while bit > 1:
        for k in sorted(parts):
            parts[k ^ bit] = swap(parts[k], axis, bit)
        bit //= 2
    return [parts[k] for k in sorted(parts) if k], swap(x, axis, 1)


def all_parts(x, far, near, axis):
    out = [x, near]
    for part in far:
        out += [part, swap(part, axis, 1)]
    return out


def move_kernel(rows, source, out, sems):
    copies = [
        pltpu.make_async_copy(source.at[g, pl.ds(0, rows)], out.at[g, pl.ds(0, rows)], sems.at[g])
        for g in range(out.shape[0])
    ]
    for copy in copies:
        copy.start()
    for copy in copies:
        copy.wait()


def move(source, rows, size, fast):
    groups, _, part = source.shape
    kind = pltpu.VMEM if fast else pltpu.HBM
    return pl.pallas_call(
        functools.partial(move_kernel, rows),
        out_shape=kind((groups, size, part), source.dtype),
        in_specs=[pl.BlockSpec(memory_space=pl.ANY)],
        out_specs=pl.BlockSpec(memory_space=pl.ANY),
        scratch_shapes=[pltpu.SemaphoreType.DMA((groups,))],
    )(source)


def spread(rows, parts, fast):
    sent = lax.all_to_all(move(parts, rows, rows, False), "pair", split_axis=0, concat_axis=0, tiled=True)
    return move(sent, rows, parts.shape[1], fast)


def first_exchange(rows, terms, cotangent):
    return spread(rows, terms, True), *far_parts(cotangent, "fsdp")


def second_exchange(lay, rows, plan, sums, cotangent, far, near, weight, adapter_down, ranked):
    cots = all_parts(cotangent, far, near, "fsdp")
    return spread(rows, sums, False), input_gradient(lay, plan, cots, weight, adapter_down, ranked)


def per_device(tokens, cotangent, value_weight, adapter_down, adapter_up, pair_ids, ranks):
    rows = tokens.shape[0]
    blocks = pair_ids.shape[0]
    groups, shares = lax.axis_size("pair"), lax.axis_size("fsdp")
    lay = Layout(groups, blocks, adapter_down.shape[0])
    norm = 1.0 / math.sqrt(rows * groups)
    me, mine = lax.axis_index("pair"), lax.axis_index("fsdp")
    where = jnp.stack([me, mine, (mine & 1) * (blocks // 2)]).astype(jnp.int32)
    ids = jnp.concatenate([pair_ids, swap(pair_ids, "pair", 1)])
    kept, sent = rank_sums(where, pair_ids, cotangent, adapter_up, tokens, adapter_down)
    ids, sent = lax.optimization_barrier((ids, sent))
    sums = add(kept, swap(sent, "fsdp", 1))
    if groups > 2:
        ids = jnp.concatenate([ids, swap(ids, "pair", 2)])
    sums, ids = lax.optimization_barrier((sums, ids))
    bit = 4
    while bit < groups:
        ids = jnp.concatenate([ids, swap(ids, "pair", bit)])
        bit *= 2
    plan = make_plan(lay, ids, ranks, where)
    bit = 2
    while bit < shares:
        theirs = swap(sums, "fsdp", bit)
        theirs, plan = lax.optimization_barrier((theirs, plan))
        sums = add(sums, theirs)
        bit *= 2
    sums = (sums, swap(sums, "fsdp", 1))
    terms = group_terms(lay, norm, plan, tokens, cotangent, sums)
    branches = [functools.partial(first_exchange, size + share(size, groups)) for size in WIDTHS]
    received, far, near = lax.switch(plan[lay.width_at], branches, terms, cotangent)
    reduced = reduce_terms(lay, adapter_down.shape[2], plan, received)
    branches = [functools.partial(second_exchange, lay, size + share(size, groups)) for size in CAPS]
    slots, input_grad = lax.switch(
        plan[lay.cap_at], branches, plan, reduced, cotangent, far, near, value_weight, adapter_down, sums
    )
    down_grad, up_grad = unpack(lay, plan, slots, tokens.shape[1], adapter_down.shape[2])
    return input_grad, down_grad, up_grad


def dense_per_device(tokens, cotangent, value_weight, adapter_down, adapter_up, pair_ids, ranks):
    rows, features = tokens.shape
    blocks = pair_ids.shape[0]
    length = rows // blocks
    npair, _, rmax = adapter_down.shape
    norm = 1.0 / math.sqrt(rows * lax.axis_size("pair"))
    mask = (jnp.arange(rmax, dtype=jnp.int32)[None, :] < ranks[:, None]).astype(jnp.float32)
    scale = 32.0 / ranks.astype(jnp.float32)
    x = tokens.reshape(blocks, length, features)
    c = cotangent.reshape(blocks, length, cotangent.shape[1])
    down, up = adapter_down[pair_ids], adapter_up[pair_ids]
    wide = {"preferred_element_type": jnp.float32}
    low = lax.psum(jnp.einsum("btd,bdr->btr", x, down, **wide).astype(jnp.bfloat16), "fsdp")
    back = lax.psum(jnp.einsum("btk,brk->btr", c, up, **wide).astype(jnp.bfloat16), "fsdp")
    rows_mask = mask[pair_ids][:, None, :]
    low = (low.astype(jnp.float32) * rows_mask).astype(jnp.bfloat16)
    back = (back.astype(jnp.float32) * rows_mask).astype(jnp.bfloat16)
    cots = lax.all_gather(cotangent, "fsdp", axis=1, tiled=True)
    base = jnp.einsum("tk,dk->td", cots, value_weight, **wide).reshape(blocks, length, features)
    factor = scale[pair_ids][:, None, None]
    input_grad = (base + factor * jnp.einsum("btr,bdr->btd", back, down, **wide)).astype(jnp.bfloat16)
    term_a = jnp.einsum("btd,btr->bdr", x, back, **wide) * (factor * norm)
    term_b = jnp.einsum("btr,btk->brk", low, c, **wide) * (factor * norm)
    onehot = (pair_ids[:, None] == jnp.arange(npair, dtype=jnp.int32)[None, :]).astype(jnp.float32)
    grads = [
        lax.psum_scatter(
            jnp.einsum("bp,bij->pij", onehot, term).astype(jnp.bfloat16), "pair", scatter_dimension=0, tiled=True
        )
        for term in (term_a, term_b)
    ]
    return input_grad.reshape(rows, features), grads[0], grads[1]


def per_shape(tokens, cotangent, value_weight, adapter_down, adapter_up, pair_ids, ranks):
    groups, shares = lax.axis_size("pair"), lax.axis_size("fsdp")
    blocks = pair_ids.shape[0]
    part = tokens.shape[1] // groups
    power = lambda v: v & (v - 1) == 0
    fits = (
        part % 128 == 0
        and part == cotangent.shape[1]
        and power(groups)
        and power(shares)
        and power(blocks)
        and min(shares, blocks) > 1
        and groups <= 8
        and WIDTHS[-1] >= blocks * adapter_down.shape[2]
        and CAPS[-1] >= adapter_down.shape[0] // groups * adapter_down.shape[2]
    )
    form = per_device if fits else dense_per_device
    return form(tokens, cotangent, value_weight, adapter_down, adapter_up, pair_ids, ranks)


def solution(mesh):
    placed = (
        P("pair", "fsdp"),
        P("pair", "fsdp"),
        P("fsdp", None),
        P(None, "fsdp", None),
        P(None, None, "fsdp"),
        P("pair"),
        P(),
    )
    return jax.shard_map(
        per_shape,
        mesh=mesh,
        in_specs=placed,
        out_specs=(P("pair", "fsdp"), P("pair", "fsdp", None), P("pair", None, "fsdp")),
        check_vma=False,
    )
```

```python
import functools
import math

import jax
import jax.numpy as jnp
from jax import lax
from jax.experimental import pallas as pl
from jax.experimental.pallas import tpu as pltpu
from jax.sharding import PartitionSpec as P

WIDTHS = tuple(range(208, 513, 16))
CAPS = (*range(144, 401, 16), 448, 512, 768)
ALIGN = 16
HEAD = 16
NT = (((1,), (1,)), ((), ()))
MIB = 1024 * 1024
SIZES = (128, 64, 32, 16)


def call(kernel, out_shape, grid, in_specs, out_specs, scratch=(), flops=0, moved=0, prefetch=1, room=40):
    return pl.pallas_call(
        kernel,
        out_shape=out_shape,
        grid_spec=pltpu.PrefetchScalarGridSpec(
            num_scalar_prefetch=prefetch,
            grid=grid,
            in_specs=in_specs,
            out_specs=out_specs,
            scratch_shapes=list(scratch),
        ),
        compiler_params=pltpu.CompilerParams(vmem_limit_bytes=room * MIB),
        cost_estimate=pl.CostEstimate(flops=flops, bytes_accessed=moved, transcendentals=0),
    )


def whole(shape):
    return pl.BlockSpec(shape, lambda i, *s: (0,) * len(shape))


def iota(shape, axis):
    return lax.broadcasted_iota(jnp.int32, shape, axis)


def aligned(index, unit=ALIGN):
    return pl.multiple_of(index, unit)


def swap(x, axis, bit):
    size = lax.axis_size(axis)
    return lax.ppermute(x, axis, [(i, i ^ bit) for i in range(size)])


def share(columns, groups):
    return -(-columns // (groups * ALIGN)) * ALIGN


class Layout:
    def __init__(self, groups, blocks, npair):
        self.groups, self.blocks, self.npair = groups, blocks, npair
        count = groups * blocks
        self.mine, self.own = 1, 2
        self.width_at, self.width, self.slot, self.cap_at, self.cap, self.small = 3, 4, 5, 6, 7, 8
        self.off = HEAD
        self.first = self.off + count
        self.owner = self.first + count
        self.into = self.owner + count
        self.pair = self.into + count
        self.rank = self.pair + count
        self.pair_into = self.rank + count
        self.pair_rank = self.pair_into + npair
        self.size = self.pair_rank + npair


def plan_kernel(lay, ids, ranks, where_ref, plan):
    groups, blocks, npair = lay.groups, lay.blocks, lay.npair
    per = npair // groups
    me = where_ref[0]
    for k in range(3):
        plan[k] = where_ref[k]

    def clear(p, carry):
        plan[lay.pair_rank + p] = 0
        return carry

    lax.fori_loop(0, npair, clear, 0)

    def group(g, widest):
        total = jnp.int32(0)
        pairs = [ids[(g ^ me) * blocks + b] for b in range(blocks)]
        places = []
        for b in range(blocks):
            i = g * blocks + b
            pair = pairs[b]
            rank = ranks[pair]
            plan[lay.pair_rank + pair] = rank
            place, new = total, rank
            for a in range(b):
                same = pairs[a] == pair
                place = jnp.where(same, places[a], place)
                new = jnp.where(same, 0, new)
            places.append(place)
            plan[lay.off + i] = place
            plan[lay.first + i] = new
            plan[lay.pair + i] = pair
            plan[lay.rank + i] = rank
            total = total + new
        return jnp.maximum(widest, total)

    widest = lax.fori_loop(0, groups, group, jnp.int32(0))

    def owner(o, fullest):
        total = jnp.int32(0)
        for k in range(per):
            p = o * per + k
            plan[lay.pair_into + p] = total
            total = total + plan[lay.pair_rank + p]
        return jnp.maximum(fullest, total)

    fullest = lax.fori_loop(0, groups, owner, jnp.int32(0))

    def block(i, carry):
        pair = plan[lay.pair + i]
        plan[lay.owner + i] = lax.div(pair, jnp.int32(per))
        plan[lay.into + i] = plan[lay.pair_into + pair]
        return carry

    lax.fori_loop(0, groups * blocks, block, 0)
    for need, sizes, at in ((widest, WIDTHS, lay.width_at), (fullest, CAPS, lay.cap_at)):
        values = [(k, size, share(size, groups)) for k, size in enumerate(sizes)]
        chosen = [jnp.int32(v) for v in values[-1]]
        for k, size, rows in reversed(values[:-1]):
            fits = need <= size
            chosen = [jnp.where(fits, v, c) for v, c in zip((k, size, rows), chosen)]
        for k in range(3):
            plan[at + k] = chosen[k]


def make_plan(lay, ids, ranks, where):
    smem = pl.BlockSpec(memory_space=pltpu.SMEM)
    return pl.pallas_call(
        functools.partial(plan_kernel, lay),
        out_shape=jax.ShapeDtypeStruct((lay.size,), jnp.int32),
        in_specs=[smem] * 3,
        out_specs=smem,
        compiler_params=pltpu.CompilerParams(vmem_limit_bytes=4 * MIB),
    )(ids, ranks, where)


def rank_kernel(blocks, where_ref, ids, cot, up, x, down, x_near, cot_near, kept, sent, ups, downs, sems):
    length, half, rmax = x.shape[0] // blocks, blocks // 2, ups.shape[1]
    own = where_ref[2]
    piece = length // 2
    waits = []
    for k in range(blocks):
        b = k ^ own
        pair = ids[b]
        pairs = [(down.at[pair], downs.at[k]), (up.at[pair], ups.at[k])]
        rows = pl.ds(aligned(b * length, length), length)
        pairs.append((cot.at[rows], cot_near.at[rows]))
        for h in range(2):
            rows = pl.ds(aligned(b * length + h * piece, piece), piece)
            pairs.append((x.at[rows], x_near.at[rows]))
        copies = [pltpu.make_async_copy(*pair, sems.at[k, n]) for n, pair in enumerate(pairs)]
        for copy in copies:
            copy.start()
        waits.append(copies)
    for k in range(blocks):
        for copy in waits[k]:
            copy.wait()
        rows = pl.ds(aligned((k ^ own) * length, length), length)
        out = kept if k < half else sent
        lines = slice(k % half * length, (k % half + 1) * length)
        back = lax.dot_general(cot_near[rows, :], ups[k], NT, preferred_element_type=jnp.float32)
        out[lines, :rmax] = back.astype(out.dtype)
        low = jnp.dot(x_near[rows, :], downs[k], preferred_element_type=jnp.float32)
        out[lines, rmax:] = low.astype(out.dtype)


def rank_sums(where, ids, cotangent, adapter_up, tokens, adapter_down):
    rows, width = cotangent.shape
    features = tokens.shape[1]
    blocks, rmax = ids.shape[0], adapter_up.shape[1]
    smem, far, near = (pl.BlockSpec(memory_space=kind) for kind in (pltpu.SMEM, pltpu.HBM, pltpu.VMEM))
    shape = (rows // 2, 2 * rmax)
    return pl.pallas_call(
        functools.partial(rank_kernel, blocks),
        out_shape=[pltpu.VMEM(v.shape, v.dtype) for v in (tokens, cotangent)]
        + [jax.ShapeDtypeStruct(shape, jnp.bfloat16)] * 2,
        in_specs=[smem] * 2 + [far] * 4,
        out_specs=[near] * 4,
        scratch_shapes=[
            pltpu.VMEM((blocks, rmax, width), jnp.bfloat16),
            pltpu.VMEM((blocks, features, rmax), jnp.bfloat16),
            pltpu.SemaphoreType.DMA((blocks, 5)),
        ],
        compiler_params=pltpu.CompilerParams(vmem_limit_bytes=50 * MIB),
        cost_estimate=pl.CostEstimate(
            flops=2 * rows * (width + features) * rmax,
            bytes_accessed=2 * rows * (width + features + 2 * rmax),
            transcendentals=0,
        ),
    )(where, ids, cotangent, adapter_up, tokens, adapter_down)


def add(a, b):
    return (a.astype(jnp.float32) + b.astype(jnp.float32)).astype(a.dtype)


def turn(rank, value):
    shape = (value.shape[1], value.shape[1])
    eye = jnp.logical_and(iota(shape, 0) == iota(shape, 1), iota(shape, 0) < rank).astype(jnp.bfloat16)
    return lax.dot_general(eye, value, NT, preferred_element_type=jnp.float32).astype(jnp.bfloat16)


def terms_kernel(lay, norm, plan, x, cot, own_sums, other_sums, out, total, turned, moved):
    groups, blocks = lay.groups, lay.blocks
    half = blocks // 2
    step = pl.program_id(0)
    length, rmax, part = turned.shape[2], turned.shape[1], out.shape[2]
    most, room = WIDTHS[-1], share(WIDTHS[-1], groups)
    pieces = out.shape[0]
    me, own = plan[0], plan[lay.own]
    width, slot = plan[lay.width], plan[lay.slot]

    def place(k, columns):
        i = me * blocks + (k ^ own)
        factor = 32.0 / jnp.full((1, columns), plan[lay.rank + i], jnp.int32).astype(jnp.float32) * norm
        return pl.ds(aligned(plan[lay.off + i]), rmax), factor

    @pl.when(step == 0)
    def _():
        total[:, :part] = jnp.zeros((total.shape[0], part), total.dtype)
        for k in range(blocks):
            b = k ^ own
            rank = plan[lay.rank + me * blocks + b]
            source = own_sums if k < half else other_sums
            lines = slice(k % half * length, (k % half + 1) * length)
            turned[k] = turn(rank, source[lines, :rmax])
            low = turn(rank, source[lines, rmax:])
            rows, factor = place(k, part)
            block = cot[pl.ds(aligned(b * length, length), length), :]
            total[rows, :part] += factor * jnp.dot(low, block, preferred_element_type=jnp.float32)
        column = iota((groups * room, most), 1)
        target = (column % groups) * slot + column // groups
        pick = (iota((groups * room, most), 0) == target).astype(jnp.bfloat16)
        up = total[:most, :part].astype(jnp.bfloat16)
        moved[...] = jnp.dot(pick, up, preferred_element_type=jnp.float32).astype(jnp.bfloat16)

    total[...] = jnp.zeros_like(total)
    for k in range(blocks):
        rows, factor = place(k, pieces * part)
        block = x[pl.ds(aligned((k ^ own) * length, length), length), :]
        total[rows, :] += factor * jnp.dot(turned[k], block, preferred_element_type=jnp.float32)
    for p in range(pieces):
        out[p, :most, :] = total[:most, p * part : (p + 1) * part].astype(jnp.bfloat16)
        out[p, pl.ds(aligned(width), room), :] = moved[pl.ds(aligned((step * pieces + p) * slot), room), :]


def group_terms(lay, norm, plan, tokens, cotangent, sums):
    rows, features = tokens.shape
    part = cotangent.shape[1]
    rmax = sums[0].shape[1] // 2
    most, room = WIDTHS[-1], share(WIDTHS[-1], lay.groups)
    pieces = 2
    shape = (lay.groups, most + room, part)
    return call(
        functools.partial(terms_kernel, lay, norm),
        pltpu.VMEM(shape, jnp.bfloat16),
        (lay.groups // pieces,),
        [pl.BlockSpec((rows, pieces * part), lambda i, plan: (0, i)), whole(cotangent.shape)]
        + [whole(v.shape) for v in sums],
        pl.BlockSpec((pieces,) + shape[1:], lambda i, plan: (i, 0, 0)),
        [
            pltpu.VMEM((most + rmax, pieces * part), jnp.float32),
            pltpu.VMEM((lay.blocks, rmax, rows // lay.blocks), jnp.bfloat16),
            pltpu.VMEM((lay.groups * room, part), jnp.bfloat16),
        ],
        flops=2 * rows * (features + part) * rmax,
        moved=2 * features * (rows + most),
        room=24,
    )(plan, tokens, cotangent, *sums)


def grad_kernel(lay, tiles, parts, plan, *refs):
    cots, (weight, down, backs, backo, out, cat) = refs[:parts], refs[parts:]
    step = pl.program_id(0)
    half = lay.blocks * tiles // 2
    block = lax.div(step, jnp.int32(tiles)) ^ plan[lay.own]
    mine = plan[lay.mine]
    width = cots[0].shape[1]
    for s, cot in enumerate(cots):
        cat[:, pl.ds(aligned((mine ^ s) * width, width), width)] = cot[...]
    rank = plan[lay.rank + plan[0] * lay.blocks + block]
    back = jnp.where(step < half, backs[...], backo[...])
    rows = jnp.where(iota(back.shape, 1) < rank, back, jnp.zeros_like(back))
    chunk = 512
    scale = 32.0 / jnp.full((1, chunk), rank, jnp.int32).astype(jnp.float32)

    def columns(c, carry):
        here = pl.ds(aligned(c * chunk, chunk), chunk)
        base = lax.dot_general(cat[...], weight[here, :], NT, preferred_element_type=jnp.float32)
        extra = lax.dot_general(rows, down[0, here, :], NT, preferred_element_type=jnp.float32)
        out[:, here] = (base + scale * extra).astype(out.dtype)
        return carry

    lax.fori_loop(0, out.shape[1] // chunk, columns, 0)


def input_gradient(lay, plan, cots, weight, adapter_down, sums):
    rows, width = cots[0].shape
    features, values = weight.shape
    blocks = lay.blocks
    tile = rows // blocks
    tiles = 1
    half = blocks * tiles // 2
    rmax = sums[0].shape[1] // 2
    here = lambda i, plan: (i ^ (plan[lay.own] * tiles), 0)

    def adapter(i, plan):
        block = lax.div(i, jnp.int32(tiles)) ^ plan[lay.own]
        return (plan[lay.pair + plan[0] * blocks + block], 0, 0)

    return call(
        functools.partial(grad_kernel, lay, tiles, len(cots)),
        jax.ShapeDtypeStruct((rows, features), jnp.bfloat16),
        (rows // tile,),
        [pl.BlockSpec((tile, width), here)] * len(cots)
        + [
            whole(weight.shape),
            pl.BlockSpec((1, features, rmax), adapter),
            pl.BlockSpec((tile, rmax), lambda i, plan: (jnp.minimum(i, half - 1), 0)),
            pl.BlockSpec((tile, rmax), lambda i, plan: (jnp.maximum(i - half, 0), 0)),
        ],
        pl.BlockSpec((tile, features), here),
        [pltpu.VMEM((tile, values), jnp.bfloat16)],
        flops=2 * rows * features * (values + rmax),
        moved=2 * features * (rows + values),
        room=32,
    )(plan, *cots, weight, adapter_down, *sums)


def reduce_kernel(lay, plan, parts, out, total, cat):
    groups, blocks = lay.groups, lay.blocks
    room, space = share(WIDTHS[-1], groups), share(CAPS[-1], groups)
    width, slot, cap, small = plan[lay.width], plan[lay.slot], plan[lay.cap], plan[lay.small]
    chunk = 128

    def clear(c, carry):
        total[pl.ds(aligned(c * chunk, chunk), chunk), :] = jnp.zeros((chunk, total.shape[1]), total.dtype)
        return carry

    lax.fori_loop(0, lax.div(groups * cap + chunk - 1, jnp.int32(chunk)), clear, 0)
    place = iota((1, groups * room), 1)
    target = jnp.full((1, groups * room), -1, jnp.int32)
    for g in range(groups):
        held = parts[g, pl.ds(aligned(width), room), :]
        cat[g * room : (g + 1) * room, :] = jnp.where(iota(held.shape, 0) < slot, held, jnp.zeros_like(held))
        for b in range(blocks):
            i = g * blocks + b
            rank, source = plan[lay.first + i], plan[lay.off + i]
            owner, into = plan[lay.owner + i], plan[lay.into + i]
            goal = owner * cap + into
            for size in SIZES:

                @pl.when(rank == size)
                def _(g=g, source=source, goal=goal, size=size):
                    here = pl.ds(aligned(source), size)
                    total[pl.ds(aligned(goal), size), :] += parts[g, here, :].astype(jnp.float32)

            start = g * room + lax.div(source, jnp.int32(groups))
            inside = jnp.logical_and(place >= start, place < start + lax.div(rank, jnp.int32(groups)))
            shift = owner * small + lax.div(into, jnp.int32(groups)) - start
            target = jnp.where(inside, place + shift, target)
    line = iota((space, groups * room), 0)

    def owner_rows(o, carry):
        def copy(c, carry):
            here = pl.ds(aligned(c * chunk, chunk), chunk)
            out[o, here, :] = total[pl.ds(aligned(o * cap + c * chunk), chunk), :].astype(out.dtype)
            return carry

        lax.fori_loop(0, lax.div(cap + chunk - 1, jnp.int32(chunk)), copy, 0)
        pick = (line + o * small == target).astype(jnp.bfloat16)
        rows = jnp.dot(pick, cat[...], preferred_element_type=jnp.float32).astype(out.dtype)
        out[o, pl.ds(aligned(cap), space), :] = rows
        return carry

    lax.fori_loop(0, groups, owner_rows, 0)


def reduce_terms(lay, rmax, plan, parts):
    part = parts.shape[2]
    groups, most = lay.groups, CAPS[-1]
    shape = (groups, most + rmax, part)
    return call(
        functools.partial(reduce_kernel, lay),
        pltpu.VMEM(shape, jnp.bfloat16),
        (1,),
        [whole(parts.shape)],
        whole(shape),
        [
            pltpu.VMEM((groups * most + 128, part), jnp.float32),
            pltpu.VMEM((groups * share(WIDTHS[-1], groups), part), jnp.bfloat16),
        ],
        flops=2 * most * WIDTHS[-1] * part,
        moved=4 * groups * most * part,
        room=30,
    )(plan, parts)


def unpack_kernel(lay, plan, slots, down, up, cat):
    groups = lay.groups
    per = lay.npair // groups
    me, cap = plan[0], plan[lay.cap]
    part, rmax, space = slots.shape[2], down.shape[2], share(CAPS[-1], groups)
    eye = (iota((part, part), 0) == iota((part, part), 1)).astype(jnp.bfloat16)
    for s in range(groups):
        held = slots[s, pl.ds(aligned(cap), space), :]
        cat[s * space : (s + 1) * space, :] = jnp.where(iota(held.shape, 0) < plan[lay.small], held, jnp.zeros_like(held))
    shape = (rmax, groups * space)
    r, column = iota(shape, 0), iota(shape, 1)
    place = (r % groups) * space + r // groups
    for k in range(per):
        start, rank = plan[lay.pair_into + me * per + k], plan[lay.pair_rank + me * per + k]

        @pl.when(rank > 0)
        def _(k=k, start=start, rank=rank):
            for s in range(groups):
                rows = slots[s, pl.ds(aligned(start), rmax), :]
                rows = jnp.where(iota(rows.shape, 0) < rank, rows, jnp.zeros_like(rows))
                value = lax.dot_general(eye, rows, NT, preferred_element_type=jnp.float32)
                down[k, s * part : (s + 1) * part, :] = value.astype(down.dtype)
            match = column == place + lax.div(start, jnp.int32(groups))
            pick = jnp.logical_and(match, r < rank).astype(jnp.bfloat16)
            up[k] = jnp.dot(pick, cat[...], preferred_element_type=jnp.float32).astype(up.dtype)

        @pl.when(rank == 0)
        def _(k=k):
            down[k] = jnp.zeros_like(down[k])
            up[k] = jnp.zeros_like(up[k])


def unpack(lay, plan, slots, features, rmax):
    part = slots.shape[2]
    per = lay.npair // lay.groups
    shapes = [(per, features, rmax), (per, rmax, part)]
    return call(
        functools.partial(unpack_kernel, lay),
        [jax.ShapeDtypeStruct(shape, jnp.bfloat16) for shape in shapes],
        (1,),
        [whole(slots.shape)],
        [whole(shape) for shape in shapes],
        [pltpu.VMEM((lay.groups * share(CAPS[-1], lay.groups), part), jnp.bfloat16)],
        flops=2 * per * features * rmax * part,
        moved=2 * per * features * rmax,
        room=20,
    )(plan, slots)


def far_parts(x, axis):
    size = lax.axis_size(axis)
    parts = {0: x}
    bit = size // 2
    while bit > 1:
        for k in sorted(parts):
            parts[k ^ bit] = swap(parts[k], axis, bit)
        bit //= 2
    return [parts[k] for k in sorted(parts) if k], swap(x, axis, 1)


def all_parts(x, far, near, axis):
    out = [x, near]
    for part in far:
        out += [part, swap(part, axis, 1)]
    return out


def move_kernel(rows, source, out, *scratch):
    groups = source.shape[0]
    steps = [source, *scratch[: len(scratch) - 1], out]
    sems = scratch[-1]
    copies = [
        [
            pltpu.make_async_copy(a.at[g, pl.ds(0, rows)], b.at[g, pl.ds(0, rows)], sems.at[hop, g])
            for g in range(groups)
        ]
        for hop, (a, b) in enumerate(zip(steps, steps[1:]))
    ]
    for copy in copies[0]:
        copy.start()
    for hop, batch in enumerate(copies):
        for g, copy in enumerate(batch):
            copy.wait()
            if hop + 1 < len(copies):
                copies[hop + 1][g].start()


def move(source, rows, size, kind, through):
    groups, _, part = source.shape
    scratch = [pltpu.VMEM((groups, rows, part), source.dtype)] if through else []
    return pl.pallas_call(
        functools.partial(move_kernel, rows),
        out_shape=kind((groups, size, part), source.dtype),
        in_specs=[pl.BlockSpec(memory_space=pl.ANY)],
        out_specs=pl.BlockSpec(memory_space=pl.ANY),
        scratch_shapes=scratch + [pltpu.SemaphoreType.DMA((1 + len(scratch), groups))],
        compiler_params=pltpu.CompilerParams(vmem_limit_bytes=12 * MIB),
    )(source)


def spread(rows, parts, through):
    sent = move(parts, rows, rows, pltpu.HBM, through)
    sent = lax.all_to_all(sent, "pair", split_axis=0, concat_axis=0, tiled=True)
    return move(sent, rows, parts.shape[1], pltpu.VMEM, False)


def first_exchange(rows, terms, cotangent):
    return spread(rows, terms, False), *far_parts(cotangent, "fsdp")


def second_exchange(lay, rows, plan, sums, cotangent, far, near, weight, adapter_down, ranked):
    cots = all_parts(cotangent, far, near, "fsdp")
    return spread(rows, sums, False), input_gradient(lay, plan, cots, weight, adapter_down, ranked)


def per_device(tokens, cotangent, value_weight, adapter_down, adapter_up, pair_ids, ranks):
    rows = tokens.shape[0]
    blocks = pair_ids.shape[0]
    groups, shares = lax.axis_size("pair"), lax.axis_size("fsdp")
    lay = Layout(groups, blocks, adapter_down.shape[0])
    norm = 1.0 / math.sqrt(rows * groups)
    me, mine = lax.axis_index("pair"), lax.axis_index("fsdp")
    where = jnp.stack([me, mine, (mine & 1) * (blocks // 2)]).astype(jnp.int32)
    ids = jnp.concatenate([pair_ids, swap(pair_ids, "pair", 1)])
    near_tokens, near_cot, kept, sent = rank_sums(where, pair_ids, cotangent, adapter_up, tokens, adapter_down)
    ids, sent = lax.optimization_barrier((ids, sent))
    sums = add(kept, swap(sent, "fsdp", 1))
    if groups > 2:
        ids = jnp.concatenate([ids, swap(ids, "pair", 2)])
    sums, ids = lax.optimization_barrier((sums, ids))
    bit = 4
    while bit < groups:
        ids = jnp.concatenate([ids, swap(ids, "pair", bit)])
        bit *= 2
    plan = make_plan(lay, ids, ranks, where)
    bit = 2
    while bit < shares:
        theirs = swap(sums, "fsdp", bit)
        theirs, plan = lax.optimization_barrier((theirs, plan))
        sums = add(sums, theirs)
        bit *= 2
    sums = (sums, swap(sums, "fsdp", 1))
    terms = group_terms(lay, norm, plan, near_tokens, near_cot, sums)
    branches = [functools.partial(first_exchange, size + share(size, groups)) for size in WIDTHS]
    received, far, near = lax.switch(plan[lay.width_at], branches, terms, cotangent)
    reduced = reduce_terms(lay, adapter_down.shape[2], plan, received)
    branches = [functools.partial(second_exchange, lay, size + share(size, groups)) for size in CAPS]
    slots, input_grad = lax.switch(
        plan[lay.cap_at], branches, plan, reduced, cotangent, far, near, value_weight, adapter_down, sums
    )
    down_grad, up_grad = unpack(lay, plan, slots, tokens.shape[1], adapter_down.shape[2])
    return input_grad, down_grad, up_grad


def dense_per_device(tokens, cotangent, value_weight, adapter_down, adapter_up, pair_ids, ranks):
    rows, features = tokens.shape
    blocks = pair_ids.shape[0]
    length = rows // blocks
    npair, _, rmax = adapter_down.shape
    norm = 1.0 / math.sqrt(rows * lax.axis_size("pair"))
    mask = (jnp.arange(rmax, dtype=jnp.int32)[None, :] < ranks[:, None]).astype(jnp.float32)
    scale = 32.0 / ranks.astype(jnp.float32)
    x = tokens.reshape(blocks, length, features)
    c = cotangent.reshape(blocks, length, cotangent.shape[1])
    down, up = adapter_down[pair_ids], adapter_up[pair_ids]
    wide = {"preferred_element_type": jnp.float32}
    low = lax.psum(jnp.einsum("btd,bdr->btr", x, down, **wide).astype(jnp.bfloat16), "fsdp")
    back = lax.psum(jnp.einsum("btk,brk->btr", c, up, **wide).astype(jnp.bfloat16), "fsdp")
    rows_mask = mask[pair_ids][:, None, :]
    low = (low.astype(jnp.float32) * rows_mask).astype(jnp.bfloat16)
    back = (back.astype(jnp.float32) * rows_mask).astype(jnp.bfloat16)
    cots = lax.all_gather(cotangent, "fsdp", axis=1, tiled=True)
    base = jnp.einsum("tk,dk->td", cots, value_weight, **wide).reshape(blocks, length, features)
    factor = scale[pair_ids][:, None, None]
    input_grad = (base + factor * jnp.einsum("btr,bdr->btd", back, down, **wide)).astype(jnp.bfloat16)
    term_a = jnp.einsum("btd,btr->bdr", x, back, **wide) * (factor * norm)
    term_b = jnp.einsum("btr,btk->brk", low, c, **wide) * (factor * norm)
    onehot = (pair_ids[:, None] == jnp.arange(npair, dtype=jnp.int32)[None, :]).astype(jnp.float32)
    grads = [
        lax.psum_scatter(
            jnp.einsum("bp,bij->pij", onehot, term).astype(jnp.bfloat16), "pair", scatter_dimension=0, tiled=True
        )
        for term in (term_a, term_b)
    ]
    return input_grad.reshape(rows, features), grads[0], grads[1]


def per_shape(tokens, cotangent, value_weight, adapter_down, adapter_up, pair_ids, ranks):
    groups, shares = lax.axis_size("pair"), lax.axis_size("fsdp")
    blocks = pair_ids.shape[0]
    part = tokens.shape[1] // groups
    power = lambda v: v & (v - 1) == 0
    fits = (
        part % 128 == 0
        and part == cotangent.shape[1]
        and power(groups)
        and power(shares)
        and power(blocks)
        and min(shares, blocks) > 1
        and groups <= 8
        and WIDTHS[-1] >= blocks * adapter_down.shape[2]
        and CAPS[-1] >= adapter_down.shape[0] // groups * adapter_down.shape[2]
    )
    form = per_device if fits else dense_per_device
    return form(tokens, cotangent, value_weight, adapter_down, adapter_up, pair_ids, ranks)


def solution(mesh):
    placed = (
        P("pair", "fsdp"),
        P("pair", "fsdp"),
        P("fsdp", None),
        P(None, "fsdp", None),
        P(None, None, "fsdp"),
        P("pair"),
        P(),
    )
    return jax.shard_map(
        per_shape,
        mesh=mesh,
        in_specs=placed,
        out_specs=(P("pair", "fsdp"), P("pair", "fsdp", None), P("pair", None, "fsdp")),
        check_vma=False,
    )
```

```python
import functools
import math

import jax
import jax.numpy as jnp
from jax import lax
from jax.experimental import pallas as pl
from jax.experimental.pallas import tpu as pltpu
from jax.sharding import PartitionSpec as P

WIDTHS = (224, 256, 288, 320, 352, 384, 416, 448, 512)
CAPS = (160, 192, 224, 256, 288, 320, 352, 384, 448, 768)
ALIGN = 16
HEAD = 16
NT = (((1,), (1,)), ((), ()))
MIB = 1024 * 1024
SIZES = (128, 64, 32, 16)


def call(kernel, out_shape, grid, in_specs, out_specs, scratch=(), flops=0, moved=0, prefetch=1, room=40):
    return pl.pallas_call(
        kernel,
        out_shape=out_shape,
        grid_spec=pltpu.PrefetchScalarGridSpec(
            num_scalar_prefetch=prefetch,
            grid=grid,
            in_specs=in_specs,
            out_specs=out_specs,
            scratch_shapes=list(scratch),
        ),
        compiler_params=pltpu.CompilerParams(vmem_limit_bytes=room * MIB),
        cost_estimate=pl.CostEstimate(flops=flops, bytes_accessed=moved, transcendentals=0),
    )


def whole(shape):
    return pl.BlockSpec(shape, lambda i, *s: (0,) * len(shape))


def iota(shape, axis):
    return lax.broadcasted_iota(jnp.int32, shape, axis)


def aligned(index, unit=ALIGN):
    return pl.multiple_of(index, unit)


def swap(x, axis, bit):
    size = lax.axis_size(axis)
    return lax.ppermute(x, axis, [(i, i ^ bit) for i in range(size)])


def share(columns, groups):
    return -(-columns // (groups * ALIGN)) * ALIGN


class Layout:
    def __init__(self, groups, blocks, npair):
        self.groups, self.blocks, self.npair = groups, blocks, npair
        count = groups * blocks
        self.mine, self.own = 1, 2
        self.width_at, self.width, self.slot, self.cap_at, self.cap, self.small = 3, 4, 5, 6, 7, 8
        self.off = HEAD
        self.first = self.off + count
        self.owner = self.first + count
        self.into = self.owner + count
        self.pair = self.into + count
        self.rank = self.pair + count
        self.pair_into = self.rank + count
        self.pair_rank = self.pair_into + npair
        self.size = self.pair_rank + npair


def plan_kernel(lay, ids, ranks, where_ref, plan):
    groups, blocks, npair = lay.groups, lay.blocks, lay.npair
    per = npair // groups
    me = where_ref[0]
    for k in range(3):
        plan[k] = where_ref[k]

    def clear(p, carry):
        plan[lay.pair_rank + p] = 0
        return carry

    lax.fori_loop(0, npair, clear, 0)

    def group(g, widest):
        total = jnp.int32(0)
        pairs = [ids[(g ^ me) * blocks + b] for b in range(blocks)]
        places = []
        for b in range(blocks):
            i = g * blocks + b
            pair = pairs[b]
            rank = ranks[pair]
            plan[lay.pair_rank + pair] = rank
            place, new = total, rank
            for a in range(b):
                same = pairs[a] == pair
                place = jnp.where(same, places[a], place)
                new = jnp.where(same, 0, new)
            places.append(place)
            plan[lay.off + i] = place
            plan[lay.first + i] = new
            plan[lay.pair + i] = pair
            plan[lay.rank + i] = rank
            total = total + new
        return jnp.maximum(widest, total)

    widest = lax.fori_loop(0, groups, group, jnp.int32(0))

    def owner(o, fullest):
        total = jnp.int32(0)
        for k in range(per):
            p = o * per + k
            plan[lay.pair_into + p] = total
            total = total + plan[lay.pair_rank + p]
        return jnp.maximum(fullest, total)

    fullest = lax.fori_loop(0, groups, owner, jnp.int32(0))

    def block(i, carry):
        pair = plan[lay.pair + i]
        plan[lay.owner + i] = lax.div(pair, jnp.int32(per))
        plan[lay.into + i] = plan[lay.pair_into + pair]
        return carry

    lax.fori_loop(0, groups * blocks, block, 0)
    for need, sizes, at in ((widest, WIDTHS, lay.width_at), (fullest, CAPS, lay.cap_at)):
        values = [(k, size, share(size, groups)) for k, size in enumerate(sizes)]
        chosen = [jnp.int32(v) for v in values[-1]]
        for k, size, rows in reversed(values[:-1]):
            fits = need <= size
            chosen = [jnp.where(fits, v, c) for v, c in zip((k, size, rows), chosen)]
        for k in range(3):
            plan[at + k] = chosen[k]


def make_plan(lay, ids, ranks, where):
    smem = pl.BlockSpec(memory_space=pltpu.SMEM)
    return pl.pallas_call(
        functools.partial(plan_kernel, lay),
        out_shape=jax.ShapeDtypeStruct((lay.size,), jnp.int32),
        in_specs=[smem] * 3,
        out_specs=smem,
        compiler_params=pltpu.CompilerParams(vmem_limit_bytes=4 * MIB),
    )(ids, ranks, where)


def rank_kernel(blocks, where_ref, ids, cot, up, x, down, x_near, cot_near, kept, sent, ups, downs, sems):
    length, half, rmax = x.shape[0] // blocks, blocks // 2, ups.shape[1]
    own = where_ref[2]
    piece = length // 2
    waits = []
    for k in range(blocks):
        b = k ^ own
        pair = ids[b]
        pairs = [(down.at[pair], downs.at[k]), (up.at[pair], ups.at[k])]
        rows = pl.ds(aligned(b * length, length), length)
        pairs.append((cot.at[rows], cot_near.at[rows]))
        for h in range(2):
            rows = pl.ds(aligned(b * length + h * piece, piece), piece)
            pairs.append((x.at[rows], x_near.at[rows]))
        copies = [pltpu.make_async_copy(*pair, sems.at[k, n]) for n, pair in enumerate(pairs)]
        for copy in copies:
            copy.start()
        waits.append(copies)
    for k in range(blocks):
        for copy in waits[k]:
            copy.wait()
        rows = pl.ds(aligned((k ^ own) * length, length), length)
        out = kept if k < half else sent
        lines = slice(k % half * length, (k % half + 1) * length)
        back = lax.dot_general(cot_near[rows, :], ups[k], NT, preferred_element_type=jnp.float32)
        out[lines, :rmax] = back.astype(out.dtype)
        low = jnp.dot(x_near[rows, :], downs[k], preferred_element_type=jnp.float32)
        out[lines, rmax:] = low.astype(out.dtype)


def rank_sums(where, ids, cotangent, adapter_up, tokens, adapter_down):
    rows, width = cotangent.shape
    features = tokens.shape[1]
    blocks, rmax = ids.shape[0], adapter_up.shape[1]
    smem, far, near = (pl.BlockSpec(memory_space=kind) for kind in (pltpu.SMEM, pltpu.HBM, pltpu.VMEM))
    shape = (rows // 2, 2 * rmax)
    return pl.pallas_call(
        functools.partial(rank_kernel, blocks),
        out_shape=[pltpu.VMEM(v.shape, v.dtype) for v in (tokens, cotangent)]
        + [jax.ShapeDtypeStruct(shape, jnp.bfloat16)] * 2,
        in_specs=[smem] * 2 + [far] * 4,
        out_specs=[near] * 4,
        scratch_shapes=[
            pltpu.VMEM((blocks, rmax, width), jnp.bfloat16),
            pltpu.VMEM((blocks, features, rmax), jnp.bfloat16),
            pltpu.SemaphoreType.DMA((blocks, 5)),
        ],
        compiler_params=pltpu.CompilerParams(vmem_limit_bytes=50 * MIB),
        cost_estimate=pl.CostEstimate(
            flops=2 * rows * (width + features) * rmax,
            bytes_accessed=2 * rows * (width + features + 2 * rmax),
            transcendentals=0,
        ),
    )(where, ids, cotangent, adapter_up, tokens, adapter_down)


def add(a, b):
    return (a.astype(jnp.float32) + b.astype(jnp.float32)).astype(a.dtype)


def turn(rank, value):
    shape = (value.shape[1], value.shape[1])
    eye = jnp.logical_and(iota(shape, 0) == iota(shape, 1), iota(shape, 0) < rank).astype(jnp.bfloat16)
    return lax.dot_general(eye, value, NT, preferred_element_type=jnp.float32).astype(jnp.bfloat16)


def terms_kernel(lay, norm, plan, x, cot, own_sums, other_sums, out, total, turned, moved):
    groups, blocks = lay.groups, lay.blocks
    half = blocks // 2
    step = pl.program_id(0)
    length, rmax, part = turned.shape[2], turned.shape[1], out.shape[2]
    most, room = WIDTHS[-1], share(WIDTHS[-1], groups)
    pieces = out.shape[0]
    me, own = plan[0], plan[lay.own]
    width, slot = plan[lay.width], plan[lay.slot]

    def place(k, columns):
        i = me * blocks + (k ^ own)
        factor = 32.0 / jnp.full((1, columns), plan[lay.rank + i], jnp.int32).astype(jnp.float32) * norm
        return pl.ds(aligned(plan[lay.off + i]), rmax), factor

    @pl.when(step == 0)
    def _():
        total[:, :part] = jnp.zeros((total.shape[0], part), total.dtype)
        for k in range(blocks):
            b = k ^ own
            rank = plan[lay.rank + me * blocks + b]
            source = own_sums if k < half else other_sums
            lines = slice(k % half * length, (k % half + 1) * length)
            turned[k] = turn(rank, source[lines, :rmax])
            low = turn(rank, source[lines, rmax:])
            rows, factor = place(k, part)
            block = cot[pl.ds(aligned(b * length, length), length), :]
            total[rows, :part] += factor * jnp.dot(low, block, preferred_element_type=jnp.float32)
        column = iota((groups * room, most), 1)
        target = (column % groups) * slot + column // groups
        pick = (iota((groups * room, most), 0) == target).astype(jnp.bfloat16)
        up = total[:most, :part].astype(jnp.bfloat16)
        moved[...] = jnp.dot(pick, up, preferred_element_type=jnp.float32).astype(jnp.bfloat16)

    total[...] = jnp.zeros_like(total)
    for k in range(blocks):
        rows, factor = place(k, pieces * part)
        block = x[pl.ds(aligned((k ^ own) * length, length), length), :]
        total[rows, :] += factor * jnp.dot(turned[k], block, preferred_element_type=jnp.float32)
    for p in range(pieces):
        out[p, :most, :] = total[:most, p * part : (p + 1) * part].astype(jnp.bfloat16)
        out[p, pl.ds(aligned(width), room), :] = moved[pl.ds(aligned((step * pieces + p) * slot), room), :]


def group_terms(lay, norm, plan, tokens, cotangent, sums):
    rows, features = tokens.shape
    part = cotangent.shape[1]
    rmax = sums[0].shape[1] // 2
    most, room = WIDTHS[-1], share(WIDTHS[-1], lay.groups)
    pieces = 2
    shape = (lay.groups, most + room, part)
    return call(
        functools.partial(terms_kernel, lay, norm),
        pltpu.VMEM(shape, jnp.bfloat16),
        (lay.groups // pieces,),
        [pl.BlockSpec((rows, pieces * part), lambda i, plan: (0, i)), whole(cotangent.shape)]
        + [whole(v.shape) for v in sums],
        pl.BlockSpec((pieces,) + shape[1:], lambda i, plan: (i, 0, 0)),
        [
            pltpu.VMEM((most + rmax, pieces * part), jnp.float32),
            pltpu.VMEM((lay.blocks, rmax, rows // lay.blocks), jnp.bfloat16),
            pltpu.VMEM((lay.groups * room, part), jnp.bfloat16),
        ],
        flops=2 * rows * (features + part) * rmax,
        moved=2 * features * (rows + most),
        room=24,
    )(plan, tokens, cotangent, *sums)


def grad_kernel(lay, tiles, parts, plan, *refs):
    cots, (weight, down, backs, backo, out, cat) = refs[:parts], refs[parts:]
    step = pl.program_id(0)
    half = lay.blocks * tiles // 2
    block = lax.div(step, jnp.int32(tiles)) ^ plan[lay.own]
    mine = plan[lay.mine]
    width = cots[0].shape[1]
    for s, cot in enumerate(cots):
        cat[:, pl.ds(aligned((mine ^ s) * width, width), width)] = cot[...]
    rank = plan[lay.rank + plan[0] * lay.blocks + block]
    back = jnp.where(step < half, backs[...], backo[...])
    rows = jnp.where(iota(back.shape, 1) < rank, back, jnp.zeros_like(back))
    chunk = 512
    scale = 32.0 / jnp.full((1, chunk), rank, jnp.int32).astype(jnp.float32)

    def columns(c, carry):
        here = pl.ds(aligned(c * chunk, chunk), chunk)
        base = lax.dot_general(cat[...], weight[here, :], NT, preferred_element_type=jnp.float32)
        extra = lax.dot_general(rows, down[0, here, :], NT, preferred_element_type=jnp.float32)
        out[:, here] = (base + scale * extra).astype(out.dtype)
        return carry

    lax.fori_loop(0, out.shape[1] // chunk, columns, 0)


def input_gradient(lay, plan, cots, weight, adapter_down, sums):
    rows, width = cots[0].shape
    features, values = weight.shape
    blocks = lay.blocks
    tile = rows // blocks
    tiles = 1
    half = blocks * tiles // 2
    rmax = sums[0].shape[1] // 2
    here = lambda i, plan: (i ^ (plan[lay.own] * tiles), 0)

    def adapter(i, plan):
        block = lax.div(i, jnp.int32(tiles)) ^ plan[lay.own]
        return (plan[lay.pair + plan[0] * blocks + block], 0, 0)

    return call(
        functools.partial(grad_kernel, lay, tiles, len(cots)),
        jax.ShapeDtypeStruct((rows, features), jnp.bfloat16),
        (rows // tile,),
        [pl.BlockSpec((tile, width), here)] * len(cots)
        + [
            whole(weight.shape),
            pl.BlockSpec((1, features, rmax), adapter),
            pl.BlockSpec((tile, rmax), lambda i, plan: (jnp.minimum(i, half - 1), 0)),
            pl.BlockSpec((tile, rmax), lambda i, plan: (jnp.maximum(i - half, 0), 0)),
        ],
        pl.BlockSpec((tile, features), here),
        [pltpu.VMEM((tile, values), jnp.bfloat16)],
        flops=2 * rows * features * (values + rmax),
        moved=2 * features * (rows + values),
        room=32,
    )(plan, *cots, weight, adapter_down, *sums)


def reduce_kernel(lay, plan, parts, out, total, cat):
    groups, blocks = lay.groups, lay.blocks
    room, space = share(WIDTHS[-1], groups), share(CAPS[-1], groups)
    width, slot, cap, small = plan[lay.width], plan[lay.slot], plan[lay.cap], plan[lay.small]
    chunk = 128

    def clear(c, carry):
        total[pl.ds(aligned(c * chunk, chunk), chunk), :] = jnp.zeros((chunk, total.shape[1]), total.dtype)
        return carry

    lax.fori_loop(0, lax.div(groups * cap + chunk - 1, jnp.int32(chunk)), clear, 0)
    place = iota((1, groups * room), 1)
    target = jnp.full((1, groups * room), -1, jnp.int32)
    for g in range(groups):
        held = parts[g, pl.ds(aligned(width), room), :]
        cat[g * room : (g + 1) * room, :] = jnp.where(iota(held.shape, 0) < slot, held, jnp.zeros_like(held))
        for b in range(blocks):
            i = g * blocks + b
            rank, source = plan[lay.first + i], plan[lay.off + i]
            owner, into = plan[lay.owner + i], plan[lay.into + i]
            goal = owner * cap + into
            for size in SIZES:

                @pl.when(rank == size)
                def _(g=g, source=source, goal=goal, size=size):
                    here = pl.ds(aligned(source), size)
                    total[pl.ds(aligned(goal), size), :] += parts[g, here, :].astype(jnp.float32)

            start = g * room + lax.div(source, jnp.int32(groups))
            inside = jnp.logical_and(place >= start, place < start + lax.div(rank, jnp.int32(groups)))
            shift = owner * small + lax.div(into, jnp.int32(groups)) - start
            target = jnp.where(inside, place + shift, target)
    line = iota((space, groups * room), 0)

    def owner_rows(o, carry):
        def copy(c, carry):
            here = pl.ds(aligned(c * chunk, chunk), chunk)
            out[o, here, :] = total[pl.ds(aligned(o * cap + c * chunk), chunk), :].astype(out.dtype)
            return carry

        lax.fori_loop(0, lax.div(cap + chunk - 1, jnp.int32(chunk)), copy, 0)
        pick = (line + o * small == target).astype(jnp.bfloat16)
        rows = jnp.dot(pick, cat[...], preferred_element_type=jnp.float32).astype(out.dtype)
        out[o, pl.ds(aligned(cap), space), :] = rows
        return carry

    lax.fori_loop(0, groups, owner_rows, 0)


def reduce_terms(lay, rmax, plan, parts):
    part = parts.shape[2]
    groups, most = lay.groups, CAPS[-1]
    shape = (groups, most + rmax, part)
    return call(
        functools.partial(reduce_kernel, lay),
        pltpu.VMEM(shape, jnp.bfloat16),
        (1,),
        [whole(parts.shape)],
        whole(shape),
        [
            pltpu.VMEM((groups * most + 128, part), jnp.float32),
            pltpu.VMEM((groups * share(WIDTHS[-1], groups), part), jnp.bfloat16),
        ],
        flops=2 * most * WIDTHS[-1] * part,
        moved=4 * groups * most * part,
        room=30,
    )(plan, parts)


def unpack_kernel(lay, plan, slots, down, up, cat):
    groups = lay.groups
    per = lay.npair // groups
    me, cap = plan[0], plan[lay.cap]
    part, rmax, space = slots.shape[2], down.shape[2], share(CAPS[-1], groups)
    eye = (iota((part, part), 0) == iota((part, part), 1)).astype(jnp.bfloat16)
    for s in range(groups):
        held = slots[s, pl.ds(aligned(cap), space), :]
        cat[s * space : (s + 1) * space, :] = jnp.where(iota(held.shape, 0) < plan[lay.small], held, jnp.zeros_like(held))
    shape = (rmax, groups * space)
    r, column = iota(shape, 0), iota(shape, 1)
    place = (r % groups) * space + r // groups
    for k in range(per):
        start, rank = plan[lay.pair_into + me * per + k], plan[lay.pair_rank + me * per + k]

        @pl.when(rank > 0)
        def _(k=k, start=start, rank=rank):
            for s in range(groups):
                rows = slots[s, pl.ds(aligned(start), rmax), :]
                rows = jnp.where(iota(rows.shape, 0) < rank, rows, jnp.zeros_like(rows))
                value = lax.dot_general(eye, rows, NT, preferred_element_type=jnp.float32)
                down[k, s * part : (s + 1) * part, :] = value.astype(down.dtype)
            match = column == place + lax.div(start, jnp.int32(groups))
            pick = jnp.logical_and(match, r < rank).astype(jnp.bfloat16)
            up[k] = jnp.dot(pick, cat[...], preferred_element_type=jnp.float32).astype(up.dtype)

        @pl.when(rank == 0)
        def _(k=k):
            down[k] = jnp.zeros_like(down[k])
            up[k] = jnp.zeros_like(up[k])


def unpack(lay, plan, slots, features, rmax):
    part = slots.shape[2]
    per = lay.npair // lay.groups
    shapes = [(per, features, rmax), (per, rmax, part)]
    return call(
        functools.partial(unpack_kernel, lay),
        [jax.ShapeDtypeStruct(shape, jnp.bfloat16) for shape in shapes],
        (1,),
        [whole(slots.shape)],
        [whole(shape) for shape in shapes],
        [pltpu.VMEM((lay.groups * share(CAPS[-1], lay.groups), part), jnp.bfloat16)],
        flops=2 * per * features * rmax * part,
        moved=2 * per * features * rmax,
        room=20,
    )(plan, slots)


def far_parts(x, axis):
    size = lax.axis_size(axis)
    parts = {0: x}
    bit = size // 2
    while bit > 1:
        for k in sorted(parts):
            parts[k ^ bit] = swap(parts[k], axis, bit)
        bit //= 2
    return [parts[k] for k in sorted(parts) if k], swap(x, axis, 1)


def all_parts(x, far, near, axis):
    out = [x, near]
    for part in far:
        out += [part, swap(part, axis, 1)]
    return out


def move_kernel(rows, source, out, *scratch):
    groups = source.shape[0]
    steps = [source, *scratch[: len(scratch) - 1], out]
    sems = scratch[-1]
    copies = [
        [
            pltpu.make_async_copy(a.at[g, pl.ds(0, rows)], b.at[g, pl.ds(0, rows)], sems.at[hop, g])
            for g in range(groups)
        ]
        for hop, (a, b) in enumerate(zip(steps, steps[1:]))
    ]
    for copy in copies[0]:
        copy.start()
    for hop, batch in enumerate(copies):
        for g, copy in enumerate(batch):
            copy.wait()
            if hop + 1 < len(copies):
                copies[hop + 1][g].start()


def move(source, rows, size, kind, through):
    groups, _, part = source.shape
    scratch = [pltpu.VMEM((groups, rows, part), source.dtype)] if through else []
    return pl.pallas_call(
        functools.partial(move_kernel, rows),
        out_shape=kind((groups, size, part), source.dtype),
        in_specs=[pl.BlockSpec(memory_space=pl.ANY)],
        out_specs=pl.BlockSpec(memory_space=pl.ANY),
        scratch_shapes=scratch + [pltpu.SemaphoreType.DMA((1 + len(scratch), groups))],
        compiler_params=pltpu.CompilerParams(vmem_limit_bytes=12 * MIB),
    )(source)


def spread(rows, parts, through):
    sent = move(parts, rows, rows, pltpu.HBM, through)
    sent = lax.all_to_all(sent, "pair", split_axis=0, concat_axis=0, tiled=True)
    return move(sent, rows, parts.shape[1], pltpu.VMEM, False)


def first_exchange(rows, terms, cotangent):
    return spread(rows, terms, False), *far_parts(cotangent, "fsdp")


def second_exchange(lay, rows, plan, sums, cotangent, far, near, weight, adapter_down, ranked):
    cots = all_parts(cotangent, far, near, "fsdp")
    return spread(rows, sums, False), input_gradient(lay, plan, cots, weight, adapter_down, ranked)


def per_device(tokens, cotangent, value_weight, adapter_down, adapter_up, pair_ids, ranks):
    rows = tokens.shape[0]
    blocks = pair_ids.shape[0]
    groups, shares = lax.axis_size("pair"), lax.axis_size("fsdp")
    lay = Layout(groups, blocks, adapter_down.shape[0])
    norm = 1.0 / math.sqrt(rows * groups)
    me, mine = lax.axis_index("pair"), lax.axis_index("fsdp")
    where = jnp.stack([me, mine, (mine & 1) * (blocks // 2)]).astype(jnp.int32)
    ids = jnp.concatenate([pair_ids, swap(pair_ids, "pair", 1)])
    near_tokens, near_cot, kept, sent = rank_sums(where, pair_ids, cotangent, adapter_up, tokens, adapter_down)
    ids, sent = lax.optimization_barrier((ids, sent))
    sums = add(kept, swap(sent, "fsdp", 1))
    if groups > 2:
        ids = jnp.concatenate([ids, swap(ids, "pair", 2)])
    sums, ids = lax.optimization_barrier((sums, ids))
    bit = 4
    while bit < groups:
        ids = jnp.concatenate([ids, swap(ids, "pair", bit)])
        bit *= 2
    plan = make_plan(lay, ids, ranks, where)
    bit = 2
    while bit < shares:
        theirs = swap(sums, "fsdp", bit)
        theirs, plan = lax.optimization_barrier((theirs, plan))
        sums = add(sums, theirs)
        bit *= 2
    sums = (sums, swap(sums, "fsdp", 1))
    terms = group_terms(lay, norm, plan, near_tokens, near_cot, sums)
    branches = [functools.partial(first_exchange, size + share(size, groups)) for size in WIDTHS]
    received, far, near = lax.switch(plan[lay.width_at], branches, terms, cotangent)
    reduced = reduce_terms(lay, adapter_down.shape[2], plan, received)
    branches = [functools.partial(second_exchange, lay, size + share(size, groups)) for size in CAPS]
    slots, input_grad = lax.switch(
        plan[lay.cap_at], branches, plan, reduced, cotangent, far, near, value_weight, adapter_down, sums
    )
    down_grad, up_grad = unpack(lay, plan, slots, tokens.shape[1], adapter_down.shape[2])
    return input_grad, down_grad, up_grad


def dense_per_device(tokens, cotangent, value_weight, adapter_down, adapter_up, pair_ids, ranks):
    rows, features = tokens.shape
    blocks = pair_ids.shape[0]
    length = rows // blocks
    npair, _, rmax = adapter_down.shape
    norm = 1.0 / math.sqrt(rows * lax.axis_size("pair"))
    mask = (jnp.arange(rmax, dtype=jnp.int32)[None, :] < ranks[:, None]).astype(jnp.float32)
    scale = 32.0 / ranks.astype(jnp.float32)
    x = tokens.reshape(blocks, length, features)
    c = cotangent.reshape(blocks, length, cotangent.shape[1])
    down, up = adapter_down[pair_ids], adapter_up[pair_ids]
    wide = {"preferred_element_type": jnp.float32}
    low = lax.psum(jnp.einsum("btd,bdr->btr", x, down, **wide).astype(jnp.bfloat16), "fsdp")
    back = lax.psum(jnp.einsum("btk,brk->btr", c, up, **wide).astype(jnp.bfloat16), "fsdp")
    rows_mask = mask[pair_ids][:, None, :]
    low = (low.astype(jnp.float32) * rows_mask).astype(jnp.bfloat16)
    back = (back.astype(jnp.float32) * rows_mask).astype(jnp.bfloat16)
    cots = lax.all_gather(cotangent, "fsdp", axis=1, tiled=True)
    base = jnp.einsum("tk,dk->td", cots, value_weight, **wide).reshape(blocks, length, features)
    factor = scale[pair_ids][:, None, None]
    input_grad = (base + factor * jnp.einsum("btr,bdr->btd", back, down, **wide)).astype(jnp.bfloat16)
    term_a = jnp.einsum("btd,btr->bdr", x, back, **wide) * (factor * norm)
    term_b = jnp.einsum("btr,btk->brk", low, c, **wide) * (factor * norm)
    onehot = (pair_ids[:, None] == jnp.arange(npair, dtype=jnp.int32)[None, :]).astype(jnp.float32)
    grads = [
        lax.psum_scatter(
            jnp.einsum("bp,bij->pij", onehot, term).astype(jnp.bfloat16), "pair", scatter_dimension=0, tiled=True
        )
        for term in (term_a, term_b)
    ]
    return input_grad.reshape(rows, features), grads[0], grads[1]


def per_shape(tokens, cotangent, value_weight, adapter_down, adapter_up, pair_ids, ranks):
    groups, shares = lax.axis_size("pair"), lax.axis_size("fsdp")
    blocks = pair_ids.shape[0]
    part = tokens.shape[1] // groups
    power = lambda v: v & (v - 1) == 0
    fits = (
        part % 128 == 0
        and part == cotangent.shape[1]
        and power(groups)
        and power(shares)
        and power(blocks)
        and min(shares, blocks) > 1
        and groups <= 8
        and WIDTHS[-1] >= blocks * adapter_down.shape[2]
        and CAPS[-1] >= adapter_down.shape[0] // groups * adapter_down.shape[2]
    )
    form = per_device if fits else dense_per_device
    return form(tokens, cotangent, value_weight, adapter_down, adapter_up, pair_ids, ranks)


def solution(mesh):
    placed = (
        P("pair", "fsdp"),
        P("pair", "fsdp"),
        P("fsdp", None),
        P(None, "fsdp", None),
        P(None, None, "fsdp"),
        P("pair"),
        P(),
    )
    return jax.shard_map(
        per_shape,
        mesh=mesh,
        in_specs=placed,
        out_specs=(P("pair", "fsdp"), P("pair", "fsdp", None), P("pair", None, "fsdp")),
        check_vma=False,
    )
```

```python
import functools
import math

import jax
import jax.numpy as jnp
from jax import lax
from jax.experimental import pallas as pl
from jax.experimental.pallas import tpu as pltpu
from jax.sharding import PartitionSpec as P

WIDTHS = (224, 256, 288, 320, 352, 384, 416, 448, 512)
CAPS = (160, 192, 224, 256, 288, 320, 352, 384, 448, 768)
ALIGN = 16
HEAD = 16
NT = (((1,), (1,)), ((), ()))
MIB = 1024 * 1024
SIZES = (128, 64, 32, 16)


def call(kernel, out_shape, grid, in_specs, out_specs, scratch=(), flops=0, moved=0, prefetch=1, room=40):
    return pl.pallas_call(
        kernel,
        out_shape=out_shape,
        grid_spec=pltpu.PrefetchScalarGridSpec(
            num_scalar_prefetch=prefetch,
            grid=grid,
            in_specs=in_specs,
            out_specs=out_specs,
            scratch_shapes=list(scratch),
        ),
        compiler_params=pltpu.CompilerParams(vmem_limit_bytes=room * MIB),
        cost_estimate=pl.CostEstimate(flops=flops, bytes_accessed=moved, transcendentals=0),
    )


def whole(shape):
    return pl.BlockSpec(shape, lambda i, *s: (0,) * len(shape))


def direct(kernel, out_shape, places, out_places, scratch, room, flops, moved):
    spec = lambda kind: pl.BlockSpec(memory_space=kind)
    return pl.pallas_call(
        kernel,
        out_shape=out_shape,
        in_specs=[spec(kind) for kind in places],
        out_specs=jax.tree.map(spec, out_places),
        scratch_shapes=scratch,
        compiler_params=pltpu.CompilerParams(vmem_limit_bytes=room * MIB),
        cost_estimate=pl.CostEstimate(flops=flops, bytes_accessed=moved, transcendentals=0),
    )


def iota(shape, axis):
    return lax.broadcasted_iota(jnp.int32, shape, axis)


def aligned(index, unit=ALIGN):
    return pl.multiple_of(index, unit)


def swap(x, axis, bit):
    size = lax.axis_size(axis)
    return lax.ppermute(x, axis, [(i, i ^ bit) for i in range(size)])


def share(columns, groups):
    return -(-columns // (groups * ALIGN)) * ALIGN


class Layout:
    def __init__(self, groups, blocks, npair):
        self.groups, self.blocks, self.npair = groups, blocks, npair
        count = groups * blocks
        self.mine, self.own = 1, 2
        self.width_at, self.width, self.slot, self.cap_at, self.cap, self.small = 3, 4, 5, 6, 7, 8
        self.off = HEAD
        self.first = self.off + count
        self.owner = self.first + count
        self.into = self.owner + count
        self.pair = self.into + count
        self.rank = self.pair + count
        self.pair_into = self.rank + count
        self.pair_rank = self.pair_into + npair
        self.size = self.pair_rank + npair


def own_half(blocks):
    return (lax.axis_index("fsdp") & 1) * (blocks // 2)


def plan_kernel(lay, ids, ranks, plan):
    groups, blocks, npair = lay.groups, lay.blocks, lay.npair
    per = npair // groups
    me = lax.axis_index("pair")
    plan[0] = me
    plan[lay.mine] = lax.axis_index("fsdp")
    plan[lay.own] = own_half(blocks)

    def clear(p, carry):
        plan[lay.pair_rank + p] = 0
        return carry

    lax.fori_loop(0, npair, clear, 0)

    def group(g, widest):
        total = jnp.int32(0)
        pairs = [ids[(g ^ me) * blocks + b] for b in range(blocks)]
        places = []
        for b in range(blocks):
            i = g * blocks + b
            pair = pairs[b]
            rank = ranks[pair]
            plan[lay.pair_rank + pair] = rank
            place, new = total, rank
            for a in range(b):
                same = pairs[a] == pair
                place = jnp.where(same, places[a], place)
                new = jnp.where(same, 0, new)
            places.append(place)
            plan[lay.off + i] = place
            plan[lay.first + i] = new
            plan[lay.pair + i] = pair
            plan[lay.rank + i] = rank
            total = total + new
        return jnp.maximum(widest, total)

    widest = lax.fori_loop(0, groups, group, jnp.int32(0))

    def owner(o, fullest):
        total = jnp.int32(0)
        for k in range(per):
            p = o * per + k
            plan[lay.pair_into + p] = total
            total = total + plan[lay.pair_rank + p]
        return jnp.maximum(fullest, total)

    fullest = lax.fori_loop(0, groups, owner, jnp.int32(0))

    def block(i, carry):
        pair = plan[lay.pair + i]
        plan[lay.owner + i] = lax.div(pair, jnp.int32(per))
        plan[lay.into + i] = plan[lay.pair_into + pair]
        return carry

    lax.fori_loop(0, groups * blocks, block, 0)
    for need, sizes, at in ((widest, WIDTHS, lay.width_at), (fullest, CAPS, lay.cap_at)):
        values = [(k, size, share(size, groups)) for k, size in enumerate(sizes)]
        chosen = [jnp.int32(v) for v in values[-1]]
        for k, size, rows in reversed(values[:-1]):
            fits = need <= size
            chosen = [jnp.where(fits, v, c) for v, c in zip((k, size, rows), chosen)]
        for k in range(3):
            plan[at + k] = chosen[k]


def make_plan(lay, ids, ranks):
    smem = pl.BlockSpec(memory_space=pltpu.SMEM)
    return pl.pallas_call(
        functools.partial(plan_kernel, lay),
        out_shape=jax.ShapeDtypeStruct((lay.size,), jnp.int32),
        in_specs=[smem] * 2,
        out_specs=smem,
        compiler_params=pltpu.CompilerParams(vmem_limit_bytes=4 * MIB),
    )(ids, ranks)


def rank_kernel(blocks, ids, cot, up, x, down, x_near, cot_near, kept, sent, ups, downs, sems):
    length, half, rmax = x.shape[0] // blocks, blocks // 2, ups.shape[1]
    own = own_half(blocks)
    piece = length // 2
    waits = []
    for k in range(blocks):
        b = k ^ own
        pair = ids[b]
        pairs = [(down.at[pair], downs.at[k]), (up.at[pair], ups.at[k])]
        rows = pl.ds(aligned(b * length, length), length)
        pairs.append((cot.at[rows], cot_near.at[rows]))
        for h in range(2):
            rows = pl.ds(aligned(b * length + h * piece, piece), piece)
            pairs.append((x.at[rows], x_near.at[rows]))
        copies = [pltpu.make_async_copy(*pair, sems.at[k, n]) for n, pair in enumerate(pairs)]
        for copy in copies:
            copy.start()
        waits.append(copies)
    for k in range(blocks):
        for copy in waits[k]:
            copy.wait()
        rows = pl.ds(aligned((k ^ own) * length, length), length)
        out = kept if k < half else sent
        lines = slice(k % half * length, (k % half + 1) * length)
        back = lax.dot_general(cot_near[rows, :], ups[k], NT, preferred_element_type=jnp.float32)
        out[lines, :rmax] = back.astype(out.dtype)
        low = jnp.dot(x_near[rows, :], downs[k], preferred_element_type=jnp.float32)
        out[lines, rmax:] = low.astype(out.dtype)


def rank_sums(ids, cotangent, adapter_up, tokens, adapter_down):
    rows, width = cotangent.shape
    features = tokens.shape[1]
    blocks, rmax = ids.shape[0], adapter_up.shape[1]
    smem, far, near = (pl.BlockSpec(memory_space=kind) for kind in (pltpu.SMEM, pltpu.HBM, pltpu.VMEM))
    shape = (rows // 2, 2 * rmax)
    return pl.pallas_call(
        functools.partial(rank_kernel, blocks),
        out_shape=[pltpu.VMEM(v.shape, v.dtype) for v in (tokens, cotangent)]
        + [jax.ShapeDtypeStruct(shape, jnp.bfloat16)] * 2,
        in_specs=[smem] + [far] * 4,
        out_specs=[near] * 4,
        scratch_shapes=[
            pltpu.VMEM((blocks, rmax, width), jnp.bfloat16),
            pltpu.VMEM((blocks, features, rmax), jnp.bfloat16),
            pltpu.SemaphoreType.DMA((blocks, 5)),
        ],
        compiler_params=pltpu.CompilerParams(vmem_limit_bytes=50 * MIB),
        cost_estimate=pl.CostEstimate(
            flops=2 * rows * (width + features) * rmax,
            bytes_accessed=2 * rows * (width + features + 2 * rmax),
            transcendentals=0,
        ),
    )(ids, cotangent, adapter_up, tokens, adapter_down)


def add(a, b):
    return (a.astype(jnp.float32) + b.astype(jnp.float32)).astype(a.dtype)


def turn(rank, value):
    shape = (value.shape[1], value.shape[1])
    eye = jnp.logical_and(iota(shape, 0) == iota(shape, 1), iota(shape, 0) < rank).astype(jnp.bfloat16)
    return lax.dot_general(eye, value, NT, preferred_element_type=jnp.float32).astype(jnp.bfloat16)


def terms_kernel(lay, norm, plan, x, cot, own_sums, other_sums, out, total, turned, moved):
    groups, blocks = lay.groups, lay.blocks
    half = blocks // 2
    length, rmax, part = turned.shape[2], turned.shape[1], out.shape[2]
    most, room = WIDTHS[-1], share(WIDTHS[-1], groups)
    pieces = total.shape[1] // part
    me, own = plan[0], plan[lay.own]
    width, slot = plan[lay.width], plan[lay.slot]

    def place(k, columns):
        i = me * blocks + (k ^ own)
        factor = 32.0 / jnp.full((1, columns), plan[lay.rank + i], jnp.int32).astype(jnp.float32) * norm
        return pl.ds(aligned(plan[lay.off + i]), rmax), factor

    total[:, :part] = jnp.zeros((total.shape[0], part), total.dtype)
    for k in range(blocks):
        b = k ^ own
        rank = plan[lay.rank + me * blocks + b]
        source = own_sums if k < half else other_sums
        lines = slice(k % half * length, (k % half + 1) * length)
        turned[k] = turn(rank, source[lines, :rmax])
        low = turn(rank, source[lines, rmax:])
        rows, factor = place(k, part)
        block = cot[pl.ds(aligned(b * length, length), length), :]
        total[rows, :part] += factor * jnp.dot(low, block, preferred_element_type=jnp.float32)
    column = iota((groups * room, most), 1)
    target = (column % groups) * slot + column // groups
    pick = (iota((groups * room, most), 0) == target).astype(jnp.bfloat16)
    up = total[:most, :part].astype(jnp.bfloat16)
    moved[...] = jnp.dot(pick, up, preferred_element_type=jnp.float32).astype(jnp.bfloat16)

    def columns(step, carry):
        total[...] = jnp.zeros_like(total)
        here = pl.ds(aligned(step * (pieces * part), pieces * part), pieces * part)
        for k in range(blocks):
            rows, factor = place(k, pieces * part)
            block = x[pl.ds(aligned((k ^ own) * length, length), length), here]
            total[rows, :] += factor * jnp.dot(turned[k], block, preferred_element_type=jnp.float32)
        for p in range(pieces):
            g = step * pieces + p
            out[g, :most, :] = total[:most, p * part : (p + 1) * part].astype(jnp.bfloat16)
            out[g, pl.ds(aligned(width), room), :] = moved[pl.ds(aligned(g * slot), room), :]
        return carry

    lax.fori_loop(0, groups // pieces, columns, 0)


def group_terms(lay, norm, plan, tokens, cotangent, sums):
    rows, features = tokens.shape
    part = cotangent.shape[1]
    rmax = sums[0].shape[1] // 2
    most, room = WIDTHS[-1], share(WIDTHS[-1], lay.groups)
    pieces = 2
    shape = (lay.groups, most + room, part)
    smem, near = pltpu.SMEM, pltpu.VMEM
    return direct(
        functools.partial(terms_kernel, lay, norm),
        pltpu.VMEM(shape, jnp.bfloat16),
        [smem, near, near, near, near],
        near,
        [
            pltpu.VMEM((most + rmax, pieces * part), jnp.float32),
            pltpu.VMEM((lay.blocks, rmax, rows // lay.blocks), jnp.bfloat16),
            pltpu.VMEM((lay.groups * room, part), jnp.bfloat16),
        ],
        room=12,
        flops=2 * rows * (features + part) * rmax,
        moved=2 * features * (rows + most),
    )(plan, tokens, cotangent, *sums)


def grad_kernel(lay, tiles, parts, plan, *refs):
    cots, (weight, down, backs, backo, out, cat) = refs[:parts], refs[parts:]
    step = pl.program_id(0)
    half = lay.blocks * tiles // 2
    block = lax.div(step, jnp.int32(tiles)) ^ plan[lay.own]
    mine = plan[lay.mine]
    width = cots[0].shape[1]
    for s, cot in enumerate(cots):
        cat[:, pl.ds(aligned((mine ^ s) * width, width), width)] = cot[...]
    rank = plan[lay.rank + plan[0] * lay.blocks + block]
    back = jnp.where(step < half, backs[...], backo[...])
    rows = jnp.where(iota(back.shape, 1) < rank, back, jnp.zeros_like(back))
    chunk = 512
    scale = 32.0 / jnp.full((1, chunk), rank, jnp.int32).astype(jnp.float32)

    def columns(c, carry):
        here = pl.ds(aligned(c * chunk, chunk), chunk)
        base = lax.dot_general(cat[...], weight[here, :], NT, preferred_element_type=jnp.float32)
        extra = lax.dot_general(rows, down[0, here, :], NT, preferred_element_type=jnp.float32)
        out[:, here] = (base + scale * extra).astype(out.dtype)
        return carry

    lax.fori_loop(0, out.shape[1] // chunk, columns, 0)


def input_gradient(lay, plan, cots, weight, adapter_down, sums):
    rows, width = cots[0].shape
    features, values = weight.shape
    blocks = lay.blocks
    tile = rows // blocks
    tiles = 1
    half = blocks * tiles // 2
    rmax = sums[0].shape[1] // 2
    here = lambda i, plan: (i ^ (plan[lay.own] * tiles), 0)

    def adapter(i, plan):
        block = lax.div(i, jnp.int32(tiles)) ^ plan[lay.own]
        return (plan[lay.pair + plan[0] * blocks + block], 0, 0)

    return call(
        functools.partial(grad_kernel, lay, tiles, len(cots)),
        jax.ShapeDtypeStruct((rows, features), jnp.bfloat16),
        (rows // tile,),
        [pl.BlockSpec((tile, width), here)] * len(cots)
        + [
            whole(weight.shape),
            pl.BlockSpec((1, features, rmax), adapter),
            pl.BlockSpec((tile, rmax), lambda i, plan: (jnp.minimum(i, half - 1), 0)),
            pl.BlockSpec((tile, rmax), lambda i, plan: (jnp.maximum(i - half, 0), 0)),
        ],
        pl.BlockSpec((tile, features), here),
        [pltpu.VMEM((tile, values), jnp.bfloat16)],
        flops=2 * rows * features * (values + rmax),
        moved=2 * features * (rows + values),
        room=32,
    )(plan, *cots, weight, adapter_down, *sums)


def reduce_kernel(lay, plan, parts, out, total, cat, lines):
    groups, blocks = lay.groups, lay.blocks
    room, space = share(WIDTHS[-1], groups), share(CAPS[-1], groups)
    width, slot, cap, small = plan[lay.width], plan[lay.slot], plan[lay.cap], plan[lay.small]
    chunk = 128

    def clear(c, carry):
        total[pl.ds(aligned(c * chunk, chunk), chunk), :] = jnp.zeros((chunk, total.shape[1]), total.dtype)
        return carry

    lax.fori_loop(0, lax.div(groups * cap + chunk - 1, jnp.int32(chunk)), clear, 0)
    place = iota((1, groups * room), 1)
    target = jnp.full((1, groups * room), -1, jnp.int32)
    for g in range(groups):
        held = parts[g, pl.ds(aligned(width), room), :]
        cat[g * room : (g + 1) * room, :] = jnp.where(iota(held.shape, 0) < slot, held, jnp.zeros_like(held))
        for b in range(blocks):
            i = g * blocks + b
            rank, source = plan[lay.first + i], plan[lay.off + i]
            owner, into = plan[lay.owner + i], plan[lay.into + i]
            goal = owner * cap + into
            for size in SIZES:

                @pl.when(rank == size)
                def _(g=g, source=source, goal=goal, size=size):
                    here = pl.ds(aligned(source), size)
                    total[pl.ds(aligned(goal), size), :] += parts[g, here, :].astype(jnp.float32)

            start = g * room + lax.div(source, jnp.int32(groups))
            inside = jnp.logical_and(place >= start, place < start + lax.div(rank, jnp.int32(groups)))
            shift = owner * small + lax.div(into, jnp.int32(groups)) - start
            target = jnp.where(inside, place + shift, target)
    line = iota((chunk, groups * room), 0)

    def up_rows(c, carry):
        pick = (line + c * chunk == target).astype(jnp.bfloat16)
        rows = jnp.dot(pick, cat[...], preferred_element_type=jnp.float32).astype(out.dtype)
        lines[pl.ds(aligned(c * chunk, chunk), chunk), :] = rows
        return carry

    lax.fori_loop(0, lax.div(groups * small + chunk - 1, jnp.int32(chunk)), up_rows, 0)

    def owner_rows(o, carry):
        def copy(c, carry):
            here = pl.ds(aligned(c * chunk, chunk), chunk)
            out[o, here, :] = total[pl.ds(aligned(o * cap + c * chunk), chunk), :].astype(out.dtype)
            return carry

        lax.fori_loop(0, lax.div(cap + chunk - 1, jnp.int32(chunk)), copy, 0)
        out[o, pl.ds(aligned(cap), space), :] = lines[pl.ds(aligned(o * small), space), :]
        return carry

    lax.fori_loop(0, groups, owner_rows, 0)


def reduce_terms(lay, rmax, plan, parts):
    part = parts.shape[2]
    groups, most = lay.groups, CAPS[-1]
    shape = (groups, most + rmax, part)
    return direct(
        functools.partial(reduce_kernel, lay),
        pltpu.VMEM(shape, jnp.bfloat16),
        [pltpu.SMEM, pltpu.VMEM],
        pltpu.VMEM,
        [
            pltpu.VMEM((groups * most + 128, part), jnp.float32),
            pltpu.VMEM((groups * share(WIDTHS[-1], groups), part), jnp.bfloat16),
            pltpu.VMEM((groups * share(most, groups), part), jnp.bfloat16),
        ],
        room=16,
        flops=2 * most * WIDTHS[-1] * part,
        moved=4 * groups * most * part,
    )(plan, parts)


def unpack_kernel(lay, plan, slots, down, up, cat):
    groups = lay.groups
    per = lay.npair // groups
    me, cap = plan[0], plan[lay.cap]
    part, rmax, space = slots.shape[2], down.shape[2], share(CAPS[-1], groups)
    eye = (iota((part, part), 0) == iota((part, part), 1)).astype(jnp.bfloat16)
    for s in range(groups):
        held = slots[s, pl.ds(aligned(cap), space), :]
        cat[s * space : (s + 1) * space, :] = jnp.where(iota(held.shape, 0) < plan[lay.small], held, jnp.zeros_like(held))
    shape = (rmax, groups * space)
    r, column = iota(shape, 0), iota(shape, 1)
    place = (r % groups) * space + r // groups
    for k in range(per):
        start, rank = plan[lay.pair_into + me * per + k], plan[lay.pair_rank + me * per + k]

        @pl.when(rank > 0)
        def _(k=k, start=start, rank=rank):
            for s in range(groups):
                rows = slots[s, pl.ds(aligned(start), rmax), :]
                rows = jnp.where(iota(rows.shape, 0) < rank, rows, jnp.zeros_like(rows))
                value = lax.dot_general(eye, rows, NT, preferred_element_type=jnp.float32)
                down[k, s * part : (s + 1) * part, :] = value.astype(down.dtype)
            match = column == place + lax.div(start, jnp.int32(groups))
            pick = jnp.logical_and(match, r < rank).astype(jnp.bfloat16)
            up[k] = jnp.dot(pick, cat[...], preferred_element_type=jnp.float32).astype(up.dtype)

        @pl.when(rank == 0)
        def _(k=k):
            down[k] = jnp.zeros_like(down[k])
            up[k] = jnp.zeros_like(up[k])


def unpack(lay, plan, slots, features, rmax):
    part = slots.shape[2]
    per = lay.npair // lay.groups
    shapes = [(per, features, rmax), (per, rmax, part)]
    return call(
        functools.partial(unpack_kernel, lay),
        [jax.ShapeDtypeStruct(shape, jnp.bfloat16) for shape in shapes],
        (1,),
        [whole(slots.shape)],
        [whole(shape) for shape in shapes],
        [pltpu.VMEM((lay.groups * share(CAPS[-1], lay.groups), part), jnp.bfloat16)],
        flops=2 * per * features * rmax * part,
        moved=2 * per * features * rmax,
        room=20,
    )(plan, slots)


def far_parts(x, axis):
    size = lax.axis_size(axis)
    parts = {0: x}
    bit = size // 2
    while bit > 1:
        for k in sorted(parts):
            parts[k ^ bit] = swap(parts[k], axis, bit)
        bit //= 2
    return [parts[k] for k in sorted(parts) if k], swap(x, axis, 1)


def all_parts(x, far, near, axis):
    out = [x, near]
    for part in far:
        out += [part, swap(part, axis, 1)]
    return out


def move_kernel(rows, source, out, *scratch):
    groups = source.shape[0]
    steps = [source, *scratch[: len(scratch) - 1], out]
    sems = scratch[-1]
    copies = [
        [
            pltpu.make_async_copy(a.at[g, pl.ds(0, rows)], b.at[g, pl.ds(0, rows)], sems.at[hop, g])
            for g in range(groups)
        ]
        for hop, (a, b) in enumerate(zip(steps, steps[1:]))
    ]
    for copy in copies[0]:
        copy.start()
    for hop, batch in enumerate(copies):
        for g, copy in enumerate(batch):
            copy.wait()
            if hop + 1 < len(copies):
                copies[hop + 1][g].start()


def move(source, rows, size, kind, through):
    groups, _, part = source.shape
    scratch = [pltpu.VMEM((groups, rows, part), source.dtype)] if through else []
    return pl.pallas_call(
        functools.partial(move_kernel, rows),
        out_shape=kind((groups, size, part), source.dtype),
        in_specs=[pl.BlockSpec(memory_space=pl.ANY)],
        out_specs=pl.BlockSpec(memory_space=pl.ANY),
        scratch_shapes=scratch + [pltpu.SemaphoreType.DMA((1 + len(scratch), groups))],
        compiler_params=pltpu.CompilerParams(vmem_limit_bytes=12 * MIB),
    )(source)


def spread(rows, parts, through):
    sent = move(parts, rows, rows, pltpu.HBM, through)
    sent = lax.all_to_all(sent, "pair", split_axis=0, concat_axis=0, tiled=True)
    return move(sent, rows, parts.shape[1], pltpu.VMEM, False)


def first_exchange(rows, terms, cotangent):
    return spread(rows, terms, False), *far_parts(cotangent, "fsdp")


def second_exchange(lay, rows, plan, sums, cotangent, far, near, weight, adapter_down, ranked):
    cots = all_parts(cotangent, far, near, "fsdp")
    return spread(rows, sums, False), input_gradient(lay, plan, cots, weight, adapter_down, ranked)


def per_device(tokens, cotangent, value_weight, adapter_down, adapter_up, pair_ids, ranks):
    rows = tokens.shape[0]
    blocks = pair_ids.shape[0]
    groups, shares = lax.axis_size("pair"), lax.axis_size("fsdp")
    lay = Layout(groups, blocks, adapter_down.shape[0])
    norm = 1.0 / math.sqrt(rows * groups)
    ids = jnp.concatenate([pair_ids, swap(pair_ids, "pair", 1)])
    near_tokens, near_cot, kept, sent = rank_sums(pair_ids, cotangent, adapter_up, tokens, adapter_down)
    ids, sent = lax.optimization_barrier((ids, sent))
    sums = add(kept, swap(sent, "fsdp", 1))
    sums, ids = lax.optimization_barrier((sums, ids))
    bit = 2
    while bit < groups:
        ids = jnp.concatenate([ids, swap(ids, "pair", bit)])
        bit *= 2
    plan = make_plan(lay, ids, ranks)
    bit = 2
    while bit < shares:
        theirs = swap(sums, "fsdp", bit)
        theirs, plan = lax.optimization_barrier((theirs, plan))
        sums = add(sums, theirs)
        bit *= 2
    sums = (sums, swap(sums, "fsdp", 1))
    terms = group_terms(lay, norm, plan, near_tokens, near_cot, sums)
    branches = [functools.partial(first_exchange, size + share(size, groups)) for size in WIDTHS]
    received, far, near = lax.switch(plan[lay.width_at], branches, terms, cotangent)
    reduced = reduce_terms(lay, adapter_down.shape[2], plan, received)
    branches = [functools.partial(second_exchange, lay, size + share(size, groups)) for size in CAPS]
    slots, input_grad = lax.switch(
        plan[lay.cap_at], branches, plan, reduced, cotangent, far, near, value_weight, adapter_down, sums
    )
    down_grad, up_grad = unpack(lay, plan, slots, tokens.shape[1], adapter_down.shape[2])
    return input_grad, down_grad, up_grad


def dense_per_device(tokens, cotangent, value_weight, adapter_down, adapter_up, pair_ids, ranks):
    rows, features = tokens.shape
    blocks = pair_ids.shape[0]
    length = rows // blocks
    npair, _, rmax = adapter_down.shape
    norm = 1.0 / math.sqrt(rows * lax.axis_size("pair"))
    mask = (jnp.arange(rmax, dtype=jnp.int32)[None, :] < ranks[:, None]).astype(jnp.float32)
    scale = 32.0 / ranks.astype(jnp.float32)
    x = tokens.reshape(blocks, length, features)
    c = cotangent.reshape(blocks, length, cotangent.shape[1])
    down, up = adapter_down[pair_ids], adapter_up[pair_ids]
    wide = {"preferred_element_type": jnp.float32}
    low = lax.psum(jnp.einsum("btd,bdr->btr", x, down, **wide).astype(jnp.bfloat16), "fsdp")
    back = lax.psum(jnp.einsum("btk,brk->btr", c, up, **wide).astype(jnp.bfloat16), "fsdp")
    rows_mask = mask[pair_ids][:, None, :]
    low = (low.astype(jnp.float32) * rows_mask).astype(jnp.bfloat16)
    back = (back.astype(jnp.float32) * rows_mask).astype(jnp.bfloat16)
    cots = lax.all_gather(cotangent, "fsdp", axis=1, tiled=True)
    base = jnp.einsum("tk,dk->td", cots, value_weight, **wide).reshape(blocks, length, features)
    factor = scale[pair_ids][:, None, None]
    input_grad = (base + factor * jnp.einsum("btr,bdr->btd", back, down, **wide)).astype(jnp.bfloat16)
    term_a = jnp.einsum("btd,btr->bdr", x, back, **wide) * (factor * norm)
    term_b = jnp.einsum("btr,btk->brk", low, c, **wide) * (factor * norm)
    onehot = (pair_ids[:, None] == jnp.arange(npair, dtype=jnp.int32)[None, :]).astype(jnp.float32)
    grads = [
        lax.psum_scatter(
            jnp.einsum("bp,bij->pij", onehot, term).astype(jnp.bfloat16), "pair", scatter_dimension=0, tiled=True
        )
        for term in (term_a, term_b)
    ]
    return input_grad.reshape(rows, features), grads[0], grads[1]


def per_shape(tokens, cotangent, value_weight, adapter_down, adapter_up, pair_ids, ranks):
    groups, shares = lax.axis_size("pair"), lax.axis_size("fsdp")
    blocks = pair_ids.shape[0]
    part = tokens.shape[1] // groups
    power = lambda v: v & (v - 1) == 0
    fits = (
        part % 128 == 0
        and part == cotangent.shape[1]
        and power(groups)
        and power(shares)
        and power(blocks)
        and min(shares, blocks) > 1
        and groups <= 8
        and WIDTHS[-1] >= blocks * adapter_down.shape[2]
        and CAPS[-1] >= adapter_down.shape[0] // groups * adapter_down.shape[2]
    )
    form = per_device if fits else dense_per_device
    return form(tokens, cotangent, value_weight, adapter_down, adapter_up, pair_ids, ranks)


def solution(mesh):
    placed = (
        P("pair", "fsdp"),
        P("pair", "fsdp"),
        P("fsdp", None),
        P(None, "fsdp", None),
        P(None, None, "fsdp"),
        P("pair"),
        P(),
    )
    return jax.shard_map(
        per_shape,
        mesh=mesh,
        in_specs=placed,
        out_specs=(P("pair", "fsdp"), P("pair", "fsdp", None), P("pair", None, "fsdp")),
        check_vma=False,
    )
```
